32 devices in a mesh: group: 4 (over y, x), tile: 8 (over z, core).
Axes of the slice: x: 2, y: 2, z: 4, core: 2. Of those that a mesh axis runs over, the one named last changes fastest.
Arguments:
- tracer: float32 [16, 64, 2048], P(None, 'group', 'tile'), may hold values from -6 to 6
- east_speed: float32 [16, 64, 2048], P(None, 'group', 'tile'), may hold values from -0.5 to 0.5
- north_speed: float32 [16, 64, 2048], P(None, 'group', 'tile'), may hold values from -0.5 to 0.5
- mixing: float32 [15, 64, 2048], P(None, 'group', 'tile'), may hold values from 0.1 to 3
- depth_levels: int32 [64, 2048], P('group', 'tile'), may hold values from 0 to 16
- sensitivity: float32 [16, 64, 2048], P(None, 'group', 'tile'), may hold values from -6 to 6
Outputs:
- final_state: float32 [16, 64, 2048], P(None, 'group', 'tile')
- adjoint_state: float32 [16, 64, 2048], P(None, 'group', 'tile')
The draws below stay inside these ranges and needn't reach their ends.
All inputs are finite; a program needn't handle non-finite values.
Results may differ from the reference program's by a relative error of at most 0.0001.
Values sent between devices are 32-bit elements; how exact they have to be, the bound alone decides.
No kernel may reach another device: no remote copies, remote signals or barrier semaphores. Data moves between devices by JAX's collectives and lax.ppermute only.
A program may use at most 64 MiB of HBM per device.

```python
import math
import jax
import jax.numpy as jnp
from jax import lax

NZ = 16
NZM = 15
NY = 64
NX = 2048


def signed_speed(key, salt):
    mixed_key = jax.random.fold_in(key, salt)
    sign_key, size_key = jax.random.split(mixed_key)
    shape = (NZ, NY, NX)
    signs = (jax.random.randint(sign_key, shape, 0, 2) * 2 - 1).astype(jnp.float32)
    magnitude = jax.random.uniform(size_key, shape, jnp.float32, 0.35, 0.5)
    return (signs * magnitude).astype(jnp.float32)


def draw_east_speed(key, part):
    return signed_speed(key, 7101)


def draw_north_speed(key, part):
    return signed_speed(key, 7202)


def draw_depth_levels(key, part):
    mixed_key = jax.random.fold_in(key, 7303)
    choose_key, level_key = jax.random.split(mixed_key)
    shape = (NY, NX)
    choose_full = jax.random.randint(choose_key, shape, 0, 4)
    shallow = jax.random.randint(level_key, shape, 0, NZ + 1)
    depth = jnp.where(choose_full != 0, NZ, shallow).astype(jnp.int32)
    row_index = lax.broadcasted_iota(jnp.int32, shape, 0)
    column_index = lax.broadcasted_iota(jnp.int32, shape, 1)
    planted = jnp.logical_and(row_index == 0, column_index == 0)
    return jnp.where(planted, 0, depth).astype(jnp.int32)


def block_scale(key, dims, pieces, least, largest):
    factor_of = 1.0
    for axis_at, parts in pieces:
        heights = jax.random.uniform(jax.random.fold_in(jax.random.fold_in(key, 6), axis_at), (parts,), jnp.float32, least / len(pieces), largest / len(pieces))
        factor_of = factor_of * jnp.repeat(jnp.exp(heights), dims[axis_at] // parts).reshape((-1,) + (1,) * (len(dims) - 1 - axis_at))
    return factor_of


def centred(key, shape, deviation, limit, shards=(), kind=jnp.bfloat16):
    entries = deviation * jax.random.normal(key, shape, jnp.float32)
    if shards:
        entries = entries * block_scale(key, shape, shards, -0.22, 0.18)
    return jnp.clip(entries, -limit, limit).astype(kind)


def setup_inputs(seed: int = 0) -> dict:
    splits = jax.random.split(jax.random.key(seed), 7)
    tracer = centred(splits[0], (NZ, NY, NX), 1.0, 6.0, ((1, 4), (2, 8)), jnp.float32)
    east_speed = draw_east_speed(jax.random.fold_in(splits[6], 71), 0)
    north_speed = draw_north_speed(jax.random.fold_in(splits[6], 71), 0)
    mixing = jnp.clip(jnp.exp(math.log(3.0) - 3.4011974 * jax.random.uniform(splits[3], (NZM, NY, NX), jnp.float32) ** block_scale(splits[3], (NZM, NY, NX), ((1, 4), (2, 8)), -0.2, 0.2)), 0.1, 3.0)
    depth_levels = draw_depth_levels(jax.random.fold_in(splits[6], 71), 0)
    sensitivity = centred(splits[5], (NZ, NY, NX), 1.0, 6.0, ((1, 4), (2, 8)), jnp.float32)
    return dict(tracer=tracer, east_speed=east_speed, north_speed=north_speed, mixing=mixing, depth_levels=depth_levels, sensitivity=sensitivity)


diffusivity = 0.1
uptake = 0.2


def interval(source, first_index, last_index, along_axis):
    return lax.slice_in_dim(source, first_index, last_index, axis=along_axis)


def trim_margin(source, margin):
    if margin == 0:
        return source
    return source[:, margin:source.shape[1] - margin, margin:source.shape[2] - margin]


def flux_change(tracer_field, face_speed, wet_mask, along_axis):
    extent = tracer_field.shape[along_axis]
    open_face = interval(wet_mask, 2, extent - 1, along_axis) * interval(wet_mask, 1, extent - 2, along_axis)
    inner = interval(tracer_field, 2, extent - 1, along_axis)
    behind = interval(tracer_field, 1, extent - 2, along_axis)
    outer = interval(tracer_field, 3, extent, along_axis) + interval(tracer_field, 0, extent - 3, along_axis)
    face_flux = open_face * (interval(face_speed, 2, extent - 1, along_axis) * (7.0 * (inner + behind) - outer) / 12.0 - diffusivity * (inner - behind))
    faces_total = face_flux.shape[along_axis]
    return interval(face_flux, 0, faces_total - 1, along_axis) - interval(face_flux, 1, faces_total, along_axis)


def explicit_step(tracer_field, east_face, north_face, wet_mask):
    across = flux_change(tracer_field, east_face, wet_mask, 2)
    across = across[:, 2:across.shape[1] - 2, :]
    north_term = flux_change(tracer_field, north_face, wet_mask, 1)
    north_term = north_term[:, :, 2:north_term.shape[2] - 2]
    middle = trim_margin(tracer_field, 2)
    return trim_margin(wet_mask, 2) * (middle + across + north_term - uptake * middle * middle)


def flux_reverse(weight, face_speed, wet_mask, along_axis):
    extent = weight.shape[along_axis]
    open_face = interval(wet_mask, 1, extent, along_axis) * interval(wet_mask, 0, extent - 1, along_axis)
    face_jump = interval(weight, 1, extent, along_axis) - interval(weight, 0, extent - 1, along_axis)
    carried = open_face * interval(face_speed, 1, extent, along_axis) * face_jump / 12.0
    spread = diffusivity * open_face * face_jump
    face_count = extent - 1
    moved = 7.0 * (interval(carried, 1, face_count - 2, along_axis) + interval(carried, 2, face_count - 1, along_axis)) - interval(carried, 0, face_count - 3, along_axis) - interval(carried, 3, face_count, along_axis)
    mixed = interval(spread, 2, face_count - 1, along_axis) - interval(spread, 1, face_count - 2, along_axis)
    return moved + mixed


def adjoint_explicit(weight, state_now, east_face, north_face, wet_mask):
    across = flux_reverse(weight, east_face, wet_mask, 2)
    across = across[:, 2:across.shape[1] - 2, :]
    north_term = flux_reverse(weight, north_face, wet_mask, 1)
    north_term = north_term[:, :, 2:north_term.shape[2] - 2]
    middle = trim_margin(weight, 2)
    return middle + across + north_term - 2.0 * uptake * state_now * middle


def factorize(mixing_field, wet_mask):
    links = mixing_field * wet_mask[:-1] * wet_mask[1:]
    layers = wet_mask.shape[0]
    zero_plane = jnp.zeros_like(wet_mask[0])
    uppers = []
    inverses = []
    above_link = zero_plane
    above_upper = zero_plane
    for position in range(layers):
        below_link = links[position] if position < layers - 1 else zero_plane
        pivot_sum = 1.0 + above_link + below_link + above_link * above_upper
        inverse = 1.0 / pivot_sum
        upper_term = -below_link * inverse
        uppers.append(upper_term)
        inverses.append(inverse)
        above_link = below_link
        above_upper = upper_term
    return jnp.stack(uppers), jnp.stack(inverses), links


def column_solve(factors, right_side):
    uppers, inverses, links = factors
    layers = right_side.shape[0]
    current = right_side[0] * inverses[0]
    forward_pass = [current]
    for position in range(1, layers):
        current = (right_side[position] + links[position - 1] * current) * inverses[position]
        forward_pass.append(current)
    result = [current]
    for position in range(layers - 2, -1, -1):
        current = forward_pass[position] - uppers[position] * current
        result.append(current)
    return jnp.stack(result[::-1])


def pad_zero(source, margin):
    return jnp.pad(source, ((0, 0), (margin, margin), (margin, margin)))


def reference(tracer, east_speed, north_speed, mixing, depth_levels, sensitivity):
    levels = jnp.arange(tracer.shape[0], dtype=jnp.int32)[:, None, None]
    wet_mask = jnp.where(levels < depth_levels[None], 1.0, 0.0).astype(tracer.dtype)
    factors = factorize(mixing, wet_mask)
    east_pad = pad_zero(east_speed, 2)
    north_pad = pad_zero(north_speed, 2)
    wet_pad = pad_zero(wet_mask, 2)
    first_state = column_solve(factors, explicit_step(pad_zero(tracer, 2), east_pad, north_pad, wet_pad))
    final_state = column_solve(factors, explicit_step(pad_zero(first_state, 2), east_pad, north_pad, wet_pad))
    adjoint = sensitivity
    for state_now in (first_state, tracer):
        gradient = wet_mask * column_solve(factors, adjoint)
        adjoint = adjoint_explicit(pad_zero(gradient, 2), state_now, east_pad, north_pad, wet_pad)
    return final_state, adjoint
```

```python
import functools

import jax
import jax.numpy as jnp
from jax import lax
from jax.experimental import pallas as pl
from jax.experimental.pallas import tpu as pltpu
from jax.sharding import PartitionSpec as P

diffusivity = 0.1
uptake = 0.2
lanes = 128
sublanes = 8


def lane_tracer_after(k):
    return 4 * k


def lane_tracer_before(k):
    return (4 * k - 2) % lanes


def lane_weight_after(k):
    return 64 + 2 * k


def lane_weight_before(k):
    return 63 + 2 * k


def lane_carried(k):
    return 96 + k


def lane_speed(k):
    return 112 + k


lane_depth = 62


def turned(value, shift, axis):
    return pltpu.roll(value, shift % value.shape[axis], axis)


def lane_index(shape):
    return lax.broadcasted_iota(jnp.int32, shape, 1)


def row_index(shape):
    return lax.broadcasted_iota(jnp.int32, shape, 0)


def explicit_flux(c, speed, is_open, axis, size):
    behind = turned(c, 1, axis)
    outer = turned(c, -1, axis) + turned(c, 2, axis)
    flux = jnp.where(is_open, speed * (7.0 * (c + behind) - outer) - diffusivity * (c - behind), 0.0)
    change = flux - turned(flux, -1, axis)
    return lax.slice_in_dim(change, 0, size, axis=axis)


def reverse_flux(h, speed, is_open, halo_carried, in_halo, axis, size):
    jump = jnp.where(is_open, h - turned(h, 1, axis), 0.0)
    carried = speed * jump
    tail = lax.slice_in_dim(carried, size, carried.shape[axis], axis=axis)
    tail = jnp.where(in_halo, halo_carried, tail)
    carried = jnp.concatenate([lax.slice_in_dim(carried, 0, size, axis=axis), tail], axis=axis)
    spread = diffusivity * jump
    seven = 7.0 * carried
    total = (seven - spread) + turned(seven + spread, -1, axis) - turned(carried, 1, axis) - turned(carried, -2, axis)
    return lax.slice_in_dim(total, 0, size, axis=axis)


def pack_columns(k, c, h, speed, open_x, before, after):
    rows = c.shape[0]
    lane = lane_index((rows, lanes))
    c_first, c_last = c[:, :lanes], c[:, -lanes:]
    h_first, h_last = h[:, :lanes], h[:, -lanes:]
    s_first, s_last = speed[:, :lanes], speed[:, -lanes:]
    o_first, o_last = open_x[:, :lanes], open_x[:, -lanes:]
    g_first = jnp.where(o_first, s_first * (h_first - turned(h_first, 1, 1)), 0.0)
    g_last = jnp.where(o_last, s_last * (h_last - turned(h_last, 1, 1)), 0.0)
    at = lane_tracer_before(k)
    before = jnp.where((lane == at) | (lane == at + 1), turned(c_last, at - (lanes - 2), 1), before)
    at = lane_weight_before(k)
    before = jnp.where(lane == at, turned(h_last, at - (lanes - 1), 1), before)
    at = lane_carried(k)
    before = jnp.where(lane == at, turned(g_last, at - (lanes - 1), 1), before)
    after = jnp.where(lane == at, turned(g_first, at - 1, 1), after)
    at = lane_tracer_after(k)
    after = jnp.where((lane == at) | (lane == at + 1), turned(c_first, at, 1), after)
    at = lane_weight_after(k)
    after = jnp.where(lane == at, turned(h_first, at, 1), after)
    return before, after


def pack_rows(k, levels, c, h, speed, open_y, even, pay_even, pay_odd):
    size = c.shape[0]
    last = slice(size - sublanes, size)
    first = slice(0, sublanes)
    g_last = jnp.where(open_y[last], speed[last] * (h[last] - turned(h[last], 1, 0)), 0.0)
    g_first = jnp.where(open_y[first], speed[first] * (h[first] - turned(h[first], 1, 0)), 0.0)
    up = (c[size - 2 : size - 1], c[size - 1 :], h[size - 1 :], g_last[sublanes - 1 :])
    down = (c[0:1], c[1:2], h[0:1], g_first[1:2])
    for item in range(4):
        at = item * levels + k
        pay_even[at : at + 1, :] = jnp.where(even, up[item], down[item])
        pay_odd[at : at + 1, :] = jnp.where(even, down[item], up[item])


def parities():
    return lax.rem(lax.axis_index("group"), 2) == 0, lax.rem(lax.axis_index("tile"), 2) == 0


def factor_kernel(
    tracer, east, north, mixing, depth, sensitivity, inverse, weight, pay_even, pay_odd, pay_core, pay_chip, passed
):
    levels, rows, columns = tracer.shape
    even_y, even_x = parities()
    deep = depth[...]
    shallow_x = jnp.minimum(deep, turned(deep, 1, 1))
    shallow_y = jnp.minimum(deep, turned(deep, 1, 0))
    above = jnp.zeros((rows, columns), jnp.float32)
    share = above
    current = above
    for k in range(levels):
        below = jnp.where(k + 1 < deep, mixing[k], 0.0) if k < levels - 1 else jnp.zeros_like(above)
        inv = 1.0 / (1.0 + below + (above - above * share))
        current = (sensitivity[k] + above * current) * inv
        share = below * inv
        above = below
        inverse[k] = inv
        passed[k] = current
    lane = lane_index((rows, lanes))
    depth_float = deep.astype(jnp.float32)
    at_depth = lane == lane_depth
    before = jnp.where(at_depth, turned(depth_float[:, -lanes:], lane_depth - (lanes - 1), 1), 0.0)
    after = jnp.where(at_depth, turned(depth_float[:, :lanes], lane_depth, 1), 0.0)
    for k in range(levels - 1, -1, -1):
        if k < levels - 1:
            share = jnp.where(k + 1 < deep, mixing[k], 0.0) * inverse[k]
            current = passed[k] + share * current
        h = jnp.where(k < deep, current, 0.0)
        weight[k] = h
        c = tracer[k]
        speed_x = east[k] * (1.0 / 12.0)
        speed_y = north[k] * (1.0 / 12.0)
        before, after = pack_columns(k, c, h, speed_x, k < shallow_x, before, after)
        at = lane_speed(k)
        after = jnp.where(lane == at, turned(speed_x[:, :lanes], at, 1), after)
        pack_rows(k, levels, c, h, speed_y, k < shallow_y, even_y, pay_even, pay_odd)
        at = 4 * levels + k
        pay_even[at : at + 1, :] = speed_y[0:1]
        pay_odd[at : at + 1, :] = speed_y[0:1]
    at = 5 * levels
    depth_up = jnp.broadcast_to(depth_float[rows - 1 :], (sublanes, columns))
    depth_down = jnp.broadcast_to(depth_float[0:1], (sublanes, columns))
    pay_even[at : at + sublanes, :] = jnp.where(even_y, depth_up, depth_down)
    pay_odd[at : at + sublanes, :] = jnp.where(even_y, depth_down, depth_up)
    pay_core[...] = jnp.where(even_x, before, after)
    pay_chip[...] = jnp.where(even_x, after, before)


def halo_rows(k, item, levels, lower, upper, size):
    columns = lower.shape[1]
    row = row_index((sublanes, columns))

    def line(ref, which):
        at = which * levels + k
        return jnp.broadcast_to(ref[at : at + 1, :], (sublanes, columns))

    if item == "tracer":
        tile = jnp.where(row == 0, line(upper, 0), line(upper, 1))
        return jnp.where(row == sublanes - 2, line(lower, 0), jnp.where(row == sublanes - 1, line(lower, 1), tile))
    if item == "weight":
        return jnp.where(row == 0, line(upper, 2), line(lower, 2))
    if item == "carried":
        return jnp.where(row == 1, line(upper, 3), line(lower, 3))
    return line(upper, 4)


def halo_lanes(k, merged, before, after):
    lane = lane_index(merged.shape)
    c = turned(merged, -lane_tracer_after(k), 1)
    h = turned(merged, -lane_weight_after(k), 1)
    at = lane_carried(k)
    g = jnp.where(lane == 1, turned(after, 1 - at, 1), turned(before, lanes - 1 - at, 1))
    return c, h, g


def merge_lanes(before, after):
    lane = lane_index(before.shape)
    c_after = (lane < 62) & (lax.rem(lane, 4) < 2)
    h_after = (lane > 62) & (lane < 96) & (lax.rem(lane, 2) == 0)
    return jnp.where(c_after | h_after, after, before)


def take_rows(even, got_even, got_odd, lower, upper):
    a, b = got_even[...], got_odd[...]
    lower[...] = jnp.where(even, b, a)
    upper[...] = jnp.where(even, a, b)


def take_lanes(even, got_core, got_chip):
    a, b = got_core[...], got_chip[...]
    return jnp.where(even, b, a), jnp.where(even, a, b)


def shallow_faces(deep, before, after, lower, upper, levels):
    rows, columns = deep.shape
    lane = lane_index((rows, lanes))
    tail = jnp.where(lane == 0, turned(after, -lane_depth, 1), turned(before, lanes - 1 - lane_depth, 1))
    ring_x = jnp.concatenate([deep, tail], axis=1)
    at = 5 * levels
    row = row_index((sublanes, columns))
    tail = jnp.where(row == 0, upper[at : at + sublanes, :], lower[at : at + sublanes, :])
    ring_y = jnp.concatenate([deep, tail], axis=0)
    return jnp.minimum(ring_x, turned(ring_x, 1, 1)), jnp.minimum(ring_y, turned(ring_y, 1, 0))


def step_level(k, levels, c, h, east_k, north_k, faces, statics, halos):
    rows, columns = c.shape
    shallow_x, shallow_y = faces
    lower1, upper1, after1 = statics
    lower, upper, merged, before, after = halos
    open_x, open_y = k < shallow_x, k < shallow_y
    c_tail, h_tail, g_tail = halo_lanes(k, merged, before, after)
    speed_x = jnp.concatenate([east_k * (1.0 / 12.0), turned(after1, -lane_speed(k), 1)], axis=1)
    speed_y = jnp.concatenate([north_k * (1.0 / 12.0), halo_rows(k, "speed", levels, lower1, upper1, rows)], axis=0)
    lane = lane_index((rows, lanes))
    row = row_index((sublanes, columns))
    lanes_given = (lane == 1) | (lane == lanes - 1)
    rows_given = (row == 1) | (row == sublanes - 1)
    c_x = jnp.concatenate([c, c_tail], axis=1)
    forward = explicit_flux(c_x, speed_x, open_x, 1, columns)
    c_y = jnp.concatenate([c, halo_rows(k, "tracer", levels, lower, upper, rows)], axis=0)
    forward = forward + explicit_flux(c_y, speed_y, open_y, 0, rows)
    h_x = jnp.concatenate([h, h_tail], axis=1)
    backward = reverse_flux(h_x, speed_x, open_x, g_tail, lanes_given, 1, columns)
    h_y = jnp.concatenate([h, halo_rows(k, "weight", levels, lower, upper, rows)], axis=0)
    given = halo_rows(k, "carried", levels, lower, upper, rows)
    backward = backward + reverse_flux(h_y, speed_y, open_y, given, rows_given, 0, rows)
    return forward, h + backward


def first_kernel(
    tracer, east, north, mixing, depth, inverse, weight, got_even, got_odd, got_core, got_chip,
    state, weight_next, pay_even, pay_odd, pay_core, pay_chip, passed, linear, lower, upper,
):
    levels, rows, columns = tracer.shape
    even_y, even_x = parities()
    take_rows(even_y, got_even, got_odd, lower, upper)
    before, after = take_lanes(even_x, got_core, got_chip)
    merged = merge_lanes(before, after)
    deep = depth[...]
    depth_float = deep.astype(jnp.float32)
    faces = shallow_faces(depth_float, before, after, lower, upper, levels)
    current = jnp.zeros((rows, columns), jnp.float32)
    above = current
    for k in range(levels):
        c, h = tracer[k], weight[k]
        forward, back = step_level(
            k, levels, c, h, east[k], north[k], faces, (lower, upper, after), (lower, upper, merged, before, after)
        )
        linear[k] = back
        right = jnp.where(k < deep, c + forward - uptake * c * c, 0.0)
        current = (right + above * current) * inverse[k]
        passed[k] = current
        if k < levels - 1:
            above = jnp.where(k + 1 < deep, mixing[k], 0.0)
    state[levels - 1] = current
    for k in range(levels - 2, -1, -1):
        current = passed[k] + (jnp.where(k + 1 < deep, mixing[k], 0.0) * inverse[k]) * current
        state[k] = current
    current = jnp.zeros((rows, columns), jnp.float32)
    for k in range(levels):
        right = linear[k] - (2.0 * uptake) * state[k] * weight[k]
        if k > 0:
            right = right + jnp.where(k < deep, mixing[k - 1], 0.0) * current
        current = right * inverse[k]
        passed[k] = current
    packed_before = jnp.zeros((rows, lanes), jnp.float32)
    packed_after = packed_before
    shallow_x, shallow_y = faces[0][:, :columns], faces[1][:rows]
    for k in range(levels - 1, -1, -1):
        if k < levels - 1:
            current = passed[k] + (jnp.where(k + 1 < deep, mixing[k], 0.0) * inverse[k]) * current
        h = jnp.where(k < deep, current, 0.0)
        weight_next[k] = h
        c = state[k]
        packed_before, packed_after = pack_columns(
            k, c, h, east[k] * (1.0 / 12.0), k < shallow_x, packed_before, packed_after
        )
        pack_rows(k, levels, c, h, north[k] * (1.0 / 12.0), k < shallow_y, even_y, pay_even, pay_odd)
    pay_core[...] = jnp.where(even_x, packed_before, packed_after)
    pay_chip[...] = jnp.where(even_x, packed_after, packed_before)


def second_kernel(
    tracer, east, north, mixing, depth, inverse, state, weight, got1_even, got1_odd, got1_core, got1_chip,
    got_even, got_odd, got_core, got_chip, final, adjoint, passed, lower1, upper1, lower, upper,
):
    levels, rows, columns = tracer.shape
    even_y, even_x = parities()
    take_rows(even_y, got1_even, got1_odd, lower1, upper1)
    take_rows(even_y, got_even, got_odd, lower, upper)
    before1, after1 = take_lanes(even_x, got1_core, got1_chip)
    before, after = take_lanes(even_x, got_core, got_chip)
    merged = merge_lanes(before, after)
    deep = depth[...]
    faces = shallow_faces(deep.astype(jnp.float32), before1, after1, lower1, upper1, levels)
    current = jnp.zeros((rows, columns), jnp.float32)
    above = current
    for k in range(levels):
        c, h = state[k], weight[k]
        forward, back = step_level(
            k, levels, c, h, east[k], north[k], faces, (lower1, upper1, after1), (lower, upper, merged, before, after)
        )
        adjoint[k] = back - (2.0 * uptake) * tracer[k] * h
        right = jnp.where(k < deep, c + forward - uptake * c * c, 0.0)
        current = (right + above * current) * inverse[k]
        passed[k] = current
        if k < levels - 1:
            above = jnp.where(k + 1 < deep, mixing[k], 0.0)
    final[levels - 1] = current
    for k in range(levels - 2, -1, -1):
        current = passed[k] + (jnp.where(k + 1 < deep, mixing[k], 0.0) * inverse[k]) * current
        final[k] = current


def pairs(axis, parity):
    devices = lax.axis_size(axis)
    swaps = []
    for i in range(parity, devices - 1, 2):
        swaps += [(i, i + 1), (i + 1, i)]
    return swaps


def exchange(pay_even, pay_odd, pay_core, pay_chip):
    got_core = lax.ppermute(pay_core, "tile", pairs("tile", 0))
    got_chip = lax.ppermute(pay_chip, "tile", pairs("tile", 1))
    got_odd = lax.ppermute(pay_odd, "group", pairs("group", 1))
    got_even = lax.ppermute(pay_even, "group", pairs("group", 0))
    return got_even, got_odd, got_core, got_chip


def shards(tracer, east_speed, north_speed, mixing, depth_levels, sensitivity):
    levels, rows, columns = tracer.shape
    f32 = jnp.float32
    field = jax.ShapeDtypeStruct((levels, rows, columns), f32)
    edge = jax.ShapeDtypeStruct((rows, lanes), f32)
    first_size = 5 * levels + sublanes
    second_size = 4 * levels
    block = pltpu.VMEM((levels, rows, columns), f32)
    params = pltpu.CompilerParams(vmem_limit_bytes=32 * 1024 * 1024)

    def lines(size):
        return jax.ShapeDtypeStruct((size, columns), f32)

    def space(size):
        return pltpu.VMEM((size, columns), f32)

    inverse, weight, *messages = pl.pallas_call(
        factor_kernel,
        out_shape=(field, field, lines(first_size), lines(first_size), edge, edge),
        scratch_shapes=[block],
        compiler_params=params,
    )(tracer, east_speed, north_speed, mixing, depth_levels, sensitivity)
    got1 = exchange(*messages)
    state, weight_next, *messages = pl.pallas_call(
        first_kernel,
        out_shape=(field, field, lines(second_size), lines(second_size), edge, edge),
        scratch_shapes=[block, block, space(first_size), space(first_size)],
        compiler_params=params,
    )(tracer, east_speed, north_speed, mixing, depth_levels, inverse, weight, *got1)
    got2 = exchange(*messages)
    final, adjoint = pl.pallas_call(
        second_kernel,
        out_shape=(field, field),
        scratch_shapes=[block, space(first_size), space(first_size), space(second_size), space(second_size)],
        compiler_params=params,
    )(tracer, east_speed, north_speed, mixing, depth_levels, inverse, state, weight_next, *got1, *got2)
    return final, adjoint


def solution(mesh):
    block = P(None, "group", "tile")
    in_specs = (block, block, block, block, P("group", "tile"), block)
    return jax.shard_map(shards, mesh=mesh, in_specs=in_specs, out_specs=(block, block), check_vma=False)
```

```python
import functools

import jax
import jax.numpy as jnp
from jax import lax
from jax.experimental import pallas as pl
from jax.experimental.pallas import tpu as pltpu
from jax.sharding import PartitionSpec as P

diffusivity = 0.1
uptake = 0.2
lanes = 128
sublanes = 8


def lane_tracer_after(k):
    return 4 * k


def lane_tracer_before(k):
    return (4 * k - 2) % lanes


def lane_weight_after(k):
    return 64 + 2 * k


def lane_weight_before(k):
    return 63 + 2 * k


def lane_carried(k):
    return 96 + k


def lane_speed(k):
    return 112 + k


lane_depth = 62


def turned(value, shift, axis):
    return pltpu.roll(value, shift % value.shape[axis], axis)


def lane_index(shape):
    return lax.broadcasted_iota(jnp.int32, shape, 1)


def row_index(shape):
    return lax.broadcasted_iota(jnp.int32, shape, 0)


def split(value, axis):
    step = lanes if axis == 2 else sublanes
    return [lax.slice_in_dim(value, i, i + step, axis=axis) for i in range(0, value.shape[axis], step)]


def shifted(ring, shift, axis, count):
    span = ring[0].shape[axis]
    moved = [turned(tile, shift, axis) for tile in ring]
    place = lax.broadcasted_iota(jnp.int32, ring[0].shape, axis)
    if shift > 0:
        return [jnp.where(place < shift, moved[i - 1], moved[i]) for i in range(count)]
    return [jnp.where(place >= span + shift, moved[(i + 1) % len(ring)], moved[i]) for i in range(count)]


def explicit_flux(ring, speeds, opens, axis):
    full = len(ring)
    behind = shifted(ring, 1, axis, full)
    ahead = shifted(ring, -1, axis, full)
    far = shifted(ring, 2, axis, full)
    flux = [
        jnp.where(o, s * (7.0 * (c + b) - (a + f)) - diffusivity * (c - b), 0.0)
        for c, b, a, f, s, o in zip(ring, behind, ahead, far, speeds, opens)
    ]
    following = shifted(flux, -1, axis, full - 1)
    return [g - n for g, n in zip(flux, following)]


def reverse_flux(ring, speeds, opens, halo_carried, in_halo, axis):
    full = len(ring)
    behind = shifted(ring, 1, axis, full)
    jump = [jnp.where(o, h - b, 0.0) for h, b, o in zip(ring, behind, opens)]
    carried = [s * j for s, j in zip(speeds, jump)]
    carried[-1] = jnp.where(in_halo, halo_carried, carried[-1])
    seven = [7.0 * g for g in carried]
    spread = [diffusivity * j for j in jump]
    ahead = shifted([a + b for a, b in zip(seven, spread)], -1, axis, full - 1)
    back = shifted(carried, 1, axis, full - 1)
    far = shifted(carried, -2, axis, full - 1)
    return [(a - b) + c - d - e for a, b, c, d, e in zip(seven, spread, ahead, back, far)]


def pack_columns(k, c, h, speed, open_x, before, after):
    rows = c.shape[0]
    lane = lane_index((rows, lanes))
    c_first, c_last = c[:, :lanes], c[:, -lanes:]
    h_first, h_last = h[:, :lanes], h[:, -lanes:]
    s_first, s_last = speed[:, :lanes], speed[:, -lanes:]
    o_first, o_last = open_x[:, :lanes], open_x[:, -lanes:]
    g_first = jnp.where(o_first, s_first * (h_first - turned(h_first, 1, 1)), 0.0)
    g_last = jnp.where(o_last, s_last * (h_last - turned(h_last, 1, 1)), 0.0)
    at = lane_tracer_before(k)
    before = jnp.where((lane == at) | (lane == at + 1), turned(c_last, at - (lanes - 2), 1), before)
    at = lane_weight_before(k)
    before = jnp.where(lane == at, turned(h_last, at - (lanes - 1), 1), before)
    at = lane_carried(k)
    before = jnp.where(lane == at, turned(g_last, at - (lanes - 1), 1), before)
    after = jnp.where(lane == at, turned(g_first, at - 1, 1), after)
    at = lane_tracer_after(k)
    after = jnp.where((lane == at) | (lane == at + 1), turned(c_first, at, 1), after)
    at = lane_weight_after(k)
    after = jnp.where(lane == at, turned(h_first, at, 1), after)
    return before, after


def pack_rows(k, levels, c, h, speed, open_y, even, pay_even, pay_odd):
    size = c.shape[0]
    last = slice(size - sublanes, size)
    first = slice(0, sublanes)
    g_last = jnp.where(open_y[last], speed[last] * (h[last] - turned(h[last], 1, 0)), 0.0)
    g_first = jnp.where(open_y[first], speed[first] * (h[first] - turned(h[first], 1, 0)), 0.0)
    up = (c[size - 2 : size - 1], c[size - 1 :], h[size - 1 :], g_last[sublanes - 1 :])
    down = (c[0:1], c[1:2], h[0:1], g_first[1:2])
    for item in range(4):
        at = item * levels + k
        pay_even[at : at + 1, :] = jnp.where(even, up[item], down[item])
        pay_odd[at : at + 1, :] = jnp.where(even, down[item], up[item])


def parities():
    return lax.rem(lax.axis_index("group"), 2) == 0, lax.rem(lax.axis_index("tile"), 2) == 0


def factor_kernel(
    tracer_far, east_far, north_far, mixing_far, depth_far, sensitivity_far,
    tracer, east, north, mixing, depth, inverse, weight, pay_even, pay_odd, pay_core, pay_chip,
    sensitivity, passed, arrived,
):
    order = (
        (depth_far, depth),
        (mixing_far, mixing),
        (sensitivity_far, sensitivity),
        (tracer_far, tracer),
        (east_far, east),
        (north_far, north),
    )
    copies = [pltpu.make_async_copy(far, near, arrived.at[i]) for i, (far, near) in enumerate(order)]
    for copy in copies:
        copy.start()
    for copy in copies[:3]:
        copy.wait()
    levels, rows, columns = tracer.shape
    even_y, even_x = parities()
    deep = depth[...]
    shallow_x = jnp.minimum(deep, turned(deep, 1, 1))
    shallow_y = jnp.minimum(deep, turned(deep, 1, 0))
    above = jnp.zeros((rows, columns), jnp.float32)
    share = above
    current = above
    for k in range(levels):
        below = jnp.where(k + 1 < deep, mixing[k], 0.0) if k < levels - 1 else jnp.zeros_like(above)
        inv = 1.0 / (1.0 + below + (above - above * share))
        current = (sensitivity[k] + above * current) * inv
        share = below * inv
        above = below
        inverse[k] = inv
        passed[k] = current
    lane = lane_index((rows, lanes))
    depth_float = deep.astype(jnp.float32)
    at_depth = lane == lane_depth
    before = jnp.where(at_depth, turned(depth_float[:, -lanes:], lane_depth - (lanes - 1), 1), 0.0)
    after = jnp.where(at_depth, turned(depth_float[:, :lanes], lane_depth, 1), 0.0)
    for copy in copies[3:]:
        copy.wait()
    for k in range(levels - 1, -1, -1):
        if k < levels - 1:
            share = jnp.where(k + 1 < deep, mixing[k], 0.0) * inverse[k]
            current = passed[k] + share * current
        h = jnp.where(k < deep, current, 0.0)
        weight[k] = h
        c = tracer[k]
        speed_x = east[k] * (1.0 / 12.0)
        speed_y = north[k] * (1.0 / 12.0)
        before, after = pack_columns(k, c, h, speed_x, k < shallow_x, before, after)
        at = lane_speed(k)
        after = jnp.where(lane == at, turned(speed_x[:, :lanes], at, 1), after)
        pack_rows(k, levels, c, h, speed_y, k < shallow_y, even_y, pay_even, pay_odd)
        at = 4 * levels + k
        pay_even[at : at + 1, :] = speed_y[0:1]
        pay_odd[at : at + 1, :] = speed_y[0:1]
    at = 5 * levels
    depth_up = jnp.broadcast_to(depth_float[rows - 1 :], (sublanes, columns))
    depth_down = jnp.broadcast_to(depth_float[0:1], (sublanes, columns))
    pay_even[at : at + sublanes, :] = jnp.where(even_y, depth_up, depth_down)
    pay_odd[at : at + sublanes, :] = jnp.where(even_y, depth_down, depth_up)
    pay_core[...] = jnp.where(even_x, before, after)
    pay_chip[...] = jnp.where(even_x, after, before)


def halo_rows(k, item, levels, lower, upper, size):
    columns = lower.shape[1]
    row = row_index((sublanes, columns))

    def line(ref, which):
        at = which * levels + k
        return jnp.broadcast_to(ref[at : at + 1, :], (sublanes, columns))

    if item == "tracer":
        tile = jnp.where(row == 0, line(upper, 0), line(upper, 1))
        return jnp.where(row == sublanes - 2, line(lower, 0), jnp.where(row == sublanes - 1, line(lower, 1), tile))
    if item == "weight":
        return jnp.where(row == 0, line(upper, 2), line(lower, 2))
    if item == "carried":
        return jnp.where(row == 1, line(upper, 3), line(lower, 3))
    return line(upper, 4)


def halo_lanes(k, merged, before, after):
    lane = lane_index(merged.shape)
    c = turned(merged, -lane_tracer_after(k), 1)
    h = turned(merged, -lane_weight_after(k), 1)
    at = lane_carried(k)
    g = jnp.where(lane == 1, turned(after, 1 - at, 1), turned(before, lanes - 1 - at, 1))
    return c, h, g


def merge_lanes(before, after):
    lane = lane_index(before.shape)
    c_after = (lane < 62) & (lax.rem(lane, 4) < 2)
    h_after = (lane > 62) & (lane < 96) & (lax.rem(lane, 2) == 0)
    return jnp.where(c_after | h_after, after, before)


def take_rows(even, got_even, got_odd, lower, upper):
    a, b = got_even[...], got_odd[...]
    lower[...] = jnp.where(even, b, a)
    upper[...] = jnp.where(even, a, b)


def take_lanes(even, got_core, got_chip):
    a, b = got_core[...], got_chip[...]
    return jnp.where(even, b, a), jnp.where(even, a, b)


def shallow_faces(deep, before, after, lower, upper, levels):
    rows, columns = deep.shape
    lane = lane_index((rows, lanes))
    tail = jnp.where(lane == 0, turned(after, -lane_depth, 1), turned(before, lanes - 1 - lane_depth, 1))
    ring_x = jnp.concatenate([deep, tail], axis=1)
    at = 5 * levels
    row = row_index((sublanes, columns))
    tail = jnp.where(row == 0, upper[at : at + sublanes, :], lower[at : at + sublanes, :])
    ring_y = jnp.concatenate([deep, tail], axis=0)
    return jnp.minimum(ring_x, turned(ring_x, 1, 1)), jnp.minimum(ring_y, turned(ring_y, 1, 0))


def step_levels(first, levels, c, h, east_part, north_part, faces, statics, halos):
    count, rows, columns = c.shape
    shallow_x, shallow_y = faces
    lower1, upper1, after1 = statics
    lower, upper, merged, before, after = halos
    inside = range(first, first + count)
    tails = [halo_lanes(k, merged, before, after) for k in inside]
    c_tail, h_tail, g_tail = (jnp.stack([tail[i] for tail in tails]) for i in range(3))
    s_tail = jnp.stack([turned(after1, -lane_speed(k), 1) for k in inside])

    def stacked(item):
        return jnp.stack([halo_rows(k, item, levels, lower, upper, rows) for k in inside])

    s_rows = jnp.stack([halo_rows(k, "speed", levels, lower1, upper1, rows) for k in inside])
    lane = lax.broadcasted_iota(jnp.int32, (count, rows, lanes), 2)
    row = lax.broadcasted_iota(jnp.int32, (count, sublanes, columns), 1)
    lanes_given = (lane == 1) | (lane == lanes - 1)
    rows_given = (row == 1) | (row == sublanes - 1)

    def opened(shallow, axis):
        level = lax.broadcasted_iota(jnp.int32, (count,) + shallow.shape, 0).astype(jnp.float32) + float(first)
        return split(level < shallow[None], axis)

    speeds = split(east_part * (1.0 / 12.0), 2) + [s_tail]
    opens = opened(shallow_x, 2)
    forward = jnp.concatenate(explicit_flux(split(c, 2) + [c_tail], speeds, opens, 2), axis=2)
    backward = jnp.concatenate(reverse_flux(split(h, 2) + [h_tail], speeds, opens, g_tail, lanes_given, 2), axis=2)
    speeds = split(north_part * (1.0 / 12.0), 1) + [s_rows]
    opens = opened(shallow_y, 1)
    forward = forward + jnp.concatenate(explicit_flux(split(c, 1) + [stacked("tracer")], speeds, opens, 1), axis=1)
    carried = stacked("carried")
    ring = split(h, 1) + [stacked("weight")]
    backward = backward + jnp.concatenate(reverse_flux(ring, speeds, opens, carried, rows_given, 1), axis=1)
    return forward, h + backward


group_size = 8


def first_kernel(
    tracer, east, north, mixing, depth, inverse, weight, got_even, got_odd, got_core, got_chip,
    state, weight_next, pay_even, pay_odd, pay_core, pay_chip, passed, linear, lower, upper,
):
    levels, rows, columns = tracer.shape
    even_y, even_x = parities()
    take_rows(even_y, got_even, got_odd, lower, upper)
    before, after = take_lanes(even_x, got_core, got_chip)
    merged = merge_lanes(before, after)
    deep = depth[...]
    depth_float = deep.astype(jnp.float32)
    faces = shallow_faces(depth_float, before, after, lower, upper, levels)
    current = jnp.zeros((rows, columns), jnp.float32)
    above = current
    for k in range(0, levels, group_size):
        part = slice(k, min(k + group_size, levels))
        c, h = tracer[part], weight[part]
        halos = (lower, upper, merged, before, after)
        forward, back = step_levels(k, levels, c, h, east[part], north[part], faces, (lower, upper, after), halos)
        linear[part] = back
        passed[part] = c + forward - uptake * c * c
    for k in range(levels):
        right = jnp.where(k < deep, passed[k], 0.0)
        current = (right + above * current) * inverse[k]
        passed[k] = current
        if k < levels - 1:
            above = jnp.where(k + 1 < deep, mixing[k], 0.0)
    state[levels - 1] = current
    for k in range(levels - 2, -1, -1):
        current = passed[k] + (jnp.where(k + 1 < deep, mixing[k], 0.0) * inverse[k]) * current
        state[k] = current
    current = jnp.zeros((rows, columns), jnp.float32)
    for k in range(levels):
        right = linear[k] - (2.0 * uptake) * state[k] * weight[k]
        if k > 0:
            right = right + jnp.where(k < deep, mixing[k - 1], 0.0) * current
        current = right * inverse[k]
        passed[k] = current
    packed_before = jnp.zeros((rows, lanes), jnp.float32)
    packed_after = packed_before
    shallow_x, shallow_y = faces[0][:, :columns], faces[1][:rows]
    for k in range(levels - 1, -1, -1):
        if k < levels - 1:
            current = passed[k] + (jnp.where(k + 1 < deep, mixing[k], 0.0) * inverse[k]) * current
        h = jnp.where(k < deep, current, 0.0)
        weight_next[k] = h
        c = state[k]
        packed_before, packed_after = pack_columns(
            k, c, h, east[k] * (1.0 / 12.0), k < shallow_x, packed_before, packed_after
        )
        pack_rows(k, levels, c, h, north[k] * (1.0 / 12.0), k < shallow_y, even_y, pay_even, pay_odd)
    pay_core[...] = jnp.where(even_x, packed_before, packed_after)
    pay_chip[...] = jnp.where(even_x, packed_after, packed_before)


def second_kernel(
    tracer, east, north, mixing, depth, inverse, state, weight, got1_even, got1_odd, got1_core, got1_chip,
    got_even, got_odd, got_core, got_chip, final_far, adjoint_far,
    final, adjoint, passed, lower1, upper1, lower, upper, sent,
):
    copies = []

    def send(near, far, part):
        copy = pltpu.make_async_copy(near.at[part], far.at[part], sent.at[len(copies)])
        copy.start()
        copies.append(copy)

    levels, rows, columns = tracer.shape
    even_y, even_x = parities()
    take_rows(even_y, got1_even, got1_odd, lower1, upper1)
    take_rows(even_y, got_even, got_odd, lower, upper)
    before1, after1 = take_lanes(even_x, got1_core, got1_chip)
    before, after = take_lanes(even_x, got_core, got_chip)
    merged = merge_lanes(before, after)
    deep = depth[...]
    faces = shallow_faces(deep.astype(jnp.float32), before1, after1, lower1, upper1, levels)
    current = jnp.zeros((rows, columns), jnp.float32)
    above = current
    for k in range(0, levels, group_size):
        part = slice(k, min(k + group_size, levels))
        c, h = state[part], weight[part]
        halos = (lower, upper, merged, before, after)
        forward, back = step_levels(k, levels, c, h, east[part], north[part], faces, (lower1, upper1, after1), halos)
        adjoint[part] = back - (2.0 * uptake) * tracer[part] * h
        send(adjoint, adjoint_far, part)
        passed[part] = c + forward - uptake * c * c
    for k in range(levels):
        right = jnp.where(k < deep, passed[k], 0.0)
        current = (right + above * current) * inverse[k]
        passed[k] = current
        if k < levels - 1:
            above = jnp.where(k + 1 < deep, mixing[k], 0.0)
    final[levels - 1] = current
    for k in range(levels - 2, -1, -1):
        current = passed[k] + (jnp.where(k + 1 < deep, mixing[k], 0.0) * inverse[k]) * current
        final[k] = current
        if k % group_size == 0:
            send(final, final_far, slice(k, min(k + group_size, levels)))
    for copy in copies:
        copy.wait()


def pairs(axis, parity):
    devices = lax.axis_size(axis)
    swaps = []
    for i in range(parity, devices - 1, 2):
        swaps += [(i, i + 1), (i + 1, i)]
    return swaps


def exchange(pay_even, pay_odd, pay_core, pay_chip):
    got_core = lax.ppermute(pay_core, "tile", pairs("tile", 0))
    got_chip = lax.ppermute(pay_chip, "tile", pairs("tile", 1))
    got_odd = lax.ppermute(pay_odd, "group", pairs("group", 1))
    got_even = lax.ppermute(pay_even, "group", pairs("group", 0))
    return got_even, got_odd, got_core, got_chip


def shards(tracer, east_speed, north_speed, mixing, depth_levels, sensitivity):
    levels, rows, columns = tracer.shape
    f32 = jnp.float32
    field = jax.ShapeDtypeStruct((levels, rows, columns), f32)
    edge = jax.ShapeDtypeStruct((rows, lanes), f32)
    first_size = 5 * levels + sublanes
    second_size = 4 * levels
    block = pltpu.VMEM((levels, rows, columns), f32)
    params = pltpu.CompilerParams(vmem_limit_bytes=32 * 1024 * 1024)

    def lines(size):
        return jax.ShapeDtypeStruct((size, columns), f32)

    def space(size):
        return pltpu.VMEM((size, columns), f32)

    far = pl.BlockSpec(memory_space=pl.ANY)
    given = (tracer, east_speed, north_speed, mixing, depth_levels)
    near = tuple(jax.ShapeDtypeStruct(array.shape, array.dtype) for array in given)
    *outcome, pay_even, pay_odd, pay_core, pay_chip = pl.pallas_call(
        factor_kernel,
        in_specs=[far] * 6,
        out_shape=near + (field, field, lines(first_size), lines(first_size), edge, edge),
        scratch_shapes=[block, block, pltpu.SemaphoreType.DMA((6,))],
        compiler_params=params,
    )(*[pltpu.with_memory_space_constraint(a, pltpu.HBM) for a in given], pltpu.with_memory_space_constraint(sensitivity, pltpu.HBM))
    *given, inverse, weight = outcome
    messages = (pay_even, pay_odd, pay_core, pay_chip)
    got1 = exchange(*messages)
    state, weight_next, *messages = pl.pallas_call(
        first_kernel,
        out_shape=(field, field, lines(second_size), lines(second_size), edge, edge),
        scratch_shapes=[block, block, space(first_size), space(first_size)],
        compiler_params=params,
    )(*given, inverse, weight, *got1)
    got2 = exchange(*messages)
    sends = pltpu.SemaphoreType.DMA((2 * -(-levels // group_size),))
    final, adjoint = pl.pallas_call(
        second_kernel,
        out_specs=[far] * 2,
        out_shape=(field, field),
        scratch_shapes=[block, block, block, space(first_size), space(first_size), space(second_size), space(second_size), sends],
        compiler_params=params,
    )(*given, inverse, state, weight_next, *got1, *got2)
    return final, adjoint


def solution(mesh):
    block = P(None, "group", "tile")
    in_specs = (block, block, block, block, P("group", "tile"), block)
    return jax.shard_map(shards, mesh=mesh, in_specs=in_specs, out_specs=(block, block), check_vma=False)
```

```python
import jax
import jax.numpy as jnp
from jax import lax
from jax.experimental import pallas as pl
from jax.experimental.pallas import tpu as pltpu
from jax.sharding import PartitionSpec as P

diffusivity = 0.1
uptake = 0.2
lanes = 128
sublanes = 8
group_size = 8

slot = 8


def turned(value, shift, axis):
    return pltpu.roll(value, shift % value.shape[axis], axis)


def index(shape, axis):
    return lax.broadcasted_iota(jnp.int32, shape, axis)


def parities():
    return lax.rem(lax.axis_index("group"), 2) == 0, lax.rem(lax.axis_index("tile"), 2) == 0


def split(value, axis):
    step = lanes if axis == 2 else sublanes
    return [lax.slice_in_dim(value, i, i + step, axis=axis) for i in range(0, value.shape[axis], step)]


def shifted(tiles, shift, axis, edge):
    span = tiles[0].shape[axis]
    moved = [turned(tile, shift, axis) for tile in tiles]
    place = index(tiles[0].shape, axis)
    if shift > 0:
        return [jnp.where(place < shift, a, b) for a, b in zip([edge] + moved[:-1], moved)]
    return [jnp.where(place >= span + shift, a, b) for a, b in zip(moved[1:] + [edge], moved)]


def face_flux(c, behind, ahead, far, speed, is_open):
    flux = speed * (7.0 * (c + behind) - (ahead + far)) - diffusivity * (c - behind)
    return jnp.where(is_open, flux, 0.0)


def explicit_flux(tiles, speeds, opens, axis, edges):
    edge_behind, edge_far, edge_ahead, edge_flux = edges
    behind = shifted(tiles, 1, axis, edge_behind)
    ahead = shifted(tiles, -1, axis, edge_ahead)
    far = shifted(tiles, 2, axis, edge_far)
    flux = [face_flux(*each) for each in zip(tiles, behind, ahead, far, speeds, opens)]
    following = shifted(flux, -1, axis, edge_flux)
    return jnp.concatenate([g - n for g, n in zip(flux, following)], axis=axis)


def reverse_flux(tiles, speeds, opens, axis, edges):
    edge_behind, edge_sum, edge_carried, edge_far = edges
    behind = shifted(tiles, 1, axis, edge_behind)
    jump = [jnp.where(o, h - b, 0.0) for h, b, o in zip(tiles, behind, opens)]
    carried = [s * j for s, j in zip(speeds, jump)]
    seven = [7.0 * g for g in carried]
    spread = [diffusivity * j for j in jump]
    ahead = shifted([a + b for a, b in zip(seven, spread)], -1, axis, edge_sum)
    back = shifted(carried, 1, axis, edge_carried)
    far = shifted(carried, -2, axis, edge_far)
    parts = zip(seven, spread, ahead, back, far)
    return jnp.concatenate([(a - b) + c - d - e for a, b, c, d, e in parts], axis=axis)


def pack_last(k, tile, packed):
    lane = index(packed.shape, 1) - slot * k
    return jnp.where((lane >= 0) & (lane < 4), turned(tile, slot * k + 4, 1), packed)


def pack_first(k, tile, packed):
    lane = index(packed.shape, 1) - slot * k
    return jnp.where((lane >= 2) & (lane < 6), turned(tile, slot * k + 2, 1), packed)


def repeated(first_slot):
    value = jnp.where(index(first_slot.shape, 1) < slot, first_slot, 0.0)
    width = slot
    while width < lanes:
        value = value + turned(value, width, 1)
        width *= 2
    return value


def pack_rows(k, levels, c, h, speed, open_y, up, down):
    size = c.shape[0]
    last = slice(size - sublanes, size)
    first = slice(0, sublanes)
    g_last = jnp.where(open_y[last], speed[last] * (h[last] - turned(h[last], 1, 0)), 0.0)
    g_first = jnp.where(open_y[first], speed[first] * (h[first] - turned(h[first], 1, 0)), 0.0)
    above = (c[size - 2 : size - 1], c[size - 1 :], h[size - 1 :], g_last[sublanes - 1 :])
    below = (c[0:1], c[1:2], h[0:1], g_first[1:2])
    for item in range(4):
        at = item * levels + k
        up[at : at + 1, :] = above[item]
        down[at : at + 1, :] = below[item]


def choose(flag, ref_true, ref_false, into):
    into[...] = jnp.where(flag, ref_true[...], ref_false[...])


def factor_kernel(
    tracer_far, east_far, north_far, mixing_far, depth_far, sensitivity_far,
    tracer, east, north, mixing, depth, inverse, weight, pay_even, pay_odd, pay_chip, pay_core, up,
    sensitivity, passed, down, arrived,
):
    order = (
        (depth_far, depth),
        (mixing_far, mixing),
        (sensitivity_far, sensitivity),
        (tracer_far, tracer),
        (east_far, east),
        (north_far, north),
    )
    copies = [pltpu.make_async_copy(far, near, arrived.at[i]) for i, (far, near) in enumerate(order)]
    for copy in copies:
        copy.start()
    for copy in copies[:3]:
        copy.wait()
    levels, rows, columns = tracer.shape
    even_y, even_x = parities()
    deep = depth[...]
    shallow_y = jnp.minimum(deep, turned(deep, 1, 0))
    above = jnp.zeros((rows, columns), jnp.float32)
    share = above
    current = above
    for k in range(levels):
        below = jnp.where(k + 1 < deep, mixing[k], 0.0) if k < levels - 1 else jnp.zeros_like(above)
        inv = 1.0 / (1.0 + below + (above - above * share))
        current = (sensitivity[k] + above * current) * inv
        share = below * inv
        above = below
        inverse[k] = inv
        passed[k] = current
    for copy in copies[3:]:
        copy.wait()
    last = [jnp.zeros((rows, lanes), jnp.float32)] * 3
    first = last
    for k in range(levels - 1, -1, -1):
        if k < levels - 1:
            share = jnp.where(k + 1 < deep, mixing[k], 0.0) * inverse[k]
            current = passed[k] + share * current
        h = jnp.where(k < deep, current, 0.0)
        weight[k] = h
        c = tracer[k]
        speed_x = east[k] * (1.0 / 12.0)
        speed_y = north[k] * (1.0 / 12.0)
        items = (c, h, speed_x)
        last = [pack_last(k, item[:, -lanes:], packed) for item, packed in zip(items, last)]
        first = [pack_first(k, item[:, :lanes], packed) for item, packed in zip(items, first)]
        pack_rows(k, levels, c, h, speed_y, k < shallow_y, up, down)
        at = 4 * levels + k
        down[at : at + 1, :] = speed_y[0:1]
    depth_float = deep.astype(jnp.float32)
    at = 5 * levels
    up[4 * levels : at, :] = jnp.zeros((levels, columns), jnp.float32)
    up[at : at + sublanes, :] = jnp.broadcast_to(depth_float[rows - 1 :], (sublanes, columns))
    down[at : at + sublanes, :] = jnp.broadcast_to(depth_float[0:1], (sublanes, columns))
    choose(even_y, up, down, pay_even)
    choose(even_y, down, up, pay_odd)
    last.append(repeated(turned(depth_float[:, -lanes:], 4, 1)))
    first.append(repeated(turned(depth_float[:, :lanes], 2, 1)))
    last, first = jnp.concatenate(last, axis=1), jnp.concatenate(first, axis=1)
    pay_chip[...] = jnp.where(even_x, first, last)
    pay_core[...] = jnp.where(even_x, last, first)


def edges_y(levels, lower, upper, own, given, edge):
    rows_of = lambda ref, item: ref[item * levels : (item + 1) * levels, :]
    c, c_next, h, carried_next = (rows_of(upper, i) for i in range(4))
    c_two, c_one, h_one = (rows_of(own, i) for i in range(3))
    speed, deep, own_deep = given
    level = index(c.shape, 0).astype(jnp.float32)
    is_open = level < jnp.minimum(deep, own_deep)
    flux = face_flux(c, c_one, c_next, c_two, speed, is_open)
    jump = jnp.where(is_open, h - h_one, 0.0)
    carried = speed * jump
    total = 7.0 * carried + diffusivity * jump
    below = tuple(rows_of(lower, i) for i in range(4))
    for item, value in enumerate(below + (c, flux, total, carried, carried_next)):
        edge[item * levels : (item + 1) * levels, :] = value


def edges_x(before, after, own_last, speeds, depths):
    c_before, h_before = before
    c_after, h_after = after
    c_own, h_own = own_last
    speed_before, speed_after = speeds
    deep_before, deep_after, deep_own = depths
    shape = c_before.shape
    place = lax.rem(index(shape, 1), slot)
    level = lax.div(index(shape, 1), slot).astype(jnp.float32)
    inner = place < 2
    c = jnp.where(inner, turned(c_own, -2, 1), c_after)
    h = jnp.where(inner, turned(h_own, -2, 1), h_after)
    deep = jnp.where(inner, turned(deep_own, -2, 1), deep_after)
    is_open = level < jnp.minimum(deep, turned(deep, 1, 1))
    flux = face_flux(c, turned(c, 1, 1), turned(c, -1, 1), turned(c, 2, 1), speed_after, is_open)
    jump = jnp.where(is_open, h - turned(h, 1, 1), 0.0)
    carried = speed_after * jump
    total = 7.0 * carried + diffusivity * jump
    is_open = level < jnp.minimum(deep_before, turned(deep_before, 1, 1))
    carried_before = jnp.where(is_open, speed_before * (h_before - turned(h_before, 1, 1)), 0.0)
    start = place < 4
    return (
        jnp.where(start, turned(c_before, -2, 1), turned(c, -3, 1)),
        jnp.where(start, turned(c_before, -3, 1), turned(flux, -3, 1)),
        jnp.where(start, turned(h_before, -3, 1), turned(total, -3, 1)),
        jnp.where(start, turned(carried_before, -3, 1), turned(carried, -4, 1)),
    )


def step_levels(first, levels, c, h, east_part, north_part, shallow, edge, packed):
    count, rows, columns = c.shape
    shallow_x, shallow_y = shallow
    inside = range(first, first + count)
    level = index((count, rows, columns), 0) + first

    lead = [jnp.stack([turned(tile, -slot * k, 1) for k in inside]) for tile in packed]
    speeds = split(east_part * (1.0 / 12.0), 2)
    opens = split(level < shallow_x[None], 2)
    forward = explicit_flux(split(c, 2), speeds, opens, 2, (lead[1], lead[0], lead[0], lead[1]))
    backward = reverse_flux(split(h, 2), speeds, opens, 2, (lead[2], lead[2], lead[3], lead[3]))

    def line(item):
        at = item * levels
        return jnp.stack([jnp.broadcast_to(edge[at + k : at + k + 1, :], (sublanes, columns)) for k in inside])

    row = index((count, sublanes, columns), 1)
    speeds = split(north_part * (1.0 / 12.0), 1)
    opens = split(level < shallow_y[None], 1)
    one = line(1)
    edges = (one, jnp.where(row == 0, line(0), one), line(4), line(5))
    forward = forward + explicit_flux(split(c, 1), speeds, opens, 1, edges)
    edges = (line(2), line(6), line(3), jnp.where(row == sublanes - 2, line(7), line(8)))
    backward = backward + reverse_flux(split(h, 1), speeds, opens, 1, edges)
    return forward, h + backward


def shallow_faces(deep, deep_before, deep_lower):
    rows, columns = deep.shape
    previous = turned(deep, 1, 1)
    head = jnp.where(index((rows, lanes), 1) == 0, turned(deep_before, -3, 1), previous[:, :lanes])
    previous_x = jnp.concatenate([head, previous[:, lanes:]], axis=1)
    previous = turned(deep, 1, 0)
    head = jnp.where(index((sublanes, columns), 0) == 0, deep_lower, previous[:sublanes])
    previous_y = jnp.concatenate([head, previous[sublanes:]], axis=0)
    return jnp.minimum(deep, previous_x).astype(jnp.int32), jnp.minimum(deep, previous_y).astype(jnp.int32)


def item_of(value, item):
    return value[:, item * lanes : (item + 1) * lanes]


def take(flag, first, second):
    a, b = first[...], second[...]
    return jnp.where(flag, b, a), jnp.where(flag, a, b)


def first_kernel(
    tracer, east, north, mixing, depth, inverse, weight, own_up, sent_chip, sent_core,
    got_even, got_odd, got_chip, got_core,
    state, weight_next, pay_even, pay_odd, pay_chip, pay_core, up, own_last,
    passed, linear, lower, upper, edge, down,
):
    levels, rows, columns = tracer.shape
    even_y, even_x = parities()
    choose(even_y, got_odd, got_even, lower)
    choose(even_y, got_even, got_odd, upper)
    before, after = take(even_x, got_core, got_chip)
    own = jnp.where(even_x, sent_core[...], sent_chip[...])
    deep = depth[...]
    at = 5 * levels
    depth_float = deep.astype(jnp.float32)
    shallow = shallow_faces(depth_float, item_of(before, 3), lower[at : at + sublanes, :])
    speed = upper[4 * levels : at, :]
    edges_y(levels, lower, upper, own_up, (speed, upper[at : at + 1, :], depth_float[rows - 1 :]), edge)
    pairs_of = lambda value: (item_of(value, 0), item_of(value, 1))
    packed = edges_x(
        pairs_of(before),
        pairs_of(after),
        pairs_of(own),
        (item_of(before, 2), item_of(after, 2)),
        (item_of(before, 3), item_of(after, 3), item_of(own, 3)),
    )
    current = jnp.zeros((rows, columns), jnp.float32)
    above = current
    for k in range(0, levels, group_size):
        part = slice(k, min(k + group_size, levels))
        c, h = tracer[part], weight[part]
        forward, back = step_levels(k, levels, c, h, east[part], north[part], shallow, edge, packed)
        linear[part] = back
        passed[part] = c + forward - uptake * c * c
    for k in range(levels):
        current = (jnp.where(k < deep, passed[k], 0.0) + above * current) * inverse[k]
        passed[k] = current
        if k < levels - 1:
            above = jnp.where(k + 1 < deep, mixing[k], 0.0)
    state[levels - 1] = current
    for k in range(levels - 2, -1, -1):
        current = passed[k] + (jnp.where(k + 1 < deep, mixing[k], 0.0) * inverse[k]) * current
        state[k] = current
    current = jnp.zeros((rows, columns), jnp.float32)
    for k in range(levels):
        right = linear[k] - (2.0 * uptake) * state[k] * weight[k]
        if k > 0:
            right = right + jnp.where(k < deep, mixing[k - 1], 0.0) * current
        current = right * inverse[k]
        passed[k] = current
    last = [jnp.zeros((rows, lanes), jnp.float32)] * 2
    first = last
    shallow_y = shallow[1]
    for k in range(levels - 1, -1, -1):
        if k < levels - 1:
            current = passed[k] + (jnp.where(k + 1 < deep, mixing[k], 0.0) * inverse[k]) * current
        h = jnp.where(k < deep, current, 0.0)
        weight_next[k] = h
        c = state[k]
        items = (c, h)
        last = [pack_last(k, item[:, -lanes:], packed) for item, packed in zip(items, last)]
        first = [pack_first(k, item[:, :lanes], packed) for item, packed in zip(items, first)]
        pack_rows(k, levels, c, h, north[k] * (1.0 / 12.0), k < shallow_y, up, down)
    choose(even_y, up, down, pay_even)
    choose(even_y, down, up, pay_odd)
    last, first = jnp.concatenate(last, axis=1), jnp.concatenate(first, axis=1)
    own_last[...] = last
    pay_chip[...] = jnp.where(even_x, first, last)
    pay_core[...] = jnp.where(even_x, last, first)


def second_kernel(
    tracer, east, north, mixing, depth, inverse, state, weight, own_up, own_last, sent_chip, sent_core,
    got1_even, got1_odd, got1_chip, got1_core, got_even, got_odd, got_chip, got_core,
    final_far, adjoint_far,
    final, adjoint, passed, lower, upper, edge, sent,
):
    copies = []

    def send(near, far, part):
        copy = pltpu.make_async_copy(near.at[part], far.at[part], sent.at[len(copies)])
        copy.start()
        copies.append(copy)

    levels, rows, columns = tracer.shape
    even_y, even_x = parities()
    choose(even_y, got_odd, got_even, lower)
    choose(even_y, got_even, got_odd, upper)
    before1, after1 = take(even_x, got1_core, got1_chip)
    before, after = take(even_x, got_core, got_chip)
    own1 = jnp.where(even_x, sent_core[...], sent_chip[...])
    deep = depth[...]
    depth_float = deep.astype(jnp.float32)
    at = 5 * levels
    lower_deep = jnp.where(even_y, got1_odd[at : at + sublanes, :], got1_even[at : at + sublanes, :])
    upper_deep = jnp.where(even_y, got1_even[at : at + 1, :], got1_odd[at : at + 1, :])
    speed = jnp.where(even_y, got1_even[4 * levels : at, :], got1_odd[4 * levels : at, :])
    shallow = shallow_faces(depth_float, item_of(before1, 3), lower_deep)
    edges_y(levels, lower, upper, own_up, (speed, upper_deep, depth_float[rows - 1 :]), edge)
    pairs_of = lambda value: (item_of(value, 0), item_of(value, 1))
    packed = edges_x(
        pairs_of(before),
        pairs_of(after),
        pairs_of(own_last[...]),
        (item_of(before1, 2), item_of(after1, 2)),
        (item_of(before1, 3), item_of(after1, 3), item_of(own1, 3)),
    )
    current = jnp.zeros((rows, columns), jnp.float32)
    above = current
    for k in range(0, levels, group_size):
        part = slice(k, min(k + group_size, levels))
        c, h = state[part], weight[part]
        forward, back = step_levels(k, levels, c, h, east[part], north[part], shallow, edge, packed)
        adjoint[part] = back - (2.0 * uptake) * tracer[part] * h
        send(adjoint, adjoint_far, part)
        passed[part] = c + forward - uptake * c * c
    for k in range(levels):
        current = (jnp.where(k < deep, passed[k], 0.0) + above * current) * inverse[k]
        passed[k] = current
        if k < levels - 1:
            above = jnp.where(k + 1 < deep, mixing[k], 0.0)
    final[levels - 1] = current
    for k in range(levels - 2, -1, -1):
        current = passed[k] + (jnp.where(k + 1 < deep, mixing[k], 0.0) * inverse[k]) * current
        final[k] = current
        if k % group_size == 0:
            send(final, final_far, slice(k, min(k + group_size, levels)))
    for copy in copies:
        copy.wait()


def pairs(axis, parity):
    devices = lax.axis_size(axis)
    swaps = []
    for i in range(parity, devices - 1, 2):
        swaps += [(i, i + 1), (i + 1, i)]
    return swaps


def exchange(pay_even, pay_odd, pay_chip, pay_core):
    got_even = lax.ppermute(pay_even, "group", pairs("group", 0))
    got_odd = lax.ppermute(pay_odd, "group", pairs("group", 1))
    got_chip = lax.ppermute(pay_chip, "tile", pairs("tile", 1))
    got_core = lax.ppermute(pay_core, "tile", pairs("tile", 0))
    return got_even, got_odd, got_chip, got_core


def shards(tracer, east_speed, north_speed, mixing, depth_levels, sensitivity):
    levels, rows, columns = tracer.shape
    assert levels * slot == lanes and rows % sublanes == 0 and columns % lanes == 0
    f32 = jnp.float32
    field = jax.ShapeDtypeStruct((levels, rows, columns), f32)
    first_size = 5 * levels + sublanes
    second_size = 4 * levels
    edge_size = 9 * levels
    block = pltpu.VMEM((levels, rows, columns), f32)
    params = pltpu.CompilerParams(vmem_limit_bytes=32 * 1024 * 1024)
    far = pl.BlockSpec(memory_space=pl.ANY)

    def lines(size):
        return jax.ShapeDtypeStruct((size, columns), f32)

    def space(size):
        return pltpu.VMEM((size, columns), f32)

    def tiles(count):
        return jax.ShapeDtypeStruct((rows, count * lanes), f32)

    given = (tracer, east_speed, north_speed, mixing, depth_levels)
    near = tuple(jax.ShapeDtypeStruct(array.shape, array.dtype) for array in given)
    distant = [pltpu.with_memory_space_constraint(array, pltpu.HBM) for array in given + (sensitivity,)]
    outcome = pl.pallas_call(
        factor_kernel,
        in_specs=[far] * 6,
        out_shape=near
        + (field, field, lines(first_size), lines(first_size), tiles(4), tiles(4), lines(first_size)),
        scratch_shapes=[block, block, space(first_size), pltpu.SemaphoreType.DMA((6,))],
        compiler_params=params,
    )(*distant)
    given = outcome[:5]
    inverse, weight, *messages, up = outcome[5:]
    got1 = exchange(*messages)
    sent1 = messages[2:]
    state, weight_next, *messages, up2, last2 = pl.pallas_call(
        first_kernel,
        out_shape=(field, field, lines(second_size), lines(second_size), tiles(2), tiles(2), lines(second_size), tiles(2)),
        scratch_shapes=[
            block, block, space(first_size), space(first_size), space(edge_size), space(second_size),
        ],
        compiler_params=params,
    )(*given, inverse, weight, up, *sent1, *got1)
    got2 = exchange(*messages)
    sends = pltpu.SemaphoreType.DMA((2 * -(-levels // group_size),))
    final, adjoint = pl.pallas_call(
        second_kernel,
        out_specs=[far] * 2,
        out_shape=(field, field),
        scratch_shapes=[block, block, block, space(second_size), space(second_size), space(edge_size), sends],
        compiler_params=params,
    )(*given, inverse, state, weight_next, up2, last2, *sent1, *got1, *got2)
    return final, adjoint


def solution(mesh):
    block = P(None, "group", "tile")
    in_specs = (block, block, block, block, P("group", "tile"), block)
    return jax.shard_map(shards, mesh=mesh, in_specs=in_specs, out_specs=(block, block), check_vma=False)
```

```python
import jax
import jax.numpy as jnp
from jax import lax
from jax.experimental import pallas as pl
from jax.experimental.pallas import tpu as pltpu
from jax.sharding import PartitionSpec as P

diffusivity = 0.1
uptake = 0.2
lanes = 128
sublanes = 8
group_size = 8

slot = 8


def turned(value, shift, axis):
    return pltpu.roll(value, shift % value.shape[axis], axis)


def index(shape, axis):
    return lax.broadcasted_iota(jnp.int32, shape, axis)


def parities():
    return lax.rem(lax.axis_index("group"), 2) == 0, lax.rem(lax.axis_index("tile"), 2) == 0


def split(value, axis):
    step = lanes if axis == 2 else sublanes
    return [lax.slice_in_dim(value, i, i + step, axis=axis) for i in range(0, value.shape[axis], step)]


def shifted(tiles, shift, axis, edge):
    span = tiles[0].shape[axis]
    moved = [turned(tile, shift, axis) for tile in tiles]
    place = index(tiles[0].shape, axis)
    if shift > 0:
        return [jnp.where(place < shift, a, b) for a, b in zip([edge] + moved[:-1], moved)]
    return [jnp.where(place >= span + shift, a, b) for a, b in zip(moved[1:] + [edge], moved)]


def face_flux(c, behind, ahead, far, speed, is_open):
    flux = speed * (7.0 * (c + behind) - (ahead + far)) - diffusivity * (c - behind)
    return jnp.where(is_open, flux, 0.0)


def explicit_flux(tiles, speeds, opens, axis, edges):
    edge_behind, edge_far, edge_ahead, edge_flux = edges
    behind = shifted(tiles, 1, axis, edge_behind)
    ahead = shifted(tiles, -1, axis, edge_ahead)
    far = shifted(tiles, 2, axis, edge_far)
    flux = [face_flux(*each) for each in zip(tiles, behind, ahead, far, speeds, opens)]
    following = shifted(flux, -1, axis, edge_flux)
    return jnp.concatenate([g - n for g, n in zip(flux, following)], axis=axis)


def reverse_flux(tiles, speeds, opens, axis, edges):
    edge_behind, edge_sum, edge_carried, edge_far = edges
    behind = shifted(tiles, 1, axis, edge_behind)
    jump = [jnp.where(o, h - b, 0.0) for h, b, o in zip(tiles, behind, opens)]
    carried = [s * j for s, j in zip(speeds, jump)]
    seven = [7.0 * g for g in carried]
    spread = [diffusivity * j for j in jump]
    ahead = shifted([a + b for a, b in zip(seven, spread)], -1, axis, edge_sum)
    back = shifted(carried, 1, axis, edge_carried)
    far = shifted(carried, -2, axis, edge_far)
    parts = zip(seven, spread, ahead, back, far)
    return jnp.concatenate([(a - b) + c - d - e for a, b, c, d, e in parts], axis=axis)


def pack_last(k, tile, packed):
    lane = index(packed.shape, 1) - slot * k
    return jnp.where((lane >= 0) & (lane < 4), turned(tile, slot * k + 4, 1), packed)


def pack_first(k, tile, packed):
    lane = index(packed.shape, 1) - slot * k
    return jnp.where((lane >= 2) & (lane < 6), turned(tile, slot * k + 2, 1), packed)


def repeated(first_slot):
    value = jnp.where(index(first_slot.shape, 1) < slot, first_slot, 0.0)
    width = slot
    while width < lanes:
        value = value + turned(value, width, 1)
        width *= 2
    return value


def pack_rows(k, levels, c, h, speed, open_y, up, down):
    size = c.shape[0]
    last = slice(size - sublanes, size)
    first = slice(0, sublanes)
    g_last = jnp.where(open_y[last], speed[last] * (h[last] - turned(h[last], 1, 0)), 0.0)
    g_first = jnp.where(open_y[first], speed[first] * (h[first] - turned(h[first], 1, 0)), 0.0)
    above = (c[size - 2 : size - 1], c[size - 1 :], h[size - 1 :], g_last[sublanes - 1 :])
    below = (c[0:1], c[1:2], h[0:1], g_first[1:2])
    for item in range(4):
        at = item * levels + k
        up[at : at + 1, :] = above[item]
        down[at : at + 1, :] = below[item]


def choose(flag, ref_true, ref_false, into):
    into[...] = jnp.where(flag, ref_true[...], ref_false[...])


def factor_kernel(
    tracer_far, east_far, north_far, mixing_far, depth_far, sensitivity_far,
    tracer, east, north, mixing, depth, inverse, weight, pay_even, pay_odd, pay_chip, pay_core, up,
    sensitivity, passed, down, arrived,
):
    order = (
        (depth_far, depth),
        (mixing_far, mixing),
        (sensitivity_far, sensitivity),
        (tracer_far, tracer),
        (east_far, east),
        (north_far, north),
    )
    copies = [pltpu.make_async_copy(far, near, arrived.at[i]) for i, (far, near) in enumerate(order)]
    for copy in copies:
        copy.start()
    for copy in copies[:3]:
        copy.wait()
    levels, rows, columns = tracer.shape
    even_y, even_x = parities()
    deep = depth[...]
    shallow_y = jnp.minimum(deep, turned(deep, 1, 0))
    above = jnp.zeros((rows, columns), jnp.float32)
    share = above
    current = above
    for k in range(levels):
        below = jnp.where(k + 1 < deep, mixing[k], 0.0) if k < levels - 1 else jnp.zeros_like(above)
        inv = 1.0 / (1.0 + below + (above - above * share))
        current = (sensitivity[k] + above * current) * inv
        share = below * inv
        above = below
        inverse[k] = inv
        passed[k] = current
    for copy in copies[3:]:
        copy.wait()
    last = [jnp.zeros((rows, lanes), jnp.float32)] * 3
    first = last
    side = [last[0]] * 2
    for k in range(levels - 1, -1, -1):
        if k < levels - 1:
            share = jnp.where(k + 1 < deep, mixing[k], 0.0) * inverse[k]
            current = passed[k] + share * current
        h = jnp.where(k < deep, current, 0.0)
        weight[k] = h
        c = tracer[k]
        speed_x = east[k] * (1.0 / 12.0)
        speed_y = north[k] * (1.0 / 12.0)
        items = (c, h, speed_x)
        last = [pack_last(k, item[:, -lanes:], packed) for item, packed in zip(items, last)]
        first = [pack_first(k, item[:, :lanes], packed) for item, packed in zip(items, first)]
        items = (speed_y, mixing[k]) if k < levels - 1 else (speed_y,)
        for i, item in enumerate(items):
            tile = jnp.where(even_x, item[:, :lanes], item[:, -lanes:])
            lane = index(tile.shape, 1) - slot * k
            side[i] = jnp.where((lane >= 0) & (lane < 4), turned(tile, slot * k + 2, 1), side[i])
        pack_rows(k, levels, c, h, speed_y, k < shallow_y, up, down)
        at = 4 * levels + k
        down[at : at + 1, :] = speed_y[0:1]
    depth_float = deep.astype(jnp.float32)
    at = 5 * levels
    up[4 * levels : at, :] = jnp.zeros((levels, columns), jnp.float32)
    up[at : at + sublanes, :] = jnp.broadcast_to(depth_float[rows - 1 :], (sublanes, columns))
    down[at : at + sublanes, :] = jnp.broadcast_to(depth_float[0:1], (sublanes, columns))
    choose(even_y, up, down, pay_even)
    choose(even_y, down, up, pay_odd)
    last.append(repeated(turned(depth_float[:, -lanes:], 4, 1)))
    first.append(repeated(turned(depth_float[:, :lanes], 2, 1)))
    last, first = jnp.concatenate(last, axis=1), jnp.concatenate(first, axis=1)
    speed_y, mixed = side
    speed_y = jnp.where(even_x, speed_y, turned(speed_y, 2, 1))
    mixed = jnp.where(even_x, turned(mixed, 4, 1), turned(mixed, 6, 1))
    side = jnp.where(lax.rem(index(mixed.shape, 1), slot) < 4, speed_y, mixed)
    pay_chip[...] = jnp.concatenate([jnp.where(even_x, first, last), side], axis=1)
    pay_core[...] = jnp.where(even_x, last, first)


def edges_y(levels, lower, upper, own, given, edge):
    rows_of = lambda ref, item: ref[item * levels : (item + 1) * levels, :]
    c, c_next, h, carried_next = (rows_of(upper, i) for i in range(4))
    c_two, c_one, h_one = (rows_of(own, i) for i in range(3))
    speed, deep, own_deep = given
    level = index(c.shape, 0).astype(jnp.float32)
    is_open = level < jnp.minimum(deep, own_deep)
    flux = face_flux(c, c_one, c_next, c_two, speed, is_open)
    jump = jnp.where(is_open, h - h_one, 0.0)
    carried = speed * jump
    total = 7.0 * carried + diffusivity * jump
    below = tuple(rows_of(lower, i) for i in range(4))
    for item, value in enumerate(below + (c, flux, total, carried, carried_next)):
        edge[item * levels : (item + 1) * levels, :] = value


def edges_x(before, after, own_last, speeds, depths):
    c_before, h_before = before
    c_after, h_after = after
    c_own, h_own = own_last
    speed_before, speed_after = speeds
    deep_before, deep_after, deep_own = depths
    shape = c_before.shape
    place = lax.rem(index(shape, 1), slot)
    level = lax.div(index(shape, 1), slot).astype(jnp.float32)
    inner = place < 2
    c = jnp.where(inner, turned(c_own, -2, 1), c_after)
    h = jnp.where(inner, turned(h_own, -2, 1), h_after)
    deep = jnp.where(inner, turned(deep_own, -2, 1), deep_after)
    is_open = level < jnp.minimum(deep, turned(deep, 1, 1))
    flux = face_flux(c, turned(c, 1, 1), turned(c, -1, 1), turned(c, 2, 1), speed_after, is_open)
    jump = jnp.where(is_open, h - turned(h, 1, 1), 0.0)
    carried = speed_after * jump
    total = 7.0 * carried + diffusivity * jump
    is_open = level < jnp.minimum(deep_before, turned(deep_before, 1, 1))
    carried_before = jnp.where(is_open, speed_before * (h_before - turned(h_before, 1, 1)), 0.0)
    start = place < 4
    return (
        jnp.where(start, turned(c_before, -2, 1), turned(c, -3, 1)),
        jnp.where(start, turned(c_before, -3, 1), turned(flux, -3, 1)),
        jnp.where(start, turned(h_before, -3, 1), turned(total, -3, 1)),
        jnp.where(start, turned(carried_before, -3, 1), turned(carried, -4, 1)),
    )


def step_levels(first, levels, c, h, east_part, north_part, shallow, edge, packed):
    count, rows, columns = c.shape
    shallow_x, shallow_y = shallow
    inside = range(first, first + count)
    level = index((count, rows, columns), 0) + first

    lead = [jnp.stack([turned(tile, -slot * k, 1) for k in inside]) for tile in packed]
    speeds = split(east_part * (1.0 / 12.0), 2)
    opens = split(level < shallow_x[None], 2)
    forward = explicit_flux(split(c, 2), speeds, opens, 2, (lead[1], lead[0], lead[0], lead[1]))
    backward = reverse_flux(split(h, 2), speeds, opens, 2, (lead[2], lead[2], lead[3], lead[3]))

    def line(item):
        at = item * levels
        return jnp.stack([jnp.broadcast_to(edge[at + k : at + k + 1, :], (sublanes, columns)) for k in inside])

    row = index((count, sublanes, columns), 1)
    speeds = split(north_part * (1.0 / 12.0), 1)
    opens = split(level < shallow_y[None], 1)
    one = line(1)
    edges = (one, jnp.where(row == 0, line(0), one), line(4), line(5))
    forward = forward + explicit_flux(split(c, 1), speeds, opens, 1, edges)
    edges = (line(2), line(6), line(3), jnp.where(row == sublanes - 2, line(7), line(8)))
    backward = backward + reverse_flux(split(h, 1), speeds, opens, 1, edges)
    return forward, h + backward


def shallow_faces(deep, deep_before, deep_lower):
    rows, columns = deep.shape
    previous = turned(deep, 1, 1)
    head = jnp.where(index((rows, lanes), 1) == 0, turned(deep_before, -3, 1), previous[:, :lanes])
    previous_x = jnp.concatenate([head, previous[:, lanes:]], axis=1)
    previous = turned(deep, 1, 0)
    head = jnp.where(index((sublanes, columns), 0) == 0, deep_lower, previous[:sublanes])
    previous_y = jnp.concatenate([head, previous[sublanes:]], axis=0)
    return jnp.minimum(deep, previous_x).astype(jnp.int32), jnp.minimum(deep, previous_y).astype(jnp.int32)


def item_of(value, item):
    return value[:, item * lanes : (item + 1) * lanes]


def take(flag, core, chip):
    return jnp.where(flag, chip, core), jnp.where(flag, core, chip)


def common(ref):
    return ref[:, : 4 * lanes]


def strip_rows(levels, message, up, down):
    c, h, _, deep, side = (item_of(message, i) for i in range(5))
    size = c.shape[0]
    level = lax.div(index(c.shape, 1), slot).astype(jnp.float32)
    is_open = level < jnp.minimum(deep, turned(deep, 1, 0))
    carried = jnp.where(is_open, side * (h - turned(h, 1, 0)), 0.0)
    at = 4 * levels
    for ref in (up, down):
        ref[at : at + sublanes, :] = jnp.zeros((sublanes, ref.shape[1]), jnp.float32)
    end = size - 1
    above = (c[end - 1 : end], c[end:], h[end:], carried[end:], deep[end:])
    below = (c[0:1], c[1:2], h[0:1], carried[1:2], deep[0:1], side[0:1])
    for ref, lines in ((up, above), (down, below)):
        for i, line in enumerate(lines):
            ref[at + i : at + i + 1, :lanes] = line


def strip_states(levels, message, own, lower, upper, even):
    c, h, speed, deep, side = (item_of(message, i) for i in range(5))
    shape = c.shape
    place = lax.rem(index(shape, 1), slot)
    level = lax.div(index(shape, 1), slot).astype(jnp.float32)
    from_own = place - jnp.where(even, 4, 0)
    from_own = (from_own == 0) | (from_own == 1)

    def joined(item, value):
        mine = item_of(own, item)
        return jnp.where(from_own, jnp.where(even, turned(mine, 2, 1), turned(mine, -2, 1)), value)

    c, h, speed, deep = (joined(i, value) for i, value in enumerate((c, h, speed, deep)))
    is_open = level < jnp.minimum(deep, turned(deep, 1, 1))
    flux = face_flux(c, turned(c, 1, 1), turned(c, -1, 1), turned(c, 2, 1), speed, is_open)
    jump = jnp.where(is_open, h - turned(h, 1, 1), 0.0)
    carried = speed * jump
    plus = 7.0 * carried + diffusivity * jump
    minus = 7.0 * carried - diffusivity * jump
    forward = flux - turned(flux, -1, 1)
    backward = minus + turned(plus, -1, 1) - turned(carried, 1, 1) - turned(carried, -2, 1)

    def line(ref, item):
        at = 4 * levels + item
        return jnp.broadcast_to(ref[at : at + 1, :lanes], (sublanes, lanes))

    def row_of(value, at):
        return jnp.broadcast_to(value[at : at + 1], (sublanes, lanes))

    rows = shape[0]
    row = index((sublanes, lanes), 0)
    tile_level = level[:sublanes]
    previous = turned(deep, 1, 0)
    previous = jnp.concatenate([jnp.where(row == 0, line(lower, 4), previous[:sublanes]), previous[sublanes:]], axis=0)
    opens = split(level < jnp.minimum(deep, previous), 0)
    speeds = split(side, 0)
    is_open = tile_level < jnp.minimum(line(upper, 4), row_of(deep, rows - 1))
    speed_end = line(upper, 5)
    c_one, c_two = row_of(c, rows - 1), row_of(c, rows - 2)
    flux = face_flux(line(upper, 0), c_one, line(upper, 1), c_two, speed_end, is_open)
    jump = jnp.where(is_open, line(upper, 2) - row_of(h, rows - 1), 0.0)
    carried = speed_end * jump
    plus = 7.0 * carried + diffusivity * jump
    edges = (line(lower, 1), jnp.where(row == 0, line(lower, 0), line(lower, 1)), line(upper, 0), flux)
    forward = forward + explicit_flux(split(c, 0), speeds, opens, 0, edges)
    edges = (line(lower, 2), plus, line(lower, 3), jnp.where(row == sublanes - 2, carried, line(upper, 3)))
    backward = backward + reverse_flux(split(h, 0), speeds, opens, 0, edges)
    right = jnp.where(level < deep, c + forward - uptake * c * c, 0.0)
    linear = h + backward
    kept = (place == 2) | (place == 3)
    links = jnp.where(kept & (level + 1.0 < deep), turned(side, -4, 1), 0.0)

    def ready(value):
        return jnp.where(even, turned(value, -4, 1), turned(value, -2, 1))

    def levels_of(value):
        value = ready(value)
        return [turned(value, -slot * k, 1) for k in range(levels)]

    right, linear, links, weights = (levels_of(value) for value in (right, linear, links, h))
    deep = ready(deep)
    inverse, passed = [], []
    above = jnp.zeros(shape, jnp.float32)
    share = above
    current = above
    for k in range(levels):
        inv = 1.0 / (1.0 + links[k] + (above - above * share))
        current = (right[k] + above * current) * inv
        share = links[k] * inv
        above = links[k]
        inverse.append(inv)
        passed.append(current)
    state = [current]
    for k in range(levels - 2, -1, -1):
        current = passed[k] + (links[k] * inverse[k]) * current
        state.insert(0, current)
    passed = []
    current = jnp.zeros(shape, jnp.float32)
    for k in range(levels):
        value = linear[k] - (2.0 * uptake) * state[k] * weights[k]
        if k > 0:
            value = value + links[k - 1] * current
        current = value * inverse[k]
        passed.append(current)
    weight = [current]
    for k in range(levels - 2, -1, -1):
        current = passed[k] + (links[k] * inverse[k]) * current
        weight.insert(0, current)
    lane = index(shape, 1)
    packed_state = jnp.zeros(shape, jnp.float32)
    packed_weight = packed_state
    for k in range(levels):
        here = lax.rem(lane + (lanes + 2 - slot * k), lanes) < 4
        packed_state = jnp.where(here, turned(state[k], slot * k, 1), packed_state)
        value = jnp.where(k < deep, weight[k], 0.0)
        packed_weight = jnp.where(here, turned(value, slot * k, 1), packed_weight)
    back = lambda value: jnp.where(even, turned(value, 4, 1), turned(value, 2, 1))
    return back(packed_state), back(packed_weight)


def first_kernel(
    tracer, east, north, mixing, depth, inverse, weight, own_up, sent_chip, sent_core,
    got_even, got_odd, got_chip, got_core,
    state, weight_next, pay_even, pay_odd, pay_core, up, own_last,
    passed, linear, lower, upper, edge, down,
):
    levels, rows, columns = tracer.shape
    even_y, even_x = parities()
    choose(even_y, got_odd, got_even, lower)
    choose(even_y, got_even, got_odd, upper)
    before, after = take(even_x, got_core[...], common(got_chip))
    own = jnp.where(even_x, sent_core[...], common(sent_chip))
    deep = depth[...]
    at = 5 * levels
    depth_float = deep.astype(jnp.float32)
    shallow = shallow_faces(depth_float, item_of(before, 3), lower[at : at + sublanes, :])
    speed = upper[4 * levels : at, :]
    edges_y(levels, lower, upper, own_up, (speed, upper[at : at + 1, :], depth_float[rows - 1 :]), edge)
    pairs_of = lambda value: (item_of(value, 0), item_of(value, 1))
    packed = edges_x(
        pairs_of(before),
        pairs_of(after),
        pairs_of(own),
        (item_of(before, 2), item_of(after, 2)),
        (item_of(before, 3), item_of(after, 3), item_of(own, 3)),
    )
    current = jnp.zeros((rows, columns), jnp.float32)
    above = current
    for k in range(0, levels, group_size):
        part = slice(k, min(k + group_size, levels))
        c, h = tracer[part], weight[part]
        forward, back = step_levels(k, levels, c, h, east[part], north[part], shallow, edge, packed)
        linear[part] = back
        passed[part] = c + forward - uptake * c * c
    for k in range(levels):
        current = (jnp.where(k < deep, passed[k], 0.0) + above * current) * inverse[k]
        passed[k] = current
        if k < levels - 1:
            above = jnp.where(k + 1 < deep, mixing[k], 0.0)
    state[levels - 1] = current
    for k in range(levels - 2, -1, -1):
        current = passed[k] + (jnp.where(k + 1 < deep, mixing[k], 0.0) * inverse[k]) * current
        state[k] = current
    current = jnp.zeros((rows, columns), jnp.float32)
    for k in range(levels):
        right = linear[k] - (2.0 * uptake) * state[k] * weight[k]
        if k > 0:
            right = right + jnp.where(k < deep, mixing[k - 1], 0.0) * current
        current = right * inverse[k]
        passed[k] = current
    last = [jnp.zeros((rows, lanes), jnp.float32)] * 2
    first = last
    shallow_y = shallow[1]
    for k in range(levels - 1, -1, -1):
        if k < levels - 1:
            current = passed[k] + (jnp.where(k + 1 < deep, mixing[k], 0.0) * inverse[k]) * current
        h = jnp.where(k < deep, current, 0.0)
        weight_next[k] = h
        c = state[k]
        items = (c, h)
        last = [pack_last(k, item[:, -lanes:], packed) for item, packed in zip(items, last)]
        first = [pack_first(k, item[:, :lanes], packed) for item, packed in zip(items, first)]
        pack_rows(k, levels, c, h, north[k] * (1.0 / 12.0), k < shallow_y, up, down)
    strip_rows(levels, got_chip[...], up, down)
    choose(even_y, up, down, pay_even)
    choose(even_y, down, up, pay_odd)
    last, first = jnp.concatenate(last, axis=1), jnp.concatenate(first, axis=1)
    own_last[...] = last
    pay_core[...] = jnp.where(even_x, last, first)


def second_kernel(
    tracer, east, north, mixing, depth, inverse, state, weight, own_up, own_last, sent_chip, sent_core,
    got1_even, got1_odd, got1_chip, got1_core, got_even, got_odd, got_core,
    final_far, adjoint_far,
    final, adjoint, passed, lower, upper, edge, sent,
):
    copies = []

    def send(near, far, part):
        copy = pltpu.make_async_copy(near.at[part], far.at[part], sent.at[len(copies)])
        copy.start()
        copies.append(copy)

    levels, rows, columns = tracer.shape
    even_y, even_x = parities()
    choose(even_y, got_odd, got_even, lower)
    choose(even_y, got_even, got_odd, upper)
    before1, after1 = take(even_x, got1_core[...], common(got1_chip))
    strip = strip_states(levels, got1_chip[...], sent_chip[...], lower, upper, even_x)
    before, after = take(even_x, got_core[...], jnp.concatenate(strip, axis=1))
    own1 = jnp.where(even_x, sent_core[...], common(sent_chip))
    deep = depth[...]
    depth_float = deep.astype(jnp.float32)
    at = 5 * levels
    lower_deep = jnp.where(even_y, got1_odd[at : at + sublanes, :], got1_even[at : at + sublanes, :])
    upper_deep = jnp.where(even_y, got1_even[at : at + 1, :], got1_odd[at : at + 1, :])
    speed = jnp.where(even_y, got1_even[4 * levels : at, :], got1_odd[4 * levels : at, :])
    shallow = shallow_faces(depth_float, item_of(before1, 3), lower_deep)
    edges_y(levels, lower, upper, own_up, (speed, upper_deep, depth_float[rows - 1 :]), edge)
    pairs_of = lambda value: (item_of(value, 0), item_of(value, 1))
    packed = edges_x(
        pairs_of(before),
        pairs_of(after),
        pairs_of(own_last[...]),
        (item_of(before1, 2), item_of(after1, 2)),
        (item_of(before1, 3), item_of(after1, 3), item_of(own1, 3)),
    )
    current = jnp.zeros((rows, columns), jnp.float32)
    above = current
    for k in range(0, levels, group_size):
        part = slice(k, min(k + group_size, levels))
        c, h = state[part], weight[part]
        forward, back = step_levels(k, levels, c, h, east[part], north[part], shallow, edge, packed)
        adjoint[part] = back - (2.0 * uptake) * tracer[part] * h
        send(adjoint, adjoint_far, part)
        passed[part] = c + forward - uptake * c * c
    for k in range(levels):
        current = (jnp.where(k < deep, passed[k], 0.0) + above * current) * inverse[k]
        passed[k] = current
        if k < levels - 1:
            above = jnp.where(k + 1 < deep, mixing[k], 0.0)
    final[levels - 1] = current
    for k in range(levels - 2, -1, -1):
        current = passed[k] + (jnp.where(k + 1 < deep, mixing[k], 0.0) * inverse[k]) * current
        final[k] = current
        if k % group_size == 0:
            send(final, final_far, slice(k, min(k + group_size, levels)))
    for copy in copies:
        copy.wait()


def pairs(axis, parity):
    devices = lax.axis_size(axis)
    swaps = []
    for i in range(parity, devices - 1, 2):
        swaps += [(i, i + 1), (i + 1, i)]
    return swaps


def exchange(pay_even, pay_odd, *pay):
    got_even = lax.ppermute(pay_even, "group", pairs("group", 0))
    got_odd = lax.ppermute(pay_odd, "group", pairs("group", 1))
    got = [lax.ppermute(each, "tile", pairs("tile", len(pay) - 1 - i)) for i, each in enumerate(pay)]
    return got_even, got_odd, *got


def shards(tracer, east_speed, north_speed, mixing, depth_levels, sensitivity):
    levels, rows, columns = tracer.shape
    assert levels * slot == lanes and rows % sublanes == 0 and columns % lanes == 0
    f32 = jnp.float32
    field = jax.ShapeDtypeStruct((levels, rows, columns), f32)
    first_size = 5 * levels + sublanes
    second_size = 4 * levels + sublanes
    edge_size = 9 * levels
    block = pltpu.VMEM((levels, rows, columns), f32)
    params = pltpu.CompilerParams(vmem_limit_bytes=32 * 1024 * 1024)
    far = pl.BlockSpec(memory_space=pl.ANY)

    def lines(size):
        return jax.ShapeDtypeStruct((size, columns), f32)

    def space(size):
        return pltpu.VMEM((size, columns), f32)

    def tiles(count):
        return jax.ShapeDtypeStruct((rows, count * lanes), f32)

    given = (tracer, east_speed, north_speed, mixing, depth_levels)
    near = tuple(jax.ShapeDtypeStruct(array.shape, array.dtype) for array in given)
    distant = [pltpu.with_memory_space_constraint(array, pltpu.HBM) for array in given + (sensitivity,)]
    outcome = pl.pallas_call(
        factor_kernel,
        in_specs=[far] * 6,
        out_shape=near
        + (field, field, lines(first_size), lines(first_size), tiles(5), tiles(4), lines(first_size)),
        scratch_shapes=[block, block, space(first_size), pltpu.SemaphoreType.DMA((6,))],
        compiler_params=params,
    )(*distant)
    given = outcome[:5]
    inverse, weight, *messages, up = outcome[5:]
    got1 = exchange(*messages)
    sent1 = messages[2:]
    state, weight_next, *messages, up2, last2 = pl.pallas_call(
        first_kernel,
        out_shape=(field, field, lines(second_size), lines(second_size), tiles(2), lines(second_size), tiles(2)),
        scratch_shapes=[
            block, block, space(first_size), space(first_size), space(edge_size), space(second_size),
        ],
        compiler_params=params,
    )(*given, inverse, weight, up, *sent1, *got1)
    got2 = exchange(*messages)
    sends = pltpu.SemaphoreType.DMA((2 * -(-levels // group_size),))
    final, adjoint = pl.pallas_call(
        second_kernel,
        out_specs=[far] * 2,
        out_shape=(field, field),
        scratch_shapes=[block, block, block, space(second_size), space(second_size), space(edge_size), sends],
        compiler_params=params,
    )(*given, inverse, state, weight_next, up2, last2, *sent1, *got1, *got2)
    return final, adjoint


def solution(mesh):
    block = P(None, "group", "tile")
    in_specs = (block, block, block, block, P("group", "tile"), block)
    return jax.shard_map(shards, mesh=mesh, in_specs=in_specs, out_specs=(block, block), check_vma=False)
```

```python
import jax
import jax.numpy as jnp
from jax import lax
from jax.experimental import pallas as pl
from jax.experimental.pallas import tpu as pltpu
from jax.sharding import PartitionSpec as P

diffusivity = 0.1
uptake = 0.2
lanes = 128
sublanes = 8
group_size = 8

slot = 8


def turned(value, shift, axis):
    return pltpu.roll(value, shift % value.shape[axis], axis)


def index(shape, axis):
    return lax.broadcasted_iota(jnp.int32, shape, axis)


def parities():
    return lax.rem(lax.axis_index("group"), 2) == 0, lax.rem(lax.axis_index("tile"), 2) == 0


def split(value, axis):
    step = lanes if axis == 2 else sublanes
    return [lax.slice_in_dim(value, i, i + step, axis=axis) for i in range(0, value.shape[axis], step)]


def shifted(tiles, shift, axis, edge):
    span = tiles[0].shape[axis]
    moved = [turned(tile, shift, axis) for tile in tiles]
    place = index(tiles[0].shape, axis)
    if shift > 0:
        return [jnp.where(place < shift, a, b) for a, b in zip([edge] + moved[:-1], moved)]
    return [jnp.where(place >= span + shift, a, b) for a, b in zip(moved[1:] + [edge], moved)]


def face_flux(c, behind, ahead, far, speed, is_open):
    flux = speed * (7.0 * (c + behind) - (ahead + far)) - diffusivity * (c - behind)
    return jnp.where(is_open, flux, 0.0)


def explicit_flux(tiles, speeds, opens, axis, edges):
    edge_behind, edge_far, edge_ahead, edge_flux = edges
    behind = shifted(tiles, 1, axis, edge_behind)
    ahead = shifted(tiles, -1, axis, edge_ahead)
    far = shifted(tiles, 2, axis, edge_far)
    flux = [face_flux(*each) for each in zip(tiles, behind, ahead, far, speeds, opens)]
    following = shifted(flux, -1, axis, edge_flux)
    return jnp.concatenate([g - n for g, n in zip(flux, following)], axis=axis)


def reverse_flux(tiles, speeds, opens, axis, edges):
    edge_behind, edge_sum, edge_carried, edge_far = edges
    behind = shifted(tiles, 1, axis, edge_behind)
    jump = [jnp.where(o, h - b, 0.0) for h, b, o in zip(tiles, behind, opens)]
    carried = [s * j for s, j in zip(speeds, jump)]
    seven = [7.0 * g for g in carried]
    spread = [diffusivity * j for j in jump]
    ahead = shifted([a + b for a, b in zip(seven, spread)], -1, axis, edge_sum)
    back = shifted(carried, 1, axis, edge_carried)
    far = shifted(carried, -2, axis, edge_far)
    parts = zip(seven, spread, ahead, back, far)
    return jnp.concatenate([(a - b) + c - d - e for a, b, c, d, e in parts], axis=axis)


def pack_last(k, tile, packed):
    lane = index(packed.shape, 1) - slot * k
    return jnp.where((lane >= 0) & (lane < 4), turned(tile, slot * k + 4, 1), packed)


def pack_first(k, tile, packed):
    lane = index(packed.shape, 1) - slot * k
    return jnp.where((lane >= 2) & (lane < 6), turned(tile, slot * k + 2, 1), packed)


def repeated(first_slot):
    value = jnp.where(index(first_slot.shape, 1) < slot, first_slot, 0.0)
    width = slot
    while width < lanes:
        value = value + turned(value, width, 1)
        width *= 2
    return value


def pack_rows(k, levels, c, h, speed, open_y, up, down):
    size = c.shape[0]
    last = slice(size - sublanes, size)
    first = slice(0, sublanes)
    g_last = jnp.where(open_y[last], speed[last] * (h[last] - turned(h[last], 1, 0)), 0.0)
    g_first = jnp.where(open_y[first], speed[first] * (h[first] - turned(h[first], 1, 0)), 0.0)
    above = (c[size - 2 : size - 1], c[size - 1 :], h[size - 1 :], g_last[sublanes - 1 :])
    below = (c[0:1], c[1:2], h[0:1], g_first[1:2])
    for item in range(4):
        at = item * levels + k
        up[at : at + 1, :] = above[item]
        down[at : at + 1, :] = below[item]


def choose(flag, ref_true, ref_false, into):
    into[...] = jnp.where(flag, ref_true[...], ref_false[...])


def factor_kernel(
    tracer_far, east_far, north_far, mixing_far, depth_far, sensitivity_far,
    tracer, east, north, mixing, depth, inverse, weight, pay_even, pay_odd, pay_chip, pay_core, up, down, beside,
    sensitivity, passed, arrived,
):
    order = (
        (depth_far, depth),
        (mixing_far, mixing),
        (sensitivity_far, sensitivity),
        (tracer_far, tracer),
        (east_far, east),
        (north_far, north),
    )
    copies = [pltpu.make_async_copy(far, near, arrived.at[i]) for i, (far, near) in enumerate(order)]
    for copy in copies:
        copy.start()
    for copy in copies[:3]:
        copy.wait()
    levels, rows, columns = tracer.shape
    even_y, even_x = parities()
    deep = depth[...]
    shallow_y = jnp.minimum(deep, turned(deep, 1, 0))
    above = jnp.zeros((rows, columns), jnp.float32)
    share = above
    current = above
    for k in range(levels):
        below = jnp.where(k + 1 < deep, mixing[k], 0.0) if k < levels - 1 else jnp.zeros_like(above)
        inv = 1.0 / (1.0 + below + (above - above * share))
        current = (sensitivity[k] + above * current) * inv
        share = below * inv
        above = below
        inverse[k] = inv
        passed[k] = current
    for copy in copies[3:]:
        copy.wait()
    last = [jnp.zeros((rows, lanes), jnp.float32)] * 3
    first = last
    side = [last[0]] * 2
    for k in range(levels - 1, -1, -1):
        if k < levels - 1:
            share = jnp.where(k + 1 < deep, mixing[k], 0.0) * inverse[k]
            current = passed[k] + share * current
        h = jnp.where(k < deep, current, 0.0)
        weight[k] = h
        c = tracer[k]
        speed_x = east[k] * (1.0 / 12.0)
        speed_y = north[k] * (1.0 / 12.0)
        items = (c, h, speed_x)
        last = [pack_last(k, item[:, -lanes:], packed) for item, packed in zip(items, last)]
        first = [pack_first(k, item[:, :lanes], packed) for item, packed in zip(items, first)]
        items = (speed_y, mixing[k]) if k < levels - 1 else (speed_y,)
        for i, item in enumerate(items):
            tile = jnp.where(even_x, item[:, :lanes], item[:, -lanes:])
            lane = index(tile.shape, 1) - slot * k
            side[i] = jnp.where((lane >= 0) & (lane < 4), turned(tile, slot * k + 2, 1), side[i])
        pack_rows(k, levels, c, h, speed_y, k < shallow_y, up, down)
        at = 4 * levels + k
        down[at : at + 1, :] = speed_y[0:1]
        up[at : at + 1, :] = speed_y[rows - 1 :]
        beside[k : k + 1, :] = speed_y[1:2]
    depth_float = deep.astype(jnp.float32)
    at = 5 * levels
    up[at : at + sublanes, :] = jnp.broadcast_to(depth_float[rows - 1 :], (sublanes, columns))
    down[at : at + sublanes, :] = jnp.broadcast_to(depth_float[0:1], (sublanes, columns))
    choose(even_y, up, down, pay_even)
    choose(even_y, down, up, pay_odd)
    last.append(repeated(turned(depth_float[:, -lanes:], 4, 1)))
    first.append(repeated(turned(depth_float[:, :lanes], 2, 1)))
    last, first = jnp.concatenate(last, axis=1), jnp.concatenate(first, axis=1)
    speed_y, mixed = side
    speed_y = jnp.where(even_x, speed_y, turned(speed_y, 2, 1))
    mixed = jnp.where(even_x, turned(mixed, 4, 1), turned(mixed, 6, 1))
    side = jnp.where(lax.rem(index(mixed.shape, 1), slot) < 4, speed_y, mixed)
    pay_chip[...] = jnp.concatenate([jnp.where(even_x, first, last), side], axis=1)
    pay_core[...] = jnp.where(even_x, last, first)


def rows_of(ref, item, levels):
    return ref[item * levels : (item + 1) * levels, :]


def borders_y(levels, lower, upper, up, down, speeds, deep, deeps, border):
    c_far, c_near, h_near, g_near = (rows_of(lower, i, levels) for i in range(4))
    c_next, c_over, h_next, g_over = (rows_of(upper, i, levels) for i in range(4))
    c_two, c_one, h_one = (rows_of(up, i, levels) for i in range(3))
    c_zero, c_first, h_zero = (rows_of(down, i, levels) for i in range(3))
    speed_start, speed_first, speed_last, speed_end = speeds
    deep_before, deep_after = deeps
    end = deep.shape[0] - 1
    level = index(c_next.shape, 0).astype(jnp.float32)
    start_open = level < jnp.minimum(deep_before, deep[0:1])
    first_open = level < jnp.minimum(deep[0:1], deep[1:2])
    last_open = level < jnp.minimum(deep[end - 1 : end], deep[end:])
    end_open = level < jnp.minimum(deep[end:], deep_after)
    start = face_flux(c_zero, c_near, c_first, c_far, speed_start, start_open)
    first = jnp.where(first_open, -speed_first * c_near, 0.0)
    last = jnp.where(last_open, -speed_last * c_next, 0.0)
    finish = face_flux(c_next, c_one, c_over, c_two, speed_end, end_open)
    start_jump = jnp.where(start_open, h_zero - h_near, 0.0)
    end_jump = jnp.where(end_open, h_next - h_one, 0.0)
    start_carried = speed_start * start_jump
    end_carried = speed_end * end_jump
    values = (
        start - first,
        first,
        -last,
        last - finish,
        7.0 * start_carried - diffusivity * start_jump - g_near,
        -start_carried,
        -end_carried,
        7.0 * end_carried + diffusivity * end_jump - g_over,
    )
    for item, value in enumerate(values):
        border[item * levels : (item + 1) * levels, :] = value


def borders_x(before, after, first, last):
    shape = before[0].shape
    place = lax.rem(index(shape, 1), slot)
    level = lax.div(index(shape, 1), slot).astype(jnp.float32)

    def faces(items):
        c, h, speed, deep = items
        is_open = level < jnp.minimum(deep, turned(deep, 1, 1))
        flux = face_flux(c, turned(c, 1, 1), turned(c, -1, 1), turned(c, 2, 1), speed, is_open)
        jump = jnp.where(is_open, h - turned(h, 1, 1), 0.0)
        return is_open, flux, jump, speed * jump

    c, _, speed, _ = items = [jnp.where(place < 4, a, turned(b, 2, 1)) for a, b in zip(before, first)]
    is_open, flux, jump, carried = faces(items)
    inner = jnp.where((place == 5) & is_open, -speed * turned(c, 2, 1), 0.0)
    forward = jnp.where(place == 4, flux, inner) - turned(inner, -1, 1)
    backward = jnp.where(place == 4, 7.0 * carried - diffusivity * jump, 0.0) - turned(carried, 1, 1)
    c, _, speed, _ = items = [jnp.where(place < 2, turned(b, -2, 1), a) for a, b in zip(after, last)]
    is_open, flux, jump, carried = faces(items)
    inner = jnp.where((place == 1) & is_open, -speed * turned(c, -1, 1), 0.0)
    forward_end = inner - turned(jnp.where(place == 2, flux, inner), -1, 1)
    total = turned(7.0 * carried + diffusivity * jump, -1, 1)
    backward_end = jnp.where(place == 1, total, 0.0) - turned(carried, -2, 1)
    start = place < 2
    return (
        jnp.where(start, turned(forward, -4, 1), turned(forward_end, -2, 1)),
        jnp.where(start, turned(backward, -4, 1), turned(backward_end, -2, 1)),
    )


def bordered(k, levels, value, border, item, packed):
    rows, columns = value.shape
    row = index((sublanes, columns), 0)

    def line(which):
        at = (item + which) * levels + k
        return jnp.broadcast_to(border[at : at + 1, :], (sublanes, columns))

    tiles = split(value, 0)
    tiles[0] = tiles[0] + jnp.where(row == 0, line(0), jnp.where(row == 1, line(1), 0.0))
    added = jnp.where(row == sublanes - 2, line(2), jnp.where(row == sublanes - 1, line(3), 0.0))
    tiles[-1] = tiles[-1] + added
    value = jnp.concatenate(tiles, axis=0)
    lead = turned(packed, -slot * k, 1)
    lane = index(lead.shape, 1)
    tiles = [value[:, i : i + lanes] for i in range(0, columns, lanes)]
    tiles[0] = tiles[0] + jnp.where(lane < 2, lead, 0.0)
    tiles[-1] = tiles[-1] + jnp.where(lane >= lanes - 2, lead, 0.0)
    return jnp.concatenate(tiles, axis=1)


def step_levels(first, c, h, east_part, north_part, shallow):
    count, rows, columns = c.shape
    shallow_x, shallow_y = shallow
    level = index((count, rows, columns), 0) + first
    none = (0.0, 0.0, 0.0, 0.0)
    speeds = split(east_part * (1.0 / 12.0), 2)
    opens = split(level < shallow_x[None], 2)
    forward = explicit_flux(split(c, 2), speeds, opens, 2, none)
    backward = reverse_flux(split(h, 2), speeds, opens, 2, none)
    speeds = split(north_part * (1.0 / 12.0), 1)
    opens = split(level < shallow_y[None], 1)
    forward = forward + explicit_flux(split(c, 1), speeds, opens, 1, none)
    backward = backward + reverse_flux(split(h, 1), speeds, opens, 1, none)
    return forward, h + backward


def inner_kernel(c_ref, h_ref, east, north, depth, *rest):
    *tracer, forward, linear = rest
    levels, rows, columns = c_ref.shape
    deep = depth[...]
    lane, row = index(deep.shape, 1), index(deep.shape, 0)
    shallow_x = jnp.where(lane == 0, 0, jnp.minimum(deep, turned(deep, 1, 1)))
    shallow_y = jnp.where(row == 0, 0, jnp.minimum(deep, turned(deep, 1, 0)))
    for k in range(0, levels, group_size):
        part = slice(k, min(k + group_size, levels))
        c, h = c_ref[part], h_ref[part]
        ahead, back = step_levels(k, c, h, east[part], north[part], (shallow_x, shallow_y))
        if tracer:
            back = back - (2.0 * uptake) * tracer[0][part] * h
        linear[part] = back
        forward[part] = c + ahead - uptake * c * c


def item_of(value, item):
    return value[:, item * lanes : (item + 1) * lanes]


def take(flag, core, chip):
    return jnp.where(flag, chip, core), jnp.where(flag, core, chip)


def common(ref):
    return ref[:, : 4 * lanes]


def strip_rows(levels, message, up, down):
    c, h, _, deep, side = (item_of(message, i) for i in range(5))
    size = c.shape[0]
    level = lax.div(index(c.shape, 1), slot).astype(jnp.float32)
    is_open = level < jnp.minimum(deep, turned(deep, 1, 0))
    carried = jnp.where(is_open, side * (h - turned(h, 1, 0)), 0.0)
    at = 4 * levels
    for ref in (up, down):
        ref[at : at + sublanes, :] = jnp.zeros((sublanes, ref.shape[1]), jnp.float32)
    end = size - 1
    above = (c[end - 1 : end], c[end:], h[end:], carried[end:], deep[end:])
    below = (c[0:1], c[1:2], h[0:1], carried[1:2], deep[0:1], side[0:1])
    for ref, lines in ((up, above), (down, below)):
        for i, line in enumerate(lines):
            ref[at + i : at + i + 1, :lanes] = line


def strip_states(levels, message, own, lower, upper, even):
    c, h, speed, deep, side = (item_of(message, i) for i in range(5))
    shape = c.shape
    place = lax.rem(index(shape, 1), slot)
    level = lax.div(index(shape, 1), slot).astype(jnp.float32)
    from_own = place - jnp.where(even, 4, 0)
    from_own = (from_own == 0) | (from_own == 1)

    def joined(item, value):
        mine = item_of(own, item)
        return jnp.where(from_own, jnp.where(even, turned(mine, 2, 1), turned(mine, -2, 1)), value)

    c, h, speed, deep = (joined(i, value) for i, value in enumerate((c, h, speed, deep)))
    is_open = level < jnp.minimum(deep, turned(deep, 1, 1))
    flux = face_flux(c, turned(c, 1, 1), turned(c, -1, 1), turned(c, 2, 1), speed, is_open)
    jump = jnp.where(is_open, h - turned(h, 1, 1), 0.0)
    carried = speed * jump
    plus = 7.0 * carried + diffusivity * jump
    minus = 7.0 * carried - diffusivity * jump
    forward = flux - turned(flux, -1, 1)
    backward = minus + turned(plus, -1, 1) - turned(carried, 1, 1) - turned(carried, -2, 1)

    def line(ref, item):
        at = 4 * levels + item
        return jnp.broadcast_to(ref[at : at + 1, :lanes], (sublanes, lanes))

    def row_of(value, at):
        return jnp.broadcast_to(value[at : at + 1], (sublanes, lanes))

    rows = shape[0]
    row = index((sublanes, lanes), 0)
    tile_level = level[:sublanes]
    previous = turned(deep, 1, 0)
    previous = jnp.concatenate([jnp.where(row == 0, line(lower, 4), previous[:sublanes]), previous[sublanes:]], axis=0)
    opens = split(level < jnp.minimum(deep, previous), 0)
    speeds = split(side, 0)
    is_open = tile_level < jnp.minimum(line(upper, 4), row_of(deep, rows - 1))
    speed_end = line(upper, 5)
    c_one, c_two = row_of(c, rows - 1), row_of(c, rows - 2)
    flux = face_flux(line(upper, 0), c_one, line(upper, 1), c_two, speed_end, is_open)
    jump = jnp.where(is_open, line(upper, 2) - row_of(h, rows - 1), 0.0)
    carried = speed_end * jump
    plus = 7.0 * carried + diffusivity * jump
    edges = (line(lower, 1), jnp.where(row == 0, line(lower, 0), line(lower, 1)), line(upper, 0), flux)
    forward = forward + explicit_flux(split(c, 0), speeds, opens, 0, edges)
    edges = (line(lower, 2), plus, line(lower, 3), jnp.where(row == sublanes - 2, carried, line(upper, 3)))
    backward = backward + reverse_flux(split(h, 0), speeds, opens, 0, edges)
    right = jnp.where(level < deep, c + forward - uptake * c * c, 0.0)
    linear = h + backward
    kept = (place == 2) | (place == 3)
    links = jnp.where(kept & (level + 1.0 < deep), turned(side, -4, 1), 0.0)

    def ready(value):
        return jnp.where(even, turned(value, -4, 1), turned(value, -2, 1))

    def levels_of(value):
        value = ready(value)
        return [turned(value, -slot * k, 1) for k in range(levels)]

    right, linear, links, weights = (levels_of(value) for value in (right, linear, links, h))
    deep = ready(deep)
    inverse, passed = [], []
    above = jnp.zeros(shape, jnp.float32)
    share = above
    current = above
    for k in range(levels):
        inv = 1.0 / (1.0 + links[k] + (above - above * share))
        current = (right[k] + above * current) * inv
        share = links[k] * inv
        above = links[k]
        inverse.append(inv)
        passed.append(current)
    state = [current]
    for k in range(levels - 2, -1, -1):
        current = passed[k] + (links[k] * inverse[k]) * current
        state.insert(0, current)
    passed = []
    current = jnp.zeros(shape, jnp.float32)
    for k in range(levels):
        value = linear[k] - (2.0 * uptake) * state[k] * weights[k]
        if k > 0:
            value = value + links[k - 1] * current
        current = value * inverse[k]
        passed.append(current)
    weight = [current]
    for k in range(levels - 2, -1, -1):
        current = passed[k] + (links[k] * inverse[k]) * current
        weight.insert(0, current)
    lane = index(shape, 1)
    packed_state = jnp.zeros(shape, jnp.float32)
    packed_weight = packed_state
    for k in range(levels):
        here = lax.rem(lane + (lanes + 2 - slot * k), lanes) < 4
        packed_state = jnp.where(here, turned(state[k], slot * k, 1), packed_state)
        value = jnp.where(k < deep, weight[k], 0.0)
        packed_weight = jnp.where(here, turned(value, slot * k, 1), packed_weight)
    back = lambda value: jnp.where(even, turned(value, 4, 1), turned(value, 2, 1))
    return back(packed_state), back(packed_weight)


def first_kernel(
    north, mixing, depth, inverse, weight, forward, linear, own_up, own_down, beside, sent_chip, sent_core,
    got_even, got_odd, got_chip, got_core,
    state, weight_next, pay_even, pay_odd, pay_core, up, down, own_first, own_last,
    passed, lower, upper, border,
):
    levels, rows, columns = weight.shape
    even_y, even_x = parities()
    choose(even_y, got_odd, got_even, lower)
    choose(even_y, got_even, got_odd, upper)
    before, after = take(even_x, got_core[...], common(got_chip))
    last, first = take(even_x, common(sent_chip), sent_core[...])
    deep = depth[...]
    depth_float = deep.astype(jnp.float32)
    at = 5 * levels
    speeds = (rows_of(own_down, 4, levels), beside[...], rows_of(own_up, 4, levels), rows_of(upper, 4, levels))
    deeps = (lower[at : at + 1, :], upper[at : at + 1, :])
    borders_y(levels, lower, upper, own_up, own_down, speeds, depth_float, deeps, border)
    four = lambda value: [item_of(value, i) for i in range(4)]
    packed = borders_x(four(before), four(after), four(first), four(last))
    current = jnp.zeros((rows, columns), jnp.float32)
    above = current
    for k in range(levels):
        right = bordered(k, levels, forward[k], border, 0, packed[0])
        current = (jnp.where(k < deep, right, 0.0) + above * current) * inverse[k]
        passed[k] = current
        if k < levels - 1:
            above = jnp.where(k + 1 < deep, mixing[k], 0.0)
    state[levels - 1] = current
    for k in range(levels - 2, -1, -1):
        current = passed[k] + (jnp.where(k + 1 < deep, mixing[k], 0.0) * inverse[k]) * current
        state[k] = current
    current = jnp.zeros((rows, columns), jnp.float32)
    for k in range(levels):
        right = bordered(k, levels, linear[k], border, 4, packed[1]) - (2.0 * uptake) * state[k] * weight[k]
        if k > 0:
            right = right + jnp.where(k < deep, mixing[k - 1], 0.0) * current
        current = right * inverse[k]
        passed[k] = current
    last = [jnp.zeros((rows, lanes), jnp.float32)] * 2
    first = last
    shallow_y = jnp.minimum(deep, turned(deep, 1, 0))
    for k in range(levels - 1, -1, -1):
        if k < levels - 1:
            current = passed[k] + (jnp.where(k + 1 < deep, mixing[k], 0.0) * inverse[k]) * current
        h = jnp.where(k < deep, current, 0.0)
        weight_next[k] = h
        c = state[k]
        items = (c, h)
        last = [pack_last(k, item[:, -lanes:], packed) for item, packed in zip(items, last)]
        first = [pack_first(k, item[:, :lanes], packed) for item, packed in zip(items, first)]
        pack_rows(k, levels, c, h, north[k] * (1.0 / 12.0), k < shallow_y, up, down)
    strip_rows(levels, got_chip[...], up, down)
    choose(even_y, up, down, pay_even)
    choose(even_y, down, up, pay_odd)
    last, first = jnp.concatenate(last, axis=1), jnp.concatenate(first, axis=1)
    own_first[...] = first
    own_last[...] = last
    pay_core[...] = jnp.where(even_x, last, first)


def second_kernel(
    mixing, depth, inverse, forward, linear, own_up, own_down, own_first, own_last,
    first_up, first_down, beside, sent_chip, sent_core,
    got1_even, got1_odd, got1_chip, got1_core, got_even, got_odd, got_core,
    final_far, adjoint_far,
    final, adjoint, passed, lower, upper, border, sent,
):
    copies = []

    def send(near, far, part):
        copy = pltpu.make_async_copy(near.at[part], far.at[part], sent.at[len(copies)])
        copy.start()
        copies.append(copy)

    levels, rows, columns = forward.shape
    even_y, even_x = parities()
    choose(even_y, got_odd, got_even, lower)
    choose(even_y, got_even, got_odd, upper)
    before1, after1 = take(even_x, got1_core[...], common(got1_chip))
    last1, first1 = take(even_x, common(sent_chip), sent_core[...])
    strip = strip_states(levels, got1_chip[...], sent_chip[...], lower, upper, even_x)
    before, after = take(even_x, got_core[...], jnp.concatenate(strip, axis=1))
    deep = depth[...]
    depth_float = deep.astype(jnp.float32)
    at = 5 * levels
    deeps = (
        jnp.where(even_y, got1_odd[at : at + 1, :], got1_even[at : at + 1, :]),
        jnp.where(even_y, got1_even[at : at + 1, :], got1_odd[at : at + 1, :]),
    )
    speed = jnp.where(even_y, rows_of(got1_even, 4, levels), rows_of(got1_odd, 4, levels))
    speeds = (rows_of(first_down, 4, levels), beside[...], rows_of(first_up, 4, levels), speed)
    borders_y(levels, lower, upper, own_up, own_down, speeds, depth_float, deeps, border)

    def four(value, fixed):
        return [item_of(value, 0), item_of(value, 1), item_of(fixed, 2), item_of(fixed, 3)]

    sides = ((before, before1), (after, after1), (own_first, first1), (own_last, last1))
    packed = borders_x(*(four(*side) for side in sides))
    current = jnp.zeros((rows, columns), jnp.float32)
    above = current
    for k in range(levels):
        adjoint[k] = bordered(k, levels, linear[k], border, 4, packed[1])
        right = bordered(k, levels, forward[k], border, 0, packed[0])
        current = (jnp.where(k < deep, right, 0.0) + above * current) * inverse[k]
        passed[k] = current
        if k < levels - 1:
            above = jnp.where(k + 1 < deep, mixing[k], 0.0)
        if (k + 1) % group_size == 0 or k == levels - 1:
            send(adjoint, adjoint_far, slice(k // group_size * group_size, k + 1))
    final[levels - 1] = current
    for k in range(levels - 2, -1, -1):
        current = passed[k] + (jnp.where(k + 1 < deep, mixing[k], 0.0) * inverse[k]) * current
        final[k] = current
        if k % group_size == 0:
            send(final, final_far, slice(k, min(k + group_size, levels)))
    for copy in copies:
        copy.wait()


def pairs(axis, parity):
    devices = lax.axis_size(axis)
    swaps = []
    for i in range(parity, devices - 1, 2):
        swaps += [(i, i + 1), (i + 1, i)]
    return swaps


def exchange(pay_even, pay_odd, *pay):
    got_even = lax.ppermute(pay_even, "group", pairs("group", 0))
    got_odd = lax.ppermute(pay_odd, "group", pairs("group", 1))
    got = [lax.ppermute(each, "tile", pairs("tile", len(pay) - 1 - i)) for i, each in enumerate(pay)]
    return got_even, got_odd, *got


def shards(tracer, east_speed, north_speed, mixing, depth_levels, sensitivity):
    levels, rows, columns = tracer.shape
    assert levels * slot == lanes and rows % sublanes == 0 and columns % lanes == 0
    f32 = jnp.float32
    field = jax.ShapeDtypeStruct((levels, rows, columns), f32)
    first_size = 5 * levels + sublanes
    second_size = 4 * levels + sublanes
    border_size = 8 * levels
    block = pltpu.VMEM((levels, rows, columns), f32)
    params = pltpu.CompilerParams(vmem_limit_bytes=32 * 1024 * 1024)
    far = pl.BlockSpec(memory_space=pl.ANY)

    def lines(size):
        return jax.ShapeDtypeStruct((size, columns), f32)

    def space(size):
        return pltpu.VMEM((size, columns), f32)

    def tiles(count):
        return jax.ShapeDtypeStruct((rows, count * lanes), f32)

    given = (tracer, east_speed, north_speed, mixing, depth_levels)
    near = tuple(jax.ShapeDtypeStruct(array.shape, array.dtype) for array in given)
    distant = [pltpu.with_memory_space_constraint(array, pltpu.HBM) for array in given + (sensitivity,)]
    outcome = pl.pallas_call(
        factor_kernel,
        in_specs=[far] * 6,
        out_shape=near
        + (field, field, lines(first_size), lines(first_size), tiles(5), tiles(4), lines(first_size), lines(first_size), lines(levels)),
        scratch_shapes=[block, block, pltpu.SemaphoreType.DMA((6,))],
        compiler_params=params,
    )(*distant)
    tracer, east_speed, north_speed, mixing, depth_levels, inverse, weight, *messages, up, down, beside = outcome
    cells = levels * rows * columns
    inner = pl.CostEstimate(flops=80 * cells, bytes_accessed=24 * cells, transcendentals=0)

    def inside(c, h, *more):
        return pl.pallas_call(inner_kernel, out_shape=(field, field), compiler_params=params, cost_estimate=inner)(
            c, h, east_speed, north_speed, depth_levels, *more
        )

    got1 = exchange(*messages)
    sent1 = messages[2:]
    parts = inside(tracer, weight)
    state, weight_next, *messages, up2, down2, first2, last2 = pl.pallas_call(
        first_kernel,
        out_shape=(field, field, lines(second_size), lines(second_size), tiles(2))
        + (lines(second_size), lines(second_size), tiles(2), tiles(2)),
        scratch_shapes=[block, space(first_size), space(first_size), space(border_size)],
        compiler_params=params,
    )(north_speed, mixing, depth_levels, inverse, weight, *parts, up, down, beside, *sent1, *got1)
    got2 = exchange(*messages)
    parts = inside(state, weight_next, tracer)
    sends = pltpu.SemaphoreType.DMA((2 * -(-levels // group_size),))
    final, adjoint = pl.pallas_call(
        second_kernel,
        out_specs=[far] * 2,
        out_shape=(field, field),
        scratch_shapes=[block, block, block, space(second_size), space(second_size), space(border_size), sends],
        compiler_params=params,
    )(mixing, depth_levels, inverse, *parts, up2, down2, first2, last2, up, down, beside, *sent1, *got1, *got2)
    return final, adjoint


def solution(mesh):
    block = P(None, "group", "tile")
    in_specs = (block, block, block, block, P("group", "tile"), block)
    return jax.shard_map(shards, mesh=mesh, in_specs=in_specs, out_specs=(block, block), check_vma=False)
```

```python
import jax
import jax.numpy as jnp
from jax import lax
from jax.experimental import pallas as pl
from jax.experimental.pallas import tpu as pltpu
from jax.sharding import PartitionSpec as P

diffusivity = 0.1
uptake = 0.2
lanes = 128
sublanes = 8
group_size = 8

slot = 8


def turned(value, shift, axis):
    return pltpu.roll(value, shift % value.shape[axis], axis)


def index(shape, axis):
    return lax.broadcasted_iota(jnp.int32, shape, axis)


def parities():
    return lax.rem(lax.axis_index("group"), 2) == 0, lax.rem(lax.axis_index("tile"), 2) == 0


def split(value, axis):
    step = lanes if axis == 2 else sublanes
    return [lax.slice_in_dim(value, i, i + step, axis=axis) for i in range(0, value.shape[axis], step)]


def shifted(tiles, shift, axis, edge):
    span = tiles[0].shape[axis]
    moved = [turned(tile, shift, axis) for tile in tiles]
    place = index(tiles[0].shape, axis)
    if shift > 0:
        return [jnp.where(place < shift, a, b) for a, b in zip([edge] + moved[:-1], moved)]
    return [jnp.where(place >= span + shift, a, b) for a, b in zip(moved[1:] + [edge], moved)]


def face_flux(c, behind, ahead, far, speed, is_open):
    flux = speed * (7.0 * (c + behind) - (ahead + far)) - diffusivity * (c - behind)
    return jnp.where(is_open, flux, 0.0)


def explicit_flux(tiles, speeds, opens, axis, edges):
    edge_behind, edge_far, edge_ahead, edge_flux = edges
    behind = shifted(tiles, 1, axis, edge_behind)
    ahead = shifted(tiles, -1, axis, edge_ahead)
    far = shifted(tiles, 2, axis, edge_far)
    flux = [face_flux(*each) for each in zip(tiles, behind, ahead, far, speeds, opens)]
    following = shifted(flux, -1, axis, edge_flux)
    return jnp.concatenate([g - n for g, n in zip(flux, following)], axis=axis)


def reverse_flux(tiles, speeds, opens, axis, edges):
    edge_behind, edge_sum, edge_carried, edge_far = edges
    behind = shifted(tiles, 1, axis, edge_behind)
    jump = [jnp.where(o, h - b, 0.0) for h, b, o in zip(tiles, behind, opens)]
    carried = [s * j for s, j in zip(speeds, jump)]
    seven = [7.0 * g for g in carried]
    spread = [diffusivity * j for j in jump]
    ahead = shifted([a + b for a, b in zip(seven, spread)], -1, axis, edge_sum)
    back = shifted(carried, 1, axis, edge_carried)
    far = shifted(carried, -2, axis, edge_far)
    parts = zip(seven, spread, ahead, back, far)
    return jnp.concatenate([(a - b) + c - d - e for a, b, c, d, e in parts], axis=axis)


def level_of(lane):
    return lax.div(lax.rem(lane + slot // 2, lanes), slot)


def pack_columns(k, item, packed):
    lane = index(packed.shape, 1)
    tile = jnp.where(lane < lanes // 2, item[:, :lanes], item[:, -lanes:])
    return jnp.where(level_of(lane) == k, turned(tile, slot * k, 1), packed)


def repeated(value):
    lane = index((value.shape[0], lanes), 1)
    value = jnp.where(lane < lanes // 2, value[:, :lanes], value[:, -lanes:])
    value = jnp.where(level_of(lane) == 0, value, 0.0)
    width = slot
    while width < lanes:
        value = value + turned(value, width, 1)
        width *= 2
    return value


def pack_rows(k, levels, c, h, speed, open_y, up, down):
    size = c.shape[0]
    last = slice(size - sublanes, size)
    first = slice(0, sublanes)
    g_last = jnp.where(open_y[last], speed[last] * (h[last] - turned(h[last], 1, 0)), 0.0)
    g_first = jnp.where(open_y[first], speed[first] * (h[first] - turned(h[first], 1, 0)), 0.0)
    above = (c[size - 2 : size - 1], c[size - 1 :], h[size - 1 :], g_last[sublanes - 1 :])
    below = (c[0:1], c[1:2], h[0:1], g_first[1:2])
    for item in range(4):
        at = item * levels + k
        up[at : at + 1, :] = above[item]
        down[at : at + 1, :] = below[item]


def inward(levels, scaled, links, inverse, joint, passed):
    middle = levels // 2
    top = bottom = None
    for i in range(levels - middle):
        k = levels - 1 - i
        bottom = scaled(k) if i == 0 else scaled(k) + (links[k] * inverse[k]) * bottom
        passed[k] = bottom
        if i < middle:
            top = scaled(i) if i == 0 else scaled(i) + (links[i - 1] * inverse[i]) * top
            passed[i] = top
    link = links[middle - 1]
    top = (top + (link * inverse[middle - 1]) * bottom) * joint
    return top, bottom + (link * inverse[middle]) * top


def outward(levels, ends, links, inverse, passed):
    middle = levels // 2
    top, bottom = ends
    yield middle - 1, top
    yield middle, bottom
    for i in range(1, levels - middle):
        k = middle + i
        bottom = passed[k] + (links[k - 1] * inverse[k]) * bottom
        yield k, bottom
        k = middle - 1 - i
        if k >= 0:
            top = passed[k] + (links[k] * inverse[k]) * top
            yield k, top


def factorized(levels, links, inverse):
    middle = levels // 2

    def pivots(order, near, far):
        share = None
        for k in order:
            pivot = 1.0
            if 0 <= far(k) < levels - 1:
                pivot = pivot + links[far(k)]
            if share is not None:
                pivot = pivot + (links[near(k)] - links[near(k)] * share)
            inverse[k] = 1.0 / pivot
            if 0 <= far(k) < levels - 1:
                share = links[far(k)] * inverse[k]
            yield

    down = pivots(range(middle), lambda k: k - 1, lambda k: k)
    up = pivots(range(levels - 1, middle - 1, -1), lambda k: k, lambda k: k - 1)
    for _ in range(levels - middle):
        next(up)
        next(down, None)
    link = links[middle - 1]
    return 1.0 / (1.0 - (link * inverse[middle - 1]) * (link * inverse[middle]))


def choose(flag, ref_true, ref_false, into):
    into[...] = jnp.where(flag, ref_true[...], ref_false[...])


def factor_kernel(
    tracer_far, east_far, north_far, mixing_far, depth_far, sensitivity_far,
    tracer, east, north, depth, links, inverse, joint, weight, pay_even, pay_odd, outer, pay_core, up, down, beside,
    mixing, sensitivity, passed, arrived,
):
    order = (
        (depth_far, depth),
        (mixing_far, mixing),
        (sensitivity_far, sensitivity),
        (tracer_far, tracer),
        (east_far, east),
        (north_far, north),
    )
    copies = [pltpu.make_async_copy(far, near, arrived.at[i]) for i, (far, near) in enumerate(order)]
    for copy in copies:
        copy.start()
    levels, rows, columns = tracer.shape
    even_y, _ = parities()
    copies[0].wait()
    deep = depth[...]
    depth_float = deep.astype(jnp.float32)
    outer[:, 3 * lanes : 4 * lanes] = repeated(depth_float)
    for copy in copies[1:3]:
        copy.wait()
    shallow_y = jnp.minimum(deep, turned(deep, 1, 0))
    for k in range(levels - 1):
        links[k] = jnp.where(k + 1 < deep, mixing[k], 0.0)
    joint[...] = factorized(levels, links, inverse)
    ends = inward(levels, lambda k: sensitivity[k] * inverse[k], links, inverse, joint[...], passed)
    for copy in copies[3:]:
        copy.wait()
    packed = [jnp.zeros((rows, lanes), jnp.float32)] * 5
    for k, current in outward(levels, ends, links, inverse, passed):
        h = jnp.where(k < deep, current, 0.0)
        weight[k] = h
        c = tracer[k]
        speed_x = east[k] * (1.0 / 12.0)
        speed_y = north[k] * (1.0 / 12.0)
        items = (c, h, speed_x, speed_y) + ((mixing[k],) if k < levels - 1 else ())
        packed[: len(items)] = [pack_columns(k, *each) for each in zip(items, packed)]
        pack_rows(k, levels, c, h, speed_y, k < shallow_y, up, down)
        at = 4 * levels + k
        down[at : at + 1, :] = speed_y[0:1]
        up[at : at + 1, :] = speed_y[rows - 1 :]
        beside[k : k + 1, :] = speed_y[1:2]
    for place, value in zip((0, 1, 2, 4, 5), packed):
        outer[:, place * lanes : (place + 1) * lanes] = value
    pay_core[...] = common(outer)
    at = 5 * levels
    up[at : at + sublanes, :] = jnp.broadcast_to(depth_float[rows - 1 :], (sublanes, columns))
    down[at : at + sublanes, :] = jnp.broadcast_to(depth_float[0:1], (sublanes, columns))
    choose(even_y, up, down, pay_even)
    choose(even_y, down, up, pay_odd)


def rows_of(ref, item, levels):
    return ref[item * levels : (item + 1) * levels, :]


def border_rows(level, lower, upper, up, down, speeds, deeps):
    c_far, c_near, h_near, g_near = lower
    c_next, c_over, h_next, g_over = upper
    c_two, c_one, h_one = up
    c_zero, c_first, h_zero = down
    speed_start, speed_first, speed_last, speed_end = speeds
    before, zero, one, two_last, last, after = deeps
    start_open = level < jnp.minimum(before, zero)
    first_open = level < jnp.minimum(zero, one)
    last_open = level < jnp.minimum(two_last, last)
    end_open = level < jnp.minimum(last, after)
    start = face_flux(c_zero, c_near, c_first, c_far, speed_start, start_open)
    first = jnp.where(first_open, -speed_first * c_near, 0.0)
    final = jnp.where(last_open, -speed_last * c_next, 0.0)
    finish = face_flux(c_next, c_one, c_over, c_two, speed_end, end_open)
    start_jump = jnp.where(start_open, h_zero - h_near, 0.0)
    end_jump = jnp.where(end_open, h_next - h_one, 0.0)
    start_carried = speed_start * start_jump
    end_carried = speed_end * end_jump
    return (
        start - first,
        first,
        -final,
        final - finish,
        7.0 * start_carried - diffusivity * start_jump - g_near,
        -start_carried,
        -end_carried,
        7.0 * end_carried + diffusivity * end_jump - g_over,
    )


def borders_y(levels, lower, upper, up, down, speeds, deep, deeps, border):
    end = deep.shape[0] - 1
    deeps = (deeps[0], deep[0:1], deep[1:2], deep[end - 1 : end], deep[end:], deeps[1])
    several = lambda ref, count: [rows_of(ref, i, levels) for i in range(count)]
    level = index((levels, deep.shape[1]), 0).astype(jnp.float32)
    values = border_rows(level, several(lower, 4), several(upper, 4), several(up, 3), several(down, 3), speeds, deeps)
    for item, value in enumerate(values):
        border[item * levels : (item + 1) * levels, :] = value


def placed(shape):
    lane = index(shape, 1)
    return lax.rem(lane, slot), level_of(lane).astype(jnp.float32)


def borders_x(before, after, own):
    place, level = placed(own[0].shape)
    start = place < slot // 2
    at = lambda value, distance: turned(value, -distance, 1)
    c, h, speed, deep = (jnp.where(start, mine, other) for mine, other in zip(own, before))
    deep_back = at(deep, -1)
    is_open = level < jnp.minimum(deep, deep_back)
    next_open = level < jnp.minimum(deep, at(deep, 1))
    back_open = level < jnp.minimum(deep_back, at(deep, -2))
    behind, far = at(c, -1), at(c, -2)
    flux = face_flux(c, behind, at(c, 1), far, speed, is_open) + jnp.where(next_open, at(speed, 1) * behind, 0.0)
    forward = jnp.where(place == 0, flux, jnp.where(is_open, -speed * far, 0.0))
    h_back = at(h, -1)
    jump = jnp.where(is_open, h - h_back, 0.0)
    back = jnp.where(back_open, at(speed, -1) * (h_back - at(h, -2)), 0.0)
    backward = jnp.where(place == 0, 7.0 * (speed * jump) - diffusivity * jump, 0.0) - back
    c, h, speed, deep = (jnp.where(start, other, mine) for mine, other in zip(own, after))
    deep_next = at(deep, 1)
    is_open = level < jnp.minimum(deep, at(deep, -1))
    next_open = level < jnp.minimum(deep, deep_next)
    over_open = level < jnp.minimum(deep_next, at(deep, 2))
    c_next, c_over, speed_next = at(c, 1), at(c, 2), at(speed, 1)
    flux = face_flux(c_next, c, c_over, at(c, -1), speed_next, next_open) + jnp.where(is_open, speed * c_next, 0.0)
    forward_end = jnp.where(place == slot - 1, -flux, jnp.where(next_open, speed_next * c_over, 0.0))
    h_next = at(h, 1)
    jump = jnp.where(next_open, h_next - h, 0.0)
    over = jnp.where(over_open, at(speed, 2) * (at(h, 2) - h_next), 0.0)
    total = 7.0 * (speed_next * jump) + diffusivity * jump
    backward_end = jnp.where(place == slot - 1, total, 0.0) - over
    return jnp.where(start, forward, forward_end), jnp.where(start, backward, backward_end)


def with_rows(k, levels, value, border, item):
    rows, columns = value.shape
    row = index((sublanes, columns), 0)

    def line(which):
        at = (item + which) * levels + k
        return jnp.broadcast_to(border[at : at + 1, :], (sublanes, columns))

    tiles = split(value, 0)
    tiles[0] = tiles[0] + jnp.where(row == 0, line(0), jnp.where(row == 1, line(1), 0.0))
    added = jnp.where(row == sublanes - 2, line(2), jnp.where(row == sublanes - 1, line(3), 0.0))
    tiles[-1] = tiles[-1] + added
    return jnp.concatenate(tiles, axis=0)


def with_columns(k, value, packed):
    lead = turned(packed, -slot * k, 1)
    lane = index(lead.shape, 1)
    tiles = [value[:, i : i + lanes] for i in range(0, value.shape[1], lanes)]
    tiles[0] = tiles[0] + jnp.where(lane < 2, lead, 0.0)
    tiles[-1] = tiles[-1] + jnp.where(lane >= lanes - 2, lead, 0.0)
    return jnp.concatenate(tiles, axis=1)


def step_levels(first, c, h, east_part, north_part, shallow):
    count, rows, columns = c.shape
    shallow_x, shallow_y = shallow
    level = index((count, rows, columns), 0) + first
    none = (0.0, 0.0, 0.0, 0.0)
    speeds = split(east_part * (1.0 / 12.0), 2)
    opens = split(level < shallow_x[None], 2)
    forward = explicit_flux(split(c, 2), speeds, opens, 2, none)
    backward = reverse_flux(split(h, 2), speeds, opens, 2, none)
    speeds = split(north_part * (1.0 / 12.0), 1)
    opens = split(level < shallow_y[None], 1)
    forward = forward + explicit_flux(split(c, 1), speeds, opens, 1, none)
    backward = backward + reverse_flux(split(h, 1), speeds, opens, 1, none)
    return forward, h + backward


def inner_kernel(c_ref, h_ref, east, north, depth, *rest):
    *tracer, forward, linear = rest
    levels, rows, columns = c_ref.shape
    deep = depth[...]
    lane, row = index(deep.shape, 1), index(deep.shape, 0)
    shallow_x = jnp.where(lane == 0, 0, jnp.minimum(deep, turned(deep, 1, 1)))
    shallow_y = jnp.where(row == 0, 0, jnp.minimum(deep, turned(deep, 1, 0)))
    for k in range(0, levels, group_size):
        part = slice(k, min(k + group_size, levels))
        c, h = c_ref[part], h_ref[part]
        ahead, back = step_levels(k, c, h, east[part], north[part], (shallow_x, shallow_y))
        if tracer:
            back = back - (2.0 * uptake) * tracer[0][part] * h
        linear[part] = back
        forward[part] = c + ahead - uptake * c * c


def item_of(value, item):
    return value[:, item * lanes : (item + 1) * lanes]


def take(flag, core, chip):
    return jnp.where(flag, chip, core), jnp.where(flag, core, chip)


def common(ref):
    return ref[:, : 4 * lanes]


def strip_rows(levels, message, up, down):
    c, h, deep, side = (item_of(message, i) for i in (0, 1, 3, 4))
    size = c.shape[0]
    _, level = placed(c.shape)
    is_open = level < jnp.minimum(deep, turned(deep, 1, 0))
    carried = jnp.where(is_open, side * (h - turned(h, 1, 0)), 0.0)
    at = 4 * levels
    for ref in (up, down):
        ref[at : at + sublanes, :] = jnp.zeros((sublanes, ref.shape[1]), jnp.float32)
    end = size - 1
    above = (c[end - 1 : end], c[end:], h[end:], carried[end:], deep[end:])
    below = (c[0:1], c[1:2], h[0:1], carried[1:2], deep[0:1], side[0:1])
    for ref, lines in ((up, above), (down, below)):
        for i, line in enumerate(lines):
            ref[at + i : at + i + 1, :lanes] = line


def second_inner_kernel(
    c_ref, h_ref, east, north, depth, tracer, outer, got_chip,
    forward, linear, base, strip_links, strip_inverse, strip_joint, strip_weight,
):
    inner_kernel(c_ref, h_ref, east, north, depth, tracer, forward, linear)
    levels = c_ref.shape[0]
    _, even = parities()
    place, level = placed((outer.shape[0], lanes))
    ours = (place < slot // 2) == even
    c, h, speed, deep = (jnp.where(ours, item_of(outer, i), item_of(got_chip, i)) for i in range(4))
    side, mixed = item_of(got_chip, 4), item_of(got_chip, 5)
    is_open = level < jnp.minimum(deep, turned(deep, 1, 1))
    flux = face_flux(c, turned(c, 1, 1), turned(c, -1, 1), turned(c, 2, 1), speed, is_open)
    jump = jnp.where(is_open, h - turned(h, 1, 1), 0.0)
    carried = speed * jump
    plus = 7.0 * carried + diffusivity * jump
    minus = 7.0 * carried - diffusivity * jump
    step = c + (flux - turned(flux, -1, 1)) - uptake * c * c
    reverse = h + minus + turned(plus, -1, 1) - turned(carried, 1, 1) - turned(carried, -2, 1)
    previous = jnp.where(index(deep.shape, 0) == 0, 0.0, turned(deep, 1, 0))
    opens = split(level < jnp.minimum(deep, previous), 0)
    none = (0.0, 0.0, 0.0, 0.0)
    base[:, :lanes] = step + explicit_flux(split(c, 0), split(side, 0), opens, 0, none)
    base[:, lanes:] = reverse + reverse_flux(split(h, 0), split(side, 0), opens, 0, none)
    ours = (place == 0) | (place == 1) | (place == slot - 2) | (place == slot - 1)
    mixed = jnp.where(ours & (level + 1.0 < deep), mixed, 0.0)
    for k in range(levels):
        strip_weight[k] = turned(h, -slot * k, 1)
        if k < levels - 1:
            strip_links[k] = turned(mixed, -slot * k, 1)
    strip_joint[...] = factorized(levels, strip_links, strip_inverse)


def strip_states(levels, message, base, factors, weights, lower, upper):
    links, inverse, joint = factors
    c, h, deep, side = (item_of(message, i) for i in (0, 1, 3, 4))
    place, level = placed(c.shape)
    end = c.shape[0] - 1

    def line(ref, item):
        at = 4 * levels + item
        return jnp.broadcast_to(ref[at : at + 1, :lanes], (sublanes, lanes))

    def row_of(value, at):
        return jnp.broadcast_to(value[at : at + 1], (sublanes, lanes))

    values = border_rows(
        level[:sublanes],
        [line(lower, i) for i in range(4)],
        [line(upper, i) for i in range(4)],
        (row_of(c, end - 1), row_of(c, end), row_of(h, end)),
        (row_of(c, 0), row_of(c, 1), row_of(h, 0)),
        (row_of(side, 0), row_of(side, 1), row_of(side, end), line(upper, 5)),
        (line(lower, 4), row_of(deep, 0), row_of(deep, 1), row_of(deep, end - 1), row_of(deep, end), line(upper, 4)),
    )
    row = index((sublanes, lanes), 0)

    def bordered(value, rows):
        tiles = split(value, 0)
        tiles[0] = tiles[0] + jnp.where(row == 0, rows[0], jnp.where(row == 1, rows[1], 0.0))
        tiles[-1] = tiles[-1] + jnp.where(row == sublanes - 2, rows[2], jnp.where(row == sublanes - 1, rows[3], 0.0))
        return jnp.concatenate(tiles, axis=0)

    right = jnp.where(level < deep, bordered(base[:, :lanes], values[:4]), 0.0)
    linear = bordered(base[:, lanes:], values[4:])
    right, linear = ([turned(value, -slot * k, 1) for k in range(levels)] for value in (right, linear))
    passed = [None] * levels
    ends = inward(levels, lambda k: right[k] * inverse[k], links, inverse, joint, passed)
    state = dict(outward(levels, ends, links, inverse, passed))

    def scaled(k):
        return (linear[k] - (2.0 * uptake) * state[k] * weights[k]) * inverse[k]

    ends = inward(levels, scaled, links, inverse, joint, passed)
    weight = dict(outward(levels, ends, links, inverse, passed))
    packed_state = packed_weight = jnp.zeros(c.shape, jnp.float32)
    for k in range(levels):
        here = level == float(k)
        packed_state = jnp.where(here, turned(state[k], slot * k, 1), packed_state)
        value = jnp.where(k < deep, weight[k], 0.0)
        packed_weight = jnp.where(here, turned(value, slot * k, 1), packed_weight)
    return packed_state, packed_weight


def first_kernel(
    north, depth, links, inverse, joint, weight, forward, linear, own_up, own_down, beside, own,
    got_even, got_odd, got_chip, got_core,
    state, weight_next, pay_even, pay_odd, outer, up, down,
    passed, scaled, lower, upper, border,
):
    levels, rows, columns = weight.shape
    even_y, even_x = parities()
    choose(even_y, got_odd, got_even, lower)
    choose(even_y, got_even, got_odd, upper)
    before, after = take(even_x, got_core[...], common(got_chip))
    deep = depth[...]
    depth_float = deep.astype(jnp.float32)
    at = 5 * levels
    speeds = (rows_of(own_down, 4, levels), beside[...], rows_of(own_up, 4, levels), rows_of(upper, 4, levels))
    deeps = (lower[at : at + 1, :], upper[at : at + 1, :])
    borders_y(levels, lower, upper, own_up, own_down, speeds, depth_float, deeps, border)
    four = lambda value: [item_of(value, i) for i in range(4)]
    packed = borders_x(four(before), four(after), four(own))
    for k in range(levels):
        scaled[k] = with_rows(k, levels, forward[k], border, 0)
        state[k] = with_rows(k, levels, linear[k], border, 4)
    for k in range(levels):
        scaled[k] = jnp.where(k < deep, with_columns(k, scaled[k], packed[0]), 0.0) * inverse[k]
        state[k] = with_columns(k, state[k], packed[1])
    ends = inward(levels, lambda k: scaled[k], links, inverse, joint[...], passed)
    for k, current in outward(levels, ends, links, inverse, passed):
        scaled[k] = (state[k] - (2.0 * uptake) * current * weight[k]) * inverse[k]
        state[k] = current
    ends = inward(levels, lambda k: scaled[k], links, inverse, joint[...], passed)
    packed = [jnp.zeros((rows, lanes), jnp.float32)] * 2
    shallow_y = jnp.minimum(deep, turned(deep, 1, 0))
    for k, current in outward(levels, ends, links, inverse, passed):
        h = jnp.where(k < deep, current, 0.0)
        weight_next[k] = h
        c = state[k]
        packed = [pack_columns(k, *each) for each in zip((c, h), packed)]
        pack_rows(k, levels, c, h, north[k] * (1.0 / 12.0), k < shallow_y, up, down)
    strip_rows(levels, got_chip[...], up, down)
    choose(even_y, up, down, pay_even)
    choose(even_y, down, up, pay_odd)
    outer[...] = jnp.concatenate(packed, axis=1)


def second_kernel(
    depth, links, inverse, joint, forward, linear, base, strip_links, strip_inverse, strip_joint, strip_weight,
    own_up, own_down, own, first_up, first_down, beside, first_own,
    got1_even, got1_odd, got1_chip, got1_core, got_even, got_odd, got_core,
    final_far, adjoint_far,
    final, adjoint, passed, scaled, lower, upper, border, sent,
):
    copies = []

    def send(near, far, part):
        copy = pltpu.make_async_copy(near.at[part], far.at[part], sent.at[len(copies)])
        copy.start()
        copies.append(copy)

    levels, rows, columns = forward.shape
    even_y, even_x = parities()
    choose(even_y, got_odd, got_even, lower)
    choose(even_y, got_even, got_odd, upper)
    before1, after1 = take(even_x, got1_core[...], common(got1_chip))
    factors = (strip_links, strip_inverse, strip_joint[...])
    strip = strip_states(levels, got1_chip, base, factors, strip_weight, lower, upper)
    before, after = take(even_x, got_core[...], jnp.concatenate(strip, axis=1))
    deep = depth[...]
    depth_float = deep.astype(jnp.float32)
    at = 5 * levels
    deeps = (
        jnp.where(even_y, got1_odd[at : at + 1, :], got1_even[at : at + 1, :]),
        jnp.where(even_y, got1_even[at : at + 1, :], got1_odd[at : at + 1, :]),
    )
    speed = jnp.where(even_y, rows_of(got1_even, 4, levels), rows_of(got1_odd, 4, levels))
    speeds = (rows_of(first_down, 4, levels), beside[...], rows_of(first_up, 4, levels), speed)
    borders_y(levels, lower, upper, own_up, own_down, speeds, depth_float, deeps, border)

    def four(value, fixed):
        return [item_of(value, 0), item_of(value, 1), item_of(fixed, 2), item_of(fixed, 3)]

    sides = ((before, before1), (after, after1), (own, first_own))
    packed = borders_x(*(four(*side) for side in sides))
    for k in range(levels):
        adjoint[k] = with_rows(k, levels, linear[k], border, 4)
        scaled[k] = with_rows(k, levels, forward[k], border, 0)
    for k in range(levels):
        scaled[k] = jnp.where(k < deep, with_columns(k, scaled[k], packed[0]), 0.0) * inverse[k]
    for k in range(levels):
        adjoint[k] = with_columns(k, adjoint[k], packed[1])
    send(adjoint, adjoint_far, slice(0, levels))
    ends = inward(levels, lambda k: scaled[k], links, inverse, joint[...], passed)
    middle = levels // 2
    quarter = middle // 2
    for k, current in outward(levels, ends, links, inverse, passed):
        final[k] = current
        if k == middle - quarter:
            send(final, final_far, slice(middle - quarter, middle + quarter))
    send(final, final_far, slice(0, middle - quarter))
    send(final, final_far, slice(middle + quarter, levels))
    for copy in copies:
        copy.wait()


def pairs(axis, parity):
    devices = lax.axis_size(axis)
    swaps = []
    for i in range(parity, devices - 1, 2):
        swaps += [(i, i + 1), (i + 1, i)]
    return swaps


def exchange(pay_even, pay_odd, *pay):
    got_even = lax.ppermute(pay_even, "group", pairs("group", 0))
    got_odd = lax.ppermute(pay_odd, "group", pairs("group", 1))
    got = [lax.ppermute(each, "tile", pairs("tile", len(pay) - 1 - i)) for i, each in enumerate(pay)]
    return got_even, got_odd, *got


def shards(tracer, east_speed, north_speed, mixing, depth_levels, sensitivity):
    levels, rows, columns = tracer.shape
    assert levels * slot == lanes and rows % sublanes == 0 and columns % lanes == 0
    f32 = jnp.float32
    field = jax.ShapeDtypeStruct((levels, rows, columns), f32)
    first_size = 5 * levels + sublanes
    second_size = 4 * levels + sublanes
    border_size = 8 * levels
    block = pltpu.VMEM((levels, rows, columns), f32)
    params = pltpu.CompilerParams(vmem_limit_bytes=32 * 1024 * 1024)
    far = pl.BlockSpec(memory_space=pl.ANY)

    def lines(size):
        return jax.ShapeDtypeStruct((size, columns), f32)

    def space(size):
        return pltpu.VMEM((size, columns), f32)

    def tiles(count):
        return jax.ShapeDtypeStruct((rows, count * lanes), f32)

    given = (tracer, east_speed, north_speed, mixing, depth_levels)
    near = tuple(jax.ShapeDtypeStruct(given[i].shape, given[i].dtype) for i in (0, 1, 2, 4))
    links = jax.ShapeDtypeStruct(mixing.shape, f32)
    plane = jax.ShapeDtypeStruct((rows, columns), f32)
    distant = [pltpu.with_memory_space_constraint(array, pltpu.HBM) for array in given + (sensitivity,)]
    outcome = pl.pallas_call(
        factor_kernel,
        in_specs=[far] * 6,
        out_shape=near
        + (links, field, plane, field, lines(first_size), lines(first_size), tiles(6), tiles(4), lines(first_size), lines(first_size), lines(levels)),
        scratch_shapes=[pltpu.VMEM(mixing.shape, f32), block, block, pltpu.SemaphoreType.DMA((6,))],
        compiler_params=params,
    )(*distant)
    tracer, east_speed, north_speed, depth_levels, *factors, weight = outcome[:8]
    pay_even, pay_odd, outer, pay_core, up, down, beside = outcome[8:]
    cells = levels * rows * columns
    inner = pl.CostEstimate(flops=80 * cells, bytes_accessed=24 * cells, transcendentals=0)

    got1 = exchange(pay_even, pay_odd, outer, pay_core)
    parts = pl.pallas_call(inner_kernel, out_shape=(field, field), compiler_params=params, cost_estimate=inner)(
        tracer, weight, east_speed, north_speed, depth_levels
    )
    state, weight_next, pay_even, pay_odd, outer2, up2, down2 = pl.pallas_call(
        first_kernel,
        out_shape=(field, field, lines(second_size), lines(second_size), tiles(2), lines(second_size), lines(second_size)),
        scratch_shapes=[block, block, space(first_size), space(first_size), space(border_size)],
        compiler_params=params,
    )(north_speed, depth_levels, *factors, weight, *parts, up, down, beside, outer, *got1)
    got2 = exchange(pay_even, pay_odd, outer2)

    def strips(count):
        return jax.ShapeDtypeStruct((count, rows, lanes), f32)

    parts = pl.pallas_call(
        second_inner_kernel,
        out_shape=(field, field, tiles(2), strips(levels - 1), strips(levels), tiles(1), strips(levels)),
        compiler_params=params,
        cost_estimate=inner,
    )(state, weight_next, east_speed, north_speed, depth_levels, tracer, outer, got1[2])
    sends = pltpu.SemaphoreType.DMA((4,))
    final, adjoint = pl.pallas_call(
        second_kernel,
        out_specs=[far] * 2,
        out_shape=(field, field),
        scratch_shapes=[block] * 4 + [space(second_size), space(second_size), space(border_size), sends],
        compiler_params=params,
    )(depth_levels, *factors, *parts, up2, down2, outer2, up, down, beside, outer, *got1, *got2)
    return final, adjoint


def solution(mesh):
    block = P(None, "group", "tile")
    in_specs = (block, block, block, block, P("group", "tile"), block)
    return jax.shard_map(shards, mesh=mesh, in_specs=in_specs, out_specs=(block, block), check_vma=False)
```

```python
import jax
import jax.numpy as jnp
from jax import lax
from jax.experimental import pallas as pl
from jax.experimental.pallas import tpu as pltpu
from jax.sharding import PartitionSpec as P

diffusivity = 0.1
uptake = 0.2
lanes = 128
sublanes = 8
group_size = 8

slot = 8


def turned(value, shift, axis):
    return pltpu.roll(value, shift % value.shape[axis], axis)


def index(shape, axis):
    return lax.broadcasted_iota(jnp.int32, shape, axis)


def parities():
    return lax.rem(lax.axis_index("group"), 2) == 0, lax.rem(lax.axis_index("tile"), 2) == 0


def split(value, axis):
    step = lanes if axis == 2 else sublanes
    return [lax.slice_in_dim(value, i, i + step, axis=axis) for i in range(0, value.shape[axis], step)]


def shifted(tiles, shift, axis, edge):
    span = tiles[0].shape[axis]
    moved = [turned(tile, shift, axis) for tile in tiles]
    place = index(tiles[0].shape, axis)
    if shift > 0:
        return [jnp.where(place < shift, a, b) for a, b in zip([edge] + moved[:-1], moved)]
    return [jnp.where(place >= span + shift, a, b) for a, b in zip(moved[1:] + [edge], moved)]


def face_flux(c, behind, ahead, far, speed, is_open):
    flux = speed * (7.0 * (c + behind) - (ahead + far)) - diffusivity * (c - behind)
    return jnp.where(is_open, flux, 0.0)


def explicit_flux(tiles, speeds, opens, axis, edges):
    edge_behind, edge_far, edge_ahead, edge_flux = edges
    behind = shifted(tiles, 1, axis, edge_behind)
    ahead = shifted(tiles, -1, axis, edge_ahead)
    far = shifted(tiles, 2, axis, edge_far)
    flux = [face_flux(*each) for each in zip(tiles, behind, ahead, far, speeds, opens)]
    following = shifted(flux, -1, axis, edge_flux)
    return jnp.concatenate([g - n for g, n in zip(flux, following)], axis=axis)


def reverse_flux(tiles, speeds, opens, axis, edges):
    edge_behind, edge_sum, edge_carried, edge_far = edges
    behind = shifted(tiles, 1, axis, edge_behind)
    jump = [jnp.where(o, h - b, 0.0) for h, b, o in zip(tiles, behind, opens)]
    carried = [s * j for s, j in zip(speeds, jump)]
    seven = [7.0 * g for g in carried]
    spread = [diffusivity * j for j in jump]
    ahead = shifted([a + b for a, b in zip(seven, spread)], -1, axis, edge_sum)
    back = shifted(carried, 1, axis, edge_carried)
    far = shifted(carried, -2, axis, edge_far)
    parts = zip(seven, spread, ahead, back, far)
    return jnp.concatenate([(a - b) + c - d - e for a, b, c, d, e in parts], axis=axis)


def level_of(lane):
    return lax.div(lax.rem(lane + slot // 2, lanes), slot)


def pack_columns(k, item, packed, ahead=0):
    lane = index(packed.shape, 1)
    tile = jnp.where(lane < lanes // 2, item[:, :lanes], item[:, -lanes:])
    return jnp.where(level_of(lane + (lanes - ahead)) == k, turned(tile, slot * k + ahead, 1), packed)


def second_item(tile):
    return turned(tile, -(slot // 2), 1)


def repeated(value):
    lane = index((value.shape[0], lanes), 1)
    value = jnp.where(lane < lanes // 2, value[:, :lanes], value[:, -lanes:])
    value = jnp.where(level_of(lane) == 0, value, 0.0)
    width = slot
    while width < lanes:
        value = value + turned(value, width, 1)
        width *= 2
    return value


def pack_rows(k, levels, c, h, speed, open_y, up, down):
    size = c.shape[0]
    last = slice(size - sublanes, size)
    first = slice(0, sublanes)
    g_last = jnp.where(open_y[last], speed[last] * (h[last] - turned(h[last], 1, 0)), 0.0)
    g_first = jnp.where(open_y[first], speed[first] * (h[first] - turned(h[first], 1, 0)), 0.0)
    above = (c[size - 2 : size - 1], c[size - 1 :], h[size - 1 :], g_last[sublanes - 1 :])
    below = (c[0:1], c[1:2], h[0:1], g_first[1:2])
    for item in range(4):
        at = item * levels + k
        up[at : at + 1, :] = above[item]
        down[at : at + 1, :] = below[item]


def inward(levels, scaled, links, inverse, joint, passed):
    middle = levels // 2
    top = bottom = None
    for i in range(levels - middle):
        k = levels - 1 - i
        bottom = scaled(k) if i == 0 else scaled(k) + (links[k] * inverse[k]) * bottom
        passed[k] = bottom
        if i < middle:
            top = scaled(i) if i == 0 else scaled(i) + (links[i - 1] * inverse[i]) * top
            passed[i] = top
    link = links[middle - 1]
    top = (top + (link * inverse[middle - 1]) * bottom) * joint
    return top, bottom + (link * inverse[middle]) * top


def outward(levels, ends, links, inverse, passed):
    middle = levels // 2
    top, bottom = ends
    yield middle - 1, top
    yield middle, bottom
    for i in range(1, levels - middle):
        k = middle + i
        bottom = passed[k] + (links[k - 1] * inverse[k]) * bottom
        yield k, bottom
        k = middle - 1 - i
        if k >= 0:
            top = passed[k] + (links[k] * inverse[k]) * top
            yield k, top


def factorized(levels, links, inverse):
    middle = levels // 2

    def pivots(order, near, far):
        share = None
        for k in order:
            pivot = 1.0
            if 0 <= far(k) < levels - 1:
                pivot = pivot + links[far(k)]
            if share is not None:
                pivot = pivot + (links[near(k)] - links[near(k)] * share)
            inverse[k] = 1.0 / pivot
            if 0 <= far(k) < levels - 1:
                share = links[far(k)] * inverse[k]
            yield

    down = pivots(range(middle), lambda k: k - 1, lambda k: k)
    up = pivots(range(levels - 1, middle - 1, -1), lambda k: k, lambda k: k - 1)
    for _ in range(levels - middle):
        next(up)
        next(down, None)
    link = links[middle - 1]
    return 1.0 / (1.0 - (link * inverse[middle - 1]) * (link * inverse[middle]))


def choose(flag, ref_true, ref_false, into):
    into[...] = jnp.where(flag, ref_true[...], ref_false[...])


def factor_kernel(
    tracer_far, east_far, north_far, mixing_far, depth_far, sensitivity_far,
    tracer, east, north, depth, links, inverse, joint, weight, pay_even, pay_odd, outer, pay_chip, pay_core, up, down, beside,
    mixing, sensitivity, passed, arrived,
):
    order = (
        (depth_far, depth),
        (mixing_far, mixing),
        (sensitivity_far, sensitivity),
        (tracer_far, tracer),
        (east_far, east),
        (north_far, north),
    )
    copies = [pltpu.make_async_copy(far, near, arrived.at[i]) for i, (far, near) in enumerate(order)]
    for copy in copies:
        copy.start()
    levels, rows, columns = tracer.shape
    even_y, even_x = parities()
    copies[0].wait()
    deep = depth[...]
    depth_float = deep.astype(jnp.float32)
    packed_depth = repeated(depth_float)
    for copy in copies[1:3]:
        copy.wait()
    shallow_y = jnp.minimum(deep, turned(deep, 1, 0))
    for k in range(levels - 1):
        links[k] = jnp.where(k + 1 < deep, mixing[k], 0.0)
    joint[...] = factorized(levels, links, inverse)
    ends = inward(levels, lambda k: sensitivity[k] * inverse[k], links, inverse, joint[...], passed)
    for copy in copies[3:]:
        copy.wait()
    packed = [jnp.zeros((rows, lanes), jnp.float32)] * 5
    for k, current in outward(levels, ends, links, inverse, passed):
        h = jnp.where(k < deep, current, 0.0)
        weight[k] = h
        c = tracer[k]
        speed_x = east[k] * (1.0 / 12.0)
        speed_y = north[k] * (1.0 / 12.0)
        items = (c, h, speed_x, speed_y) + ((mixing[k],) if k < levels - 1 else ())
        ahead = (0, slot // 2, 0, slot // 2, slot // 2)
        packed[: len(items)] = [pack_columns(k, *each) for each in zip(items, packed, ahead)]
        pack_rows(k, levels, c, h, speed_y, k < shallow_y, up, down)
        at = 4 * levels + k
        down[at : at + 1, :] = speed_y[0:1]
        up[at : at + 1, :] = speed_y[rows - 1 :]
        beside[k : k + 1, :] = speed_y[1:2]
    start = lax.rem(index((rows, lanes), 1), slot) < slot // 2
    twice = ((packed[0], packed[1]), (packed[2], packed[3]), (packed_depth, packed[4]))
    first = jnp.concatenate([jnp.where(start, a, b) for a, b in twice], axis=1)
    last = jnp.concatenate([jnp.where(start, b, a) for a, b in twice], axis=1)
    pay_chip[...] = jnp.where(even_x, first, last)
    pay_core[...] = jnp.where(even_x, last, first)
    outer[...] = jnp.concatenate([packed[0], packed[1], packed[2], packed_depth], axis=1)
    at = 5 * levels
    up[at : at + sublanes, :] = jnp.broadcast_to(depth_float[rows - 1 :], (sublanes, columns))
    down[at : at + sublanes, :] = jnp.broadcast_to(depth_float[0:1], (sublanes, columns))
    choose(even_y, up, down, pay_even)
    choose(even_y, down, up, pay_odd)


def rows_of(ref, item, levels):
    return ref[item * levels : (item + 1) * levels, :]


def border_rows(level, lower, upper, up, down, speeds, deeps):
    c_far, c_near, h_near, g_near = lower
    c_next, c_over, h_next, g_over = upper
    c_two, c_one, h_one = up
    c_zero, c_first, h_zero = down
    speed_start, speed_first, speed_last, speed_end = speeds
    before, zero, one, two_last, last, after = deeps
    start_open = level < jnp.minimum(before, zero)
    first_open = level < jnp.minimum(zero, one)
    last_open = level < jnp.minimum(two_last, last)
    end_open = level < jnp.minimum(last, after)
    start = face_flux(c_zero, c_near, c_first, c_far, speed_start, start_open)
    first = jnp.where(first_open, -speed_first * c_near, 0.0)
    final = jnp.where(last_open, -speed_last * c_next, 0.0)
    finish = face_flux(c_next, c_one, c_over, c_two, speed_end, end_open)
    start_jump = jnp.where(start_open, h_zero - h_near, 0.0)
    end_jump = jnp.where(end_open, h_next - h_one, 0.0)
    start_carried = speed_start * start_jump
    end_carried = speed_end * end_jump
    return (
        start - first,
        first,
        -final,
        final - finish,
        7.0 * start_carried - diffusivity * start_jump - g_near,
        -start_carried,
        -end_carried,
        7.0 * end_carried + diffusivity * end_jump - g_over,
    )


def borders_y(levels, lower, upper, up, down, speeds, deep, deeps, border):
    end = deep.shape[0] - 1
    deeps = (deeps[0], deep[0:1], deep[1:2], deep[end - 1 : end], deep[end:], deeps[1])
    several = lambda ref, count: [rows_of(ref, i, levels) for i in range(count)]
    level = index((levels, deep.shape[1]), 0).astype(jnp.float32)
    values = border_rows(level, several(lower, 4), several(upper, 4), several(up, 3), several(down, 3), speeds, deeps)
    for item, value in enumerate(values):
        border[item * levels : (item + 1) * levels, :] = value


def placed(shape):
    lane = index(shape, 1)
    return lax.rem(lane, slot), level_of(lane).astype(jnp.float32)


def borders_x(before, after, own):
    place, level = placed(own[0].shape)
    start = place < slot // 2
    at = lambda value, distance: turned(value, -distance, 1)
    c, h, speed, deep = (jnp.where(start, mine, other) for mine, other in zip(own, before))
    deep_back = at(deep, -1)
    is_open = level < jnp.minimum(deep, deep_back)
    next_open = level < jnp.minimum(deep, at(deep, 1))
    back_open = level < jnp.minimum(deep_back, at(deep, -2))
    behind, far = at(c, -1), at(c, -2)
    flux = face_flux(c, behind, at(c, 1), far, speed, is_open) + jnp.where(next_open, at(speed, 1) * behind, 0.0)
    forward = jnp.where(place == 0, flux, jnp.where(is_open, -speed * far, 0.0))
    h_back = at(h, -1)
    jump = jnp.where(is_open, h - h_back, 0.0)
    back = jnp.where(back_open, at(speed, -1) * (h_back - at(h, -2)), 0.0)
    backward = jnp.where(place == 0, 7.0 * (speed * jump) - diffusivity * jump, 0.0) - back
    c, h, speed, deep = (jnp.where(start, other, mine) for mine, other in zip(own, after))
    deep_next = at(deep, 1)
    is_open = level < jnp.minimum(deep, at(deep, -1))
    next_open = level < jnp.minimum(deep, deep_next)
    over_open = level < jnp.minimum(deep_next, at(deep, 2))
    c_next, c_over, speed_next = at(c, 1), at(c, 2), at(speed, 1)
    flux = face_flux(c_next, c, c_over, at(c, -1), speed_next, next_open) + jnp.where(is_open, speed * c_next, 0.0)
    forward_end = jnp.where(place == slot - 1, -flux, jnp.where(next_open, speed_next * c_over, 0.0))
    h_next = at(h, 1)
    jump = jnp.where(next_open, h_next - h, 0.0)
    over = jnp.where(over_open, at(speed, 2) * (at(h, 2) - h_next), 0.0)
    total = 7.0 * (speed_next * jump) + diffusivity * jump
    backward_end = jnp.where(place == slot - 1, total, 0.0) - over
    return jnp.where(start, forward, forward_end), jnp.where(start, backward, backward_end)


def with_rows(k, levels, value, border, item):
    rows, columns = value.shape
    row = index((sublanes, columns), 0)

    def line(which):
        at = (item + which) * levels + k
        return jnp.broadcast_to(border[at : at + 1, :], (sublanes, columns))

    tiles = split(value, 0)
    tiles[0] = tiles[0] + jnp.where(row == 0, line(0), jnp.where(row == 1, line(1), 0.0))
    added = jnp.where(row == sublanes - 2, line(2), jnp.where(row == sublanes - 1, line(3), 0.0))
    tiles[-1] = tiles[-1] + added
    return jnp.concatenate(tiles, axis=0)


def with_columns(k, value, packed):
    lead = turned(packed, -slot * k, 1)
    lane = index(lead.shape, 1)
    tiles = [value[:, i : i + lanes] for i in range(0, value.shape[1], lanes)]
    tiles[0] = tiles[0] + jnp.where(lane < 2, lead, 0.0)
    tiles[-1] = tiles[-1] + jnp.where(lane >= lanes - 2, lead, 0.0)
    return jnp.concatenate(tiles, axis=1)


def step_levels(first, c, h, east_part, north_part, shallow):
    count, rows, columns = c.shape
    shallow_x, shallow_y = shallow
    level = index((count, rows, columns), 0) + first
    none = (0.0, 0.0, 0.0, 0.0)
    speeds = split(east_part * (1.0 / 12.0), 2)
    opens = split(level < shallow_x[None], 2)
    forward = explicit_flux(split(c, 2), speeds, opens, 2, none)
    backward = reverse_flux(split(h, 2), speeds, opens, 2, none)
    speeds = split(north_part * (1.0 / 12.0), 1)
    opens = split(level < shallow_y[None], 1)
    forward = forward + explicit_flux(split(c, 1), speeds, opens, 1, none)
    backward = backward + reverse_flux(split(h, 1), speeds, opens, 1, none)
    return forward, h + backward


def inner_kernel(c_ref, h_ref, east, north, depth, *rest):
    *tracer, forward, linear = rest
    levels, rows, columns = c_ref.shape
    deep = depth[...]
    lane, row = index(deep.shape, 1), index(deep.shape, 0)
    shallow_x = jnp.where(lane == 0, 0, jnp.minimum(deep, turned(deep, 1, 1)))
    shallow_y = jnp.where(row == 0, 0, jnp.minimum(deep, turned(deep, 1, 0)))
    for k in range(0, levels, group_size):
        part = slice(k, min(k + group_size, levels))
        c, h = c_ref[part], h_ref[part]
        ahead, back = step_levels(k, c, h, east[part], north[part], (shallow_x, shallow_y))
        if tracer:
            back = back - (2.0 * uptake) * tracer[0][part] * h
        linear[part] = back
        forward[part] = c + ahead - uptake * c * c


def item_of(value, item):
    return value[:, item * lanes : (item + 1) * lanes]


def take(flag, core, chip):
    return jnp.where(flag, chip, core), jnp.where(flag, core, chip)


def four_items(message):
    values, speeds, depths = (item_of(message, i) for i in range(3))
    return [values, second_item(values), speeds, depths]


def own_items(outer):
    values, shifted_values, speeds, depths = (item_of(outer, i) for i in range(4))
    return [values, second_item(shifted_values), speeds, depths]


def strip_rows(levels, message, up, down):
    c, h, speeds, deep = four_items(message)
    side = second_item(speeds)
    size = c.shape[0]
    _, level = placed(c.shape)
    is_open = level < jnp.minimum(deep, turned(deep, 1, 0))
    carried = jnp.where(is_open, side * (h - turned(h, 1, 0)), 0.0)
    at = 4 * levels
    for ref in (up, down):
        ref[at : at + sublanes, :] = jnp.zeros((sublanes, ref.shape[1]), jnp.float32)
    end = size - 1
    above = (c[end - 1 : end], c[end:], h[end:], carried[end:], deep[end:])
    below = (c[0:1], c[1:2], h[0:1], carried[1:2], deep[0:1], side[0:1])
    for ref, lines in ((up, above), (down, below)):
        for i, line in enumerate(lines):
            ref[at + i : at + i + 1, :lanes] = line


def second_inner_kernel(
    c_ref, h_ref, east, north, depth, tracer, outer, got_chip,
    forward, linear, base, strip_links, strip_inverse, strip_joint, strip_weight, strip_values, outer_next,
):
    levels = c_ref.shape[0]
    packed = [jnp.zeros((outer.shape[0], lanes), jnp.float32)] * 2
    for k in range(levels):
        packed = [pack_columns(k, *each) for each in zip((c_ref[k], h_ref[k]), packed)]
    outer_next[...] = jnp.concatenate(packed, axis=1)
    inner_kernel(c_ref, h_ref, east, north, depth, tracer, forward, linear)
    _, even = parities()
    place, level = placed((outer.shape[0], lanes))
    ours = (place < slot // 2) == even
    items = four_items(got_chip)
    side, mixed = second_item(items[2]), second_item(items[3])
    strip_values[...] = jnp.concatenate([items[0], items[1], items[3], side], axis=1)
    c, h, speed, deep = (jnp.where(ours, mine, item) for mine, item in zip(own_items(outer), items))
    is_open = level < jnp.minimum(deep, turned(deep, 1, 1))
    flux = face_flux(c, turned(c, 1, 1), turned(c, -1, 1), turned(c, 2, 1), speed, is_open)
    jump = jnp.where(is_open, h - turned(h, 1, 1), 0.0)
    carried = speed * jump
    plus = 7.0 * carried + diffusivity * jump
    minus = 7.0 * carried - diffusivity * jump
    step = c + (flux - turned(flux, -1, 1)) - uptake * c * c
    reverse = h + minus + turned(plus, -1, 1) - turned(carried, 1, 1) - turned(carried, -2, 1)
    previous = jnp.where(index(deep.shape, 0) == 0, 0.0, turned(deep, 1, 0))
    opens = split(level < jnp.minimum(deep, previous), 0)
    none = (0.0, 0.0, 0.0, 0.0)
    base[:, :lanes] = step + explicit_flux(split(c, 0), split(side, 0), opens, 0, none)
    base[:, lanes:] = reverse + reverse_flux(split(h, 0), split(side, 0), opens, 0, none)
    ours = (place == 0) | (place == 1) | (place == slot - 2) | (place == slot - 1)
    mixed = jnp.where(ours & (level + 1.0 < deep), mixed, 0.0)
    for k in range(levels):
        strip_weight[k] = turned(h, -slot * k, 1)
        if k < levels - 1:
            strip_links[k] = turned(mixed, -slot * k, 1)
    strip_joint[...] = factorized(levels, strip_links, strip_inverse)


def strip_states(levels, values, base, factors, weights, lower, upper):
    links, inverse, joint = factors
    c, h, deep, side = (item_of(values, i) for i in range(4))
    place, level = placed(c.shape)
    end = c.shape[0] - 1

    def line(ref, item):
        at = 4 * levels + item
        return jnp.broadcast_to(ref[at : at + 1, :lanes], (sublanes, lanes))

    def row_of(value, at):
        return jnp.broadcast_to(value[at : at + 1], (sublanes, lanes))

    added = border_rows(
        level[:sublanes],
        [line(lower, i) for i in range(4)],
        [line(upper, i) for i in range(4)],
        (row_of(c, end - 1), row_of(c, end), row_of(h, end)),
        (row_of(c, 0), row_of(c, 1), row_of(h, 0)),
        (row_of(side, 0), row_of(side, 1), row_of(side, end), line(upper, 5)),
        (line(lower, 4), row_of(deep, 0), row_of(deep, 1), row_of(deep, end - 1), row_of(deep, end), line(upper, 4)),
    )
    row = index((sublanes, lanes), 0)

    def bordered(value, rows):
        tiles = split(value, 0)
        tiles[0] = tiles[0] + jnp.where(row == 0, rows[0], jnp.where(row == 1, rows[1], 0.0))
        tiles[-1] = tiles[-1] + jnp.where(row == sublanes - 2, rows[2], jnp.where(row == sublanes - 1, rows[3], 0.0))
        return jnp.concatenate(tiles, axis=0)

    right = jnp.where(level < deep, bordered(base[:, :lanes], added[:4]), 0.0)
    linear = bordered(base[:, lanes:], added[4:])
    right, linear = ([turned(value, -slot * k, 1) for k in range(levels)] for value in (right, linear))
    passed = [None] * levels
    ends = inward(levels, lambda k: right[k] * inverse[k], links, inverse, joint, passed)
    state = dict(outward(levels, ends, links, inverse, passed))

    def scaled(k):
        return (linear[k] - (2.0 * uptake) * state[k] * weights[k]) * inverse[k]

    ends = inward(levels, scaled, links, inverse, joint, passed)
    weight = dict(outward(levels, ends, links, inverse, passed))
    packed_state = packed_weight = jnp.zeros(c.shape, jnp.float32)
    for k in range(levels):
        here = level == float(k)
        packed_state = jnp.where(here, turned(state[k], slot * k, 1), packed_state)
        value = jnp.where(k < deep, weight[k], 0.0)
        packed_weight = jnp.where(here, turned(value, slot * k, 1), packed_weight)
    return packed_state, packed_weight


def first_kernel(
    north, depth, links, inverse, joint, weight, forward, linear, own_up, own_down, beside, own,
    got_even, got_odd, got_chip, got_core,
    state, weight_next, pay_even, pay_odd, up, down,
    passed, scaled, lower, upper, border,
):
    levels, rows, columns = weight.shape
    even_y, even_x = parities()
    choose(even_y, got_odd, got_even, lower)
    choose(even_y, got_even, got_odd, upper)
    before, after = take(even_x, got_core[...], got_chip[...])
    deep = depth[...]
    depth_float = deep.astype(jnp.float32)
    at = 5 * levels
    speeds = (rows_of(own_down, 4, levels), beside[...], rows_of(own_up, 4, levels), rows_of(upper, 4, levels))
    deeps = (lower[at : at + 1, :], upper[at : at + 1, :])
    borders_y(levels, lower, upper, own_up, own_down, speeds, depth_float, deeps, border)
    packed = borders_x(four_items(before), four_items(after), own_items(own))
    for k in range(levels):
        scaled[k] = with_rows(k, levels, forward[k], border, 0)
        state[k] = with_rows(k, levels, linear[k], border, 4)
    for k in range(levels):
        scaled[k] = jnp.where(k < deep, with_columns(k, scaled[k], packed[0]), 0.0) * inverse[k]
        state[k] = with_columns(k, state[k], packed[1])
    ends = inward(levels, lambda k: scaled[k], links, inverse, joint[...], passed)
    for k, current in outward(levels, ends, links, inverse, passed):
        scaled[k] = (state[k] - (2.0 * uptake) * current * weight[k]) * inverse[k]
        state[k] = current
    ends = inward(levels, lambda k: scaled[k], links, inverse, joint[...], passed)
    shallow_y = jnp.minimum(deep, turned(deep, 1, 0))
    for k, current in outward(levels, ends, links, inverse, passed):
        h = jnp.where(k < deep, current, 0.0)
        weight_next[k] = h
        c = state[k]
        pack_rows(k, levels, c, h, north[k] * (1.0 / 12.0), k < shallow_y, up, down)
    strip_rows(levels, got_chip[...], up, down)
    choose(even_y, up, down, pay_even)
    choose(even_y, down, up, pay_odd)


def second_kernel(
    depth, links, inverse, joint, forward, linear, base, strip_links, strip_inverse, strip_joint, strip_weight, strip_values,
    own_up, own_down, own, first_up, first_down, beside, first_own,
    got1_even, got1_odd, got1_chip, got1_core, got_even, got_odd, got_core,
    final_far, adjoint_far,
    final, adjoint, passed, scaled, lower, upper, border, sent,
):
    copies = []

    def send(near, far, part):
        copy = pltpu.make_async_copy(near.at[part], far.at[part], sent.at[len(copies)])
        copy.start()
        copies.append(copy)

    levels, rows, columns = forward.shape
    even_y, even_x = parities()
    choose(even_y, got_odd, got_even, lower)
    choose(even_y, got_even, got_odd, upper)
    before1, after1 = take(even_x, got1_core[...], got1_chip[...])
    factors = (strip_links, strip_inverse, strip_joint[...])
    strip = strip_states(levels, strip_values, base, factors, strip_weight, lower, upper)
    before, after = take(even_x, got_core[...], jnp.concatenate(strip, axis=1))
    deep = depth[...]
    depth_float = deep.astype(jnp.float32)
    at = 5 * levels
    deeps = (
        jnp.where(even_y, got1_odd[at : at + 1, :], got1_even[at : at + 1, :]),
        jnp.where(even_y, got1_even[at : at + 1, :], got1_odd[at : at + 1, :]),
    )
    speed = jnp.where(even_y, rows_of(got1_even, 4, levels), rows_of(got1_odd, 4, levels))
    speeds = (rows_of(first_down, 4, levels), beside[...], rows_of(first_up, 4, levels), speed)
    borders_y(levels, lower, upper, own_up, own_down, speeds, depth_float, deeps, border)

    pair = lambda value: [item_of(value, 0), item_of(value, 1)]
    ends = (pair(before) + four_items(before1)[2:], pair(after) + four_items(after1)[2:])
    mine = pair(own) + [item_of(first_own, 2), item_of(first_own, 3)]
    packed = borders_x(*ends, mine)
    for k in range(levels):
        adjoint[k] = with_rows(k, levels, linear[k], border, 4)
        scaled[k] = with_rows(k, levels, forward[k], border, 0)
    for k in range(levels):
        scaled[k] = jnp.where(k < deep, with_columns(k, scaled[k], packed[0]), 0.0) * inverse[k]
    for k in range(levels):
        adjoint[k] = with_columns(k, adjoint[k], packed[1])
    send(adjoint, adjoint_far, slice(0, levels))
    ends = inward(levels, lambda k: scaled[k], links, inverse, joint[...], passed)
    middle = levels // 2
    quarter = middle // 2
    for k, current in outward(levels, ends, links, inverse, passed):
        final[k] = current
        if k == middle - quarter:
            send(final, final_far, slice(middle - quarter, middle + quarter))
    send(final, final_far, slice(0, middle - quarter))
    send(final, final_far, slice(middle + quarter, levels))
    for copy in copies:
        copy.wait()


def pairs(axis, parity):
    devices = lax.axis_size(axis)
    swaps = []
    for i in range(parity, devices - 1, 2):
        swaps += [(i, i + 1), (i + 1, i)]
    return swaps


def exchange(pay_even, pay_odd, *pay):
    got_even = lax.ppermute(pay_even, "group", pairs("group", 0))
    got_odd = lax.ppermute(pay_odd, "group", pairs("group", 1))
    got = [lax.ppermute(each, "tile", pairs("tile", len(pay) - 1 - i)) for i, each in enumerate(pay)]
    return got_even, got_odd, *got


def shards(tracer, east_speed, north_speed, mixing, depth_levels, sensitivity):
    levels, rows, columns = tracer.shape
    assert levels * slot == lanes and rows % sublanes == 0 and columns % lanes == 0
    f32 = jnp.float32
    field = jax.ShapeDtypeStruct((levels, rows, columns), f32)
    first_size = 5 * levels + sublanes
    second_size = 4 * levels + sublanes
    border_size = 8 * levels
    block = pltpu.VMEM((levels, rows, columns), f32)
    params = pltpu.CompilerParams(vmem_limit_bytes=32 * 1024 * 1024)
    far = pl.BlockSpec(memory_space=pl.ANY)

    def lines(size):
        return jax.ShapeDtypeStruct((size, columns), f32)

    def space(size):
        return pltpu.VMEM((size, columns), f32)

    def tiles(count):
        return jax.ShapeDtypeStruct((rows, count * lanes), f32)

    given = (tracer, east_speed, north_speed, mixing, depth_levels)
    near = tuple(jax.ShapeDtypeStruct(given[i].shape, given[i].dtype) for i in (0, 1, 2, 4))
    links = jax.ShapeDtypeStruct(mixing.shape, f32)
    plane = jax.ShapeDtypeStruct((rows, columns), f32)
    distant = [pltpu.with_memory_space_constraint(array, pltpu.HBM) for array in given + (sensitivity,)]
    outcome = pl.pallas_call(
        factor_kernel,
        in_specs=[far] * 6,
        out_shape=near
        + (links, field, plane, field, lines(first_size), lines(first_size), tiles(4), tiles(3), tiles(3), lines(first_size), lines(first_size), lines(levels)),
        scratch_shapes=[pltpu.VMEM(mixing.shape, f32), block, block, pltpu.SemaphoreType.DMA((6,))],
        compiler_params=params,
    )(*distant)
    tracer, east_speed, north_speed, depth_levels, *factors, weight = outcome[:8]
    *messages, up, down, beside = outcome[8:]
    pay_even, pay_odd, outer, pay_chip, pay_core = messages
    cells = levels * rows * columns
    inner = pl.CostEstimate(flops=80 * cells, bytes_accessed=24 * cells, transcendentals=0)

    got1 = exchange(pay_even, pay_odd, pay_chip, pay_core)
    parts = pl.pallas_call(inner_kernel, out_shape=(field, field), compiler_params=params, cost_estimate=inner)(
        tracer, weight, east_speed, north_speed, depth_levels
    )
    state, weight_next, pay_even, pay_odd, up2, down2 = pl.pallas_call(
        first_kernel,
        out_shape=(field, field) + (lines(second_size),) * 4,
        scratch_shapes=[block, block, space(first_size), space(first_size), space(border_size)],
        compiler_params=params,
    )(north_speed, depth_levels, *factors, weight, *parts, up, down, beside, outer, *got1)

    def strips(count):
        return jax.ShapeDtypeStruct((count, rows, lanes), f32)

    *parts, outer2 = pl.pallas_call(
        second_inner_kernel,
        out_shape=(field, field, tiles(2), strips(levels - 1), strips(levels), tiles(1), strips(levels), tiles(4), tiles(2)),
        compiler_params=params,
        cost_estimate=inner,
    )(state, weight_next, east_speed, north_speed, depth_levels, tracer, outer, got1[2])
    got2 = exchange(pay_even, pay_odd, outer2)
    sends = pltpu.SemaphoreType.DMA((4,))
    final, adjoint = pl.pallas_call(
        second_kernel,
        out_specs=[far] * 2,
        out_shape=(field, field),
        scratch_shapes=[block] * 4 + [space(second_size), space(second_size), space(border_size), sends],
        compiler_params=params,
    )(depth_levels, *factors, *parts, up2, down2, outer2, up, down, beside, outer, *got1, *got2)
    return final, adjoint


def solution(mesh):
    block = P(None, "group", "tile")
    in_specs = (block, block, block, block, P("group", "tile"), block)
    return jax.shard_map(shards, mesh=mesh, in_specs=in_specs, out_specs=(block, block), check_vma=False)
```

```python
import jax
import jax.numpy as jnp
from jax import lax
from jax.experimental import pallas as pl
from jax.experimental.pallas import tpu as pltpu
from jax.sharding import PartitionSpec as P

diffusivity = 0.1
uptake = 0.2
lanes = 128
sublanes = 8
group_size = 8

slot = 8


def turned(value, shift, axis):
    return pltpu.roll(value, shift % value.shape[axis], axis)


def index(shape, axis):
    return lax.broadcasted_iota(jnp.int32, shape, axis)


def parities():
    return lax.rem(lax.axis_index("group"), 2) == 0, lax.rem(lax.axis_index("tile"), 2) == 0


def split(value, axis):
    step = lanes if axis == 2 else sublanes
    return [lax.slice_in_dim(value, i, i + step, axis=axis) for i in range(0, value.shape[axis], step)]


def shifted(tiles, shift, axis, edge):
    span = tiles[0].shape[axis]
    moved = [turned(tile, shift, axis) for tile in tiles]
    place = index(tiles[0].shape, axis)
    if shift > 0:
        return [jnp.where(place < shift, a, b) for a, b in zip([edge] + moved[:-1], moved)]
    return [jnp.where(place >= span + shift, a, b) for a, b in zip(moved[1:] + [edge], moved)]


def face_flux(c, behind, ahead, far, speed, is_open):
    flux = speed * (7.0 * (c + behind) - (ahead + far)) - diffusivity * (c - behind)
    return jnp.where(is_open, flux, 0.0)


def explicit_flux(tiles, speeds, opens, axis, edges):
    edge_behind, edge_far, edge_ahead, edge_flux = edges
    behind = shifted(tiles, 1, axis, edge_behind)
    ahead = shifted(tiles, -1, axis, edge_ahead)
    far = shifted(tiles, 2, axis, edge_far)
    flux = [face_flux(*each) for each in zip(tiles, behind, ahead, far, speeds, opens)]
    following = shifted(flux, -1, axis, edge_flux)
    return jnp.concatenate([g - n for g, n in zip(flux, following)], axis=axis)


def reverse_flux(tiles, speeds, opens, axis, edges):
    edge_behind, edge_sum, edge_carried, edge_far = edges
    behind = shifted(tiles, 1, axis, edge_behind)
    jump = [jnp.where(o, h - b, 0.0) for h, b, o in zip(tiles, behind, opens)]
    carried = [s * j for s, j in zip(speeds, jump)]
    seven = [7.0 * g for g in carried]
    spread = [diffusivity * j for j in jump]
    ahead = shifted([a + b for a, b in zip(seven, spread)], -1, axis, edge_sum)
    back = shifted(carried, 1, axis, edge_carried)
    far = shifted(carried, -2, axis, edge_far)
    parts = zip(seven, spread, ahead, back, far)
    return jnp.concatenate([(a - b) + c - d - e for a, b, c, d, e in parts], axis=axis)


def level_of(lane):
    return lax.div(lax.rem(lane + slot // 2, lanes), slot)


def pack_columns(k, item, packed, ahead=0):
    lane = index(packed.shape, 1)
    tile = jnp.where(lane < lanes // 2, item[:, :lanes], item[:, -lanes:])
    return jnp.where(level_of(lane + (lanes - ahead)) == k, turned(tile, slot * k + ahead, 1), packed)


def second_item(tile):
    return turned(tile, -(slot // 2), 1)


def repeated(value):
    lane = index((value.shape[0], lanes), 1)
    value = jnp.where(lane < lanes // 2, value[:, :lanes], value[:, -lanes:])
    value = jnp.where(level_of(lane) == 0, value, 0.0)
    width = slot
    while width < lanes:
        value = value + turned(value, width, 1)
        width *= 2
    return value


def edge_rows(c, h, speed, open_y):
    size = c.shape[0]
    last = slice(size - sublanes, size)
    first = slice(0, sublanes)
    g_last = jnp.where(open_y[last], speed[last] * (h[last] - turned(h[last], 1, 0)), 0.0)
    g_first = jnp.where(open_y[first], speed[first] * (h[first] - turned(h[first], 1, 0)), 0.0)
    end = size - 1
    up = [c[end - 1 : end], c[end:], h[end:], g_last[sublanes - 1 :]]
    return up, [c[0:1], c[1:2], h[0:1], g_first[1:2]]


def store_rows(found, ref):
    levels = len(found)
    for item in range(len(found[0])):
        for k in range(0, levels, sublanes):
            tile = jnp.concatenate([found[i][item] for i in range(k, k + sublanes)], axis=0)
            ref[item * levels + k : item * levels + k + sublanes, :] = tile


def inward(levels, scaled, links, inverse, joint, passed):
    middle = levels // 2
    top = bottom = None
    for i in range(levels - middle):
        k = levels - 1 - i
        bottom = scaled(k) if i == 0 else scaled(k) + (links[k] * inverse[k]) * bottom
        passed[k] = bottom
        if i < middle:
            top = scaled(i) if i == 0 else scaled(i) + (links[i - 1] * inverse[i]) * top
            passed[i] = top
    link = links[middle - 1]
    top = (top + (link * inverse[middle - 1]) * bottom) * joint
    return top, bottom + (link * inverse[middle]) * top


def outward(levels, ends, links, inverse, passed):
    middle = levels // 2
    top, bottom = ends
    yield middle - 1, top
    yield middle, bottom
    for i in range(1, levels - middle):
        k = middle + i
        bottom = passed[k] + (links[k - 1] * inverse[k]) * bottom
        yield k, bottom
        k = middle - 1 - i
        if k >= 0:
            top = passed[k] + (links[k] * inverse[k]) * top
            yield k, top


def factorized(levels, links, inverse):
    middle = levels // 2

    def pivots(order, near, far):
        share = None
        for k in order:
            pivot = 1.0
            if 0 <= far(k) < levels - 1:
                pivot = pivot + links[far(k)]
            if share is not None:
                pivot = pivot + (links[near(k)] - links[near(k)] * share)
            inverse[k] = 1.0 / pivot
            if 0 <= far(k) < levels - 1:
                share = links[far(k)] * inverse[k]
            yield

    down = pivots(range(middle), lambda k: k - 1, lambda k: k)
    up = pivots(range(levels - 1, middle - 1, -1), lambda k: k, lambda k: k - 1)
    for _ in range(levels - middle):
        next(up)
        next(down, None)
    link = links[middle - 1]
    return 1.0 / (1.0 - (link * inverse[middle - 1]) * (link * inverse[middle]))


class Either:
    def __init__(self, flag, first, second):
        self.flag, self.first, self.second = flag, first, second

    def __getitem__(self, where):
        return jnp.where(self.flag, self.first[where], self.second[where])


def choose(flag, ref_true, ref_false, into):
    into[...] = jnp.where(flag, ref_true[...], ref_false[...])


def factor_kernel(
    tracer_far, east_far, north_far, mixing_far, depth_far, sensitivity_far,
    tracer, east, north, depth, links, inverse, joint, weight, pay_even, pay_odd, outer, pay_chip, pay_core, up, down, beside,
    mixing, sensitivity, passed, arrived,
):
    order = (
        (depth_far, depth),
        (mixing_far, mixing),
        (sensitivity_far, sensitivity),
        (tracer_far, tracer),
        (east_far, east),
        (north_far, north),
    )
    copies = [pltpu.make_async_copy(far, near, arrived.at[i]) for i, (far, near) in enumerate(order)]
    for copy in copies:
        copy.start()
    levels, rows, columns = tracer.shape
    even_y, even_x = parities()
    copies[0].wait()
    deep = depth[...]
    depth_float = deep.astype(jnp.float32)
    packed_depth = repeated(depth_float)
    for copy in copies[1:3]:
        copy.wait()
    shallow_y = jnp.minimum(deep, turned(deep, 1, 0))
    for k in range(levels - 1):
        links[k] = jnp.where(k + 1 < deep, mixing[k], 0.0)
    joint[...] = factorized(levels, links, inverse)
    ends = inward(levels, lambda k: sensitivity[k] * inverse[k], links, inverse, joint[...], passed)
    for copy in copies[3:]:
        copy.wait()
    packed = [jnp.zeros((rows, lanes), jnp.float32)] * 5
    rows_up, rows_down, rows_beside = {}, {}, {}
    for k, current in outward(levels, ends, links, inverse, passed):
        h = jnp.where(k < deep, current, 0.0)
        weight[k] = h
        c = tracer[k]
        speed_x = east[k] * (1.0 / 12.0)
        speed_y = north[k] * (1.0 / 12.0)
        items = (c, h, speed_x, speed_y) + ((mixing[k],) if k < levels - 1 else ())
        ahead = (0, slot // 2, 0, slot // 2, slot // 2)
        packed[: len(items)] = [pack_columns(k, *each) for each in zip(items, packed, ahead)]
        rows_up[k], rows_down[k] = edge_rows(c, h, speed_y, k < shallow_y)
        rows_up[k].append(speed_y[rows - 1 :])
        rows_down[k].append(speed_y[0:1])
        rows_beside[k] = [speed_y[1:2]]
    for found, ref in ((rows_up, up), (rows_down, down), (rows_beside, beside)):
        store_rows(found, ref)
    start = lax.rem(index((rows, lanes), 1), slot) < slot // 2
    twice = ((packed[0], packed[1]), (packed[2], packed[3]), (packed_depth, packed[4]))
    first = jnp.concatenate([jnp.where(start, a, b) for a, b in twice], axis=1)
    last = jnp.concatenate([jnp.where(start, b, a) for a, b in twice], axis=1)
    pay_chip[...] = jnp.where(even_x, first, last)
    pay_core[...] = jnp.where(even_x, last, first)
    outer[...] = jnp.concatenate([packed[0], packed[1], packed[2], packed_depth], axis=1)
    at = 5 * levels
    up[at : at + sublanes, :] = jnp.broadcast_to(depth_float[rows - 1 :], (sublanes, columns))
    down[at : at + sublanes, :] = jnp.broadcast_to(depth_float[0:1], (sublanes, columns))
    choose(even_y, up, down, pay_even)
    choose(even_y, down, up, pay_odd)


def rows_of(ref, item, levels):
    return ref[item * levels : (item + 1) * levels, :]


def border_rows(level, lower, upper, up, down, speeds, deeps):
    c_far, c_near, h_near, g_near = lower
    c_next, c_over, h_next, g_over = upper
    c_two, c_one, h_one = up
    c_zero, c_first, h_zero = down
    speed_start, speed_first, speed_last, speed_end = speeds
    before, zero, one, two_last, last, after = deeps
    start_open = level < jnp.minimum(before, zero)
    first_open = level < jnp.minimum(zero, one)
    last_open = level < jnp.minimum(two_last, last)
    end_open = level < jnp.minimum(last, after)
    start = face_flux(c_zero, c_near, c_first, c_far, speed_start, start_open)
    first = jnp.where(first_open, -speed_first * c_near, 0.0)
    final = jnp.where(last_open, -speed_last * c_next, 0.0)
    finish = face_flux(c_next, c_one, c_over, c_two, speed_end, end_open)
    start_jump = jnp.where(start_open, h_zero - h_near, 0.0)
    end_jump = jnp.where(end_open, h_next - h_one, 0.0)
    start_carried = speed_start * start_jump
    end_carried = speed_end * end_jump
    return (
        start - first,
        first,
        -final,
        final - finish,
        7.0 * start_carried - diffusivity * start_jump - g_near,
        -start_carried,
        -end_carried,
        7.0 * end_carried + diffusivity * end_jump - g_over,
    )


def borders_y(levels, lower, upper, up, down, speeds, deep, deeps, border):
    end = deep.shape[0] - 1
    deeps = (deeps[0], deep[0:1], deep[1:2], deep[end - 1 : end], deep[end:], deeps[1])
    several = lambda ref, count: [rows_of(ref, i, levels) for i in range(count)]
    level = index((levels, deep.shape[1]), 0).astype(jnp.float32)
    values = border_rows(level, several(lower, 4), several(upper, 4), several(up, 3), several(down, 3), speeds, deeps)
    for item, value in enumerate(values):
        border[item * levels : (item + 1) * levels, :] = value


def placed(shape):
    lane = index(shape, 1)
    return lax.rem(lane, slot), level_of(lane).astype(jnp.float32)


def borders_x(before, after, own):
    place, level = placed(own[0].shape)
    start = place < slot // 2
    at = lambda value, distance: turned(value, -distance, 1)
    c, h, speed, deep = (jnp.where(start, mine, other) for mine, other in zip(own, before))
    deep_back = at(deep, -1)
    is_open = level < jnp.minimum(deep, deep_back)
    next_open = level < jnp.minimum(deep, at(deep, 1))
    back_open = level < jnp.minimum(deep_back, at(deep, -2))
    behind, far = at(c, -1), at(c, -2)
    flux = face_flux(c, behind, at(c, 1), far, speed, is_open) + jnp.where(next_open, at(speed, 1) * behind, 0.0)
    forward = jnp.where(place == 0, flux, jnp.where(is_open, -speed * far, 0.0))
    h_back = at(h, -1)
    jump = jnp.where(is_open, h - h_back, 0.0)
    back = jnp.where(back_open, at(speed, -1) * (h_back - at(h, -2)), 0.0)
    backward = jnp.where(place == 0, 7.0 * (speed * jump) - diffusivity * jump, 0.0) - back
    c, h, speed, deep = (jnp.where(start, other, mine) for mine, other in zip(own, after))
    deep_next = at(deep, 1)
    is_open = level < jnp.minimum(deep, at(deep, -1))
    next_open = level < jnp.minimum(deep, deep_next)
    over_open = level < jnp.minimum(deep_next, at(deep, 2))
    c_next, c_over, speed_next = at(c, 1), at(c, 2), at(speed, 1)
    flux = face_flux(c_next, c, c_over, at(c, -1), speed_next, next_open) + jnp.where(is_open, speed * c_next, 0.0)
    forward_end = jnp.where(place == slot - 1, -flux, jnp.where(next_open, speed_next * c_over, 0.0))
    h_next = at(h, 1)
    jump = jnp.where(next_open, h_next - h, 0.0)
    over = jnp.where(over_open, at(speed, 2) * (at(h, 2) - h_next), 0.0)
    total = 7.0 * (speed_next * jump) + diffusivity * jump
    backward_end = jnp.where(place == slot - 1, total, 0.0) - over
    return jnp.where(start, forward, forward_end), jnp.where(start, backward, backward_end)


def with_rows(k, levels, value, border, item):
    rows, columns = value.shape
    row = index((sublanes, columns), 0)

    def line(which):
        at = (item + which) * levels + k
        return jnp.broadcast_to(border[at : at + 1, :], (sublanes, columns))

    tiles = split(value, 0)
    tiles[0] = tiles[0] + jnp.where(row == 0, line(0), jnp.where(row == 1, line(1), 0.0))
    added = jnp.where(row == sublanes - 2, line(2), jnp.where(row == sublanes - 1, line(3), 0.0))
    tiles[-1] = tiles[-1] + added
    return jnp.concatenate(tiles, axis=0)


def with_columns(k, value, packed):
    lead = turned(packed, -slot * k, 1)
    lane = index(lead.shape, 1)
    tiles = [value[:, i : i + lanes] for i in range(0, value.shape[1], lanes)]
    tiles[0] = tiles[0] + jnp.where(lane < 2, lead, 0.0)
    tiles[-1] = tiles[-1] + jnp.where(lane >= lanes - 2, lead, 0.0)
    return jnp.concatenate(tiles, axis=1)


def step_levels(first, c, h, east_part, north_part, shallow):
    count, rows, columns = c.shape
    shallow_x, shallow_y = shallow
    level = index((count, rows, columns), 0) + first
    none = (0.0, 0.0, 0.0, 0.0)
    speeds = split(east_part * (1.0 / 12.0), 2)
    opens = split(level < shallow_x[None], 2)
    forward = explicit_flux(split(c, 2), speeds, opens, 2, none)
    backward = reverse_flux(split(h, 2), speeds, opens, 2, none)
    speeds = split(north_part * (1.0 / 12.0), 1)
    opens = split(level < shallow_y[None], 1)
    forward = forward + explicit_flux(split(c, 1), speeds, opens, 1, none)
    backward = backward + reverse_flux(split(h, 1), speeds, opens, 1, none)
    return forward, h + backward


def inner_kernel(c_ref, h_ref, east, north, depth, *rest):
    *tracer, forward, linear = rest
    levels, rows, columns = c_ref.shape
    deep = depth[...]
    lane, row = index(deep.shape, 1), index(deep.shape, 0)
    shallow_x = jnp.where(lane == 0, 0, jnp.minimum(deep, turned(deep, 1, 1)))
    shallow_y = jnp.where(row == 0, 0, jnp.minimum(deep, turned(deep, 1, 0)))
    for k in range(0, levels, group_size):
        part = slice(k, min(k + group_size, levels))
        c, h = c_ref[part], h_ref[part]
        ahead, back = step_levels(k, c, h, east[part], north[part], (shallow_x, shallow_y))
        if tracer:
            back = back - (2.0 * uptake) * tracer[0][part] * h
        linear[part] = back
        forward[part] = c + ahead - uptake * c * c


def item_of(value, item):
    return value[:, item * lanes : (item + 1) * lanes]


def take(flag, core, chip):
    return jnp.where(flag, chip, core), jnp.where(flag, core, chip)


def four_items(message):
    values, speeds, depths = (item_of(message, i) for i in range(3))
    return [values, second_item(values), speeds, depths]


def own_items(outer):
    values, shifted_values, speeds, depths = (item_of(outer, i) for i in range(4))
    return [values, second_item(shifted_values), speeds, depths]


def strip_rows(levels, message, up, down):
    c, h, speeds, deep = four_items(message)
    side = second_item(speeds)
    size = c.shape[0]
    _, level = placed(c.shape)
    is_open = level < jnp.minimum(deep, turned(deep, 1, 0))
    carried = jnp.where(is_open, side * (h - turned(h, 1, 0)), 0.0)
    at = 4 * levels
    for ref in (up, down):
        ref[at : at + sublanes, :] = jnp.zeros((sublanes, ref.shape[1]), jnp.float32)
    end = size - 1
    above = (c[end - 1 : end], c[end:], h[end:], carried[end:], deep[end:])
    below = (c[0:1], c[1:2], h[0:1], carried[1:2], deep[0:1], side[0:1])
    for ref, lines in ((up, above), (down, below)):
        for i, line in enumerate(lines):
            ref[at + i : at + i + 1, :lanes] = line


def second_inner_kernel(
    c_ref, h_ref, east, north, depth, tracer, outer, got_chip,
    forward, linear, base, strip_links, strip_inverse, strip_joint, strip_weight, strip_values, outer_next,
):
    levels = c_ref.shape[0]
    packed = [jnp.zeros((outer.shape[0], lanes), jnp.float32)] * 2
    for k in range(levels):
        packed = [pack_columns(k, *each) for each in zip((c_ref[k], h_ref[k]), packed)]
    outer_next[...] = jnp.concatenate(packed, axis=1)
    inner_kernel(c_ref, h_ref, east, north, depth, tracer, forward, linear)
    _, even = parities()
    place, level = placed((outer.shape[0], lanes))
    ours = (place < slot // 2) == even
    items = four_items(got_chip)
    side, mixed = second_item(items[2]), second_item(items[3])
    strip_values[...] = jnp.concatenate([items[0], items[1], items[3], side], axis=1)
    c, h, speed, deep = (jnp.where(ours, mine, item) for mine, item in zip(own_items(outer), items))
    is_open = level < jnp.minimum(deep, turned(deep, 1, 1))
    flux = face_flux(c, turned(c, 1, 1), turned(c, -1, 1), turned(c, 2, 1), speed, is_open)
    jump = jnp.where(is_open, h - turned(h, 1, 1), 0.0)
    carried = speed * jump
    plus = 7.0 * carried + diffusivity * jump
    minus = 7.0 * carried - diffusivity * jump
    step = c + (flux - turned(flux, -1, 1)) - uptake * c * c
    reverse = h + minus + turned(plus, -1, 1) - turned(carried, 1, 1) - turned(carried, -2, 1)
    previous = jnp.where(index(deep.shape, 0) == 0, 0.0, turned(deep, 1, 0))
    opens = split(level < jnp.minimum(deep, previous), 0)
    none = (0.0, 0.0, 0.0, 0.0)
    base[:, :lanes] = step + explicit_flux(split(c, 0), split(side, 0), opens, 0, none)
    base[:, lanes:] = reverse + reverse_flux(split(h, 0), split(side, 0), opens, 0, none)
    ours = (place == 0) | (place == 1) | (place == slot - 2) | (place == slot - 1)
    mixed = jnp.where(ours & (level + 1.0 < deep), mixed, 0.0)
    for k in range(levels):
        strip_weight[k] = turned(h, -slot * k, 1)
        if k < levels - 1:
            strip_links[k] = turned(mixed, -slot * k, 1)
    strip_joint[...] = factorized(levels, strip_links, strip_inverse)


def strip_states(levels, values, base, factors, weights, lower, upper):
    links, inverse, joint = factors
    c, h, deep, side = (item_of(values, i) for i in range(4))
    place, level = placed(c.shape)
    end = c.shape[0] - 1

    def line(ref, item):
        at = 4 * levels + item
        return jnp.broadcast_to(ref[at : at + 1, :lanes], (sublanes, lanes))

    def row_of(value, at):
        return jnp.broadcast_to(value[at : at + 1], (sublanes, lanes))

    added = border_rows(
        level[:sublanes],
        [line(lower, i) for i in range(4)],
        [line(upper, i) for i in range(4)],
        (row_of(c, end - 1), row_of(c, end), row_of(h, end)),
        (row_of(c, 0), row_of(c, 1), row_of(h, 0)),
        (row_of(side, 0), row_of(side, 1), row_of(side, end), line(upper, 5)),
        (line(lower, 4), row_of(deep, 0), row_of(deep, 1), row_of(deep, end - 1), row_of(deep, end), line(upper, 4)),
    )
    row = index((sublanes, lanes), 0)

    def bordered(value, rows):
        tiles = split(value, 0)
        tiles[0] = tiles[0] + jnp.where(row == 0, rows[0], jnp.where(row == 1, rows[1], 0.0))
        tiles[-1] = tiles[-1] + jnp.where(row == sublanes - 2, rows[2], jnp.where(row == sublanes - 1, rows[3], 0.0))
        return jnp.concatenate(tiles, axis=0)

    right = jnp.where(level < deep, bordered(base[:, :lanes], added[:4]), 0.0)
    linear = bordered(base[:, lanes:], added[4:])
    right, linear = ([turned(value, -slot * k, 1) for k in range(levels)] for value in (right, linear))
    passed = [None] * levels
    ends = inward(levels, lambda k: right[k] * inverse[k], links, inverse, joint, passed)
    state = dict(outward(levels, ends, links, inverse, passed))

    def scaled(k):
        return (linear[k] - (2.0 * uptake) * state[k] * weights[k]) * inverse[k]

    ends = inward(levels, scaled, links, inverse, joint, passed)
    weight = dict(outward(levels, ends, links, inverse, passed))
    packed_state = packed_weight = jnp.zeros(c.shape, jnp.float32)
    for k in range(levels):
        here = level == float(k)
        packed_state = jnp.where(here, turned(state[k], slot * k, 1), packed_state)
        value = jnp.where(k < deep, weight[k], 0.0)
        packed_weight = jnp.where(here, turned(value, slot * k, 1), packed_weight)
    return packed_state, packed_weight


def outer_rows(value):
    axis = value.ndim - 2
    size = value.shape[axis]
    first = lax.slice_in_dim(value, 0, sublanes, axis=axis)
    last = lax.slice_in_dim(value, size - sublanes, size, axis=axis)
    return jnp.where(index(first.shape, axis) < sublanes // 2, first, last)


def first_inner_kernel(
    c_ref, h_ref, east, north, depth, links, inverse, joint,
    forward, linear, north_rows, depth_rows, links_rows, inverse_rows, joint_rows, h_rows, forward_rows, linear_rows,
):
    inner_kernel(c_ref, h_ref, east, north, depth, forward, linear)
    depth_rows[...] = outer_rows(depth[...])
    joint_rows[...] = outer_rows(joint[...])
    pairs_of = ((north, north_rows), (links, links_rows), (inverse, inverse_rows), (h_ref, h_rows))
    for whole, rows in pairs_of + ((forward, forward_rows), (linear, linear_rows)):
        for k in range(whole.shape[0]):
            rows[k] = outer_rows(whole[k])


def first_step(
    depth, links, inverse, joint, weight, forward, linear, own_up, own_down, beside, sides, got, state, passed, scaled, border
):
    levels = weight.shape[0]
    even_y, _ = parities()
    got_even, got_odd = got
    lower, upper = Either(even_y, got_odd, got_even), Either(even_y, got_even, got_odd)
    deep = depth[...]
    depth_float = deep.astype(jnp.float32)
    at = 5 * levels
    speeds = (rows_of(own_down, 4, levels), beside[...], rows_of(own_up, 4, levels), rows_of(upper, 4, levels))
    deeps = (lower[at : at + 1, :], upper[at : at + 1, :])
    borders_y(levels, lower, upper, own_up, own_down, speeds, depth_float, deeps, border)
    packed = borders_x(*sides)
    for k in range(levels):
        scaled[k] = with_rows(k, levels, forward[k], border, 0)
        state[k] = with_rows(k, levels, linear[k], border, 4)
    for k in range(levels):
        scaled[k] = jnp.where(k < deep, with_columns(k, scaled[k], packed[0]), 0.0) * inverse[k]
        state[k] = with_columns(k, state[k], packed[1])
    ends = inward(levels, lambda k: scaled[k], links, inverse, joint[...], passed)
    for k, current in outward(levels, ends, links, inverse, passed):
        scaled[k] = (state[k] - (2.0 * uptake) * current * weight[k]) * inverse[k]
        state[k] = current
    return inward(levels, lambda k: scaled[k], links, inverse, joint[...], passed)


def sides_of(got_chip, got_core, own):
    _, even = parities()
    before, after = take(even, got_core[...], got_chip[...])
    return four_items(before), four_items(after), own_items(own)


def edge_kernel(
    north, depth, links, inverse, joint, weight, forward, linear, own_up, own_down, beside, own,
    got_even, got_odd, got_chip, got_core,
    pay_even, pay_odd, up, down,
    state, passed, scaled, border,
):
    levels = weight.shape[0]
    even_y, _ = parities()
    sides = [[outer_rows(item) for item in side] for side in sides_of(got_chip, got_core, own)]
    deep = depth[...]
    ends = first_step(
        depth, links, inverse, joint, weight, forward, linear, own_up, own_down, beside,
        sides, (got_even, got_odd), state, passed, scaled, border,
    )
    shallow_y = jnp.minimum(deep, turned(deep, 1, 0))
    rows_up, rows_down = {}, {}
    for k, current in outward(levels, ends, links, inverse, passed):
        h = jnp.where(k < deep, current, 0.0)
        rows_up[k], rows_down[k] = edge_rows(state[k], h, north[k] * (1.0 / 12.0), k < shallow_y)
    store_rows(rows_up, up)
    store_rows(rows_down, down)
    strip_rows(levels, got_chip[...], up, down)
    choose(even_y, up, down, pay_even)
    choose(even_y, down, up, pay_odd)


def first_kernel(
    depth, links, inverse, joint, weight, forward, linear, own_up, own_down, beside, own,
    got_even, got_odd, got_chip, got_core,
    state, weight_next,
    passed, scaled, border,
):
    levels = weight.shape[0]
    ends = first_step(
        depth, links, inverse, joint, weight, forward, linear, own_up, own_down, beside,
        sides_of(got_chip, got_core, own), (got_even, got_odd), state, passed, scaled, border,
    )
    deep = depth[...]
    for k, current in outward(levels, ends, links, inverse, passed):
        weight_next[k] = jnp.where(k < deep, current, 0.0)


def second_kernel(
    depth, links, inverse, joint, forward, linear, base, strip_links, strip_inverse, strip_joint, strip_weight, strip_values,
    own_up, own_down, own, first_up, first_down, beside, first_own,
    got1_even, got1_odd, got1_chip, got1_core, got_even, got_odd, got_core,
    final_far, adjoint_far,
    final, adjoint, passed, scaled, border, sent,
):
    copies = []

    def send(near, far, part):
        copy = pltpu.make_async_copy(near.at[part], far.at[part], sent.at[len(copies)])
        copy.start()
        copies.append(copy)

    levels, rows, columns = forward.shape
    even_y, even_x = parities()
    lower, upper = Either(even_y, got_odd, got_even), Either(even_y, got_even, got_odd)
    before1, after1 = take(even_x, got1_core[...], got1_chip[...])
    factors = (strip_links, strip_inverse, strip_joint[...])
    strip = strip_states(levels, strip_values, base, factors, strip_weight, lower, upper)
    before, after = take(even_x, got_core[...], jnp.concatenate(strip, axis=1))
    deep = depth[...]
    depth_float = deep.astype(jnp.float32)
    at = 5 * levels
    lower1, upper1 = Either(even_y, got1_odd, got1_even), Either(even_y, got1_even, got1_odd)
    deeps = (lower1[at : at + 1, :], upper1[at : at + 1, :])
    speed = rows_of(upper1, 4, levels)
    speeds = (rows_of(first_down, 4, levels), beside[...], rows_of(first_up, 4, levels), speed)
    borders_y(levels, lower, upper, own_up, own_down, speeds, depth_float, deeps, border)

    pair = lambda value: [item_of(value, 0), item_of(value, 1)]
    ends = (pair(before) + four_items(before1)[2:], pair(after) + four_items(after1)[2:])
    mine = pair(own) + [item_of(first_own, 2), item_of(first_own, 3)]
    packed = borders_x(*ends, mine)
    for k in range(levels):
        adjoint[k] = with_rows(k, levels, linear[k], border, 4)
        scaled[k] = with_rows(k, levels, forward[k], border, 0)
    for k in range(levels):
        scaled[k] = jnp.where(k < deep, with_columns(k, scaled[k], packed[0]), 0.0) * inverse[k]
    for k in range(levels):
        adjoint[k] = with_columns(k, adjoint[k], packed[1])
    send(adjoint, adjoint_far, slice(0, levels))
    ends = inward(levels, lambda k: scaled[k], links, inverse, joint[...], passed)
    middle = levels // 2
    quarter = middle // 2
    for k, current in outward(levels, ends, links, inverse, passed):
        final[k] = current
        if k == middle - quarter:
            send(final, final_far, slice(middle - quarter, middle + quarter))
    send(final, final_far, slice(0, middle - quarter))
    send(final, final_far, slice(middle + quarter, levels))
    for copy in copies:
        copy.wait()


def pairs(axis, parity):
    devices = lax.axis_size(axis)
    swaps = []
    for i in range(parity, devices - 1, 2):
        swaps += [(i, i + 1), (i + 1, i)]
    return swaps


def exchange(pay_even, pay_odd, *pay):
    got_even = lax.ppermute(pay_even, "group", pairs("group", 0))
    got_odd = lax.ppermute(pay_odd, "group", pairs("group", 1))
    got = [lax.ppermute(each, "tile", pairs("tile", len(pay) - 1 - i)) for i, each in enumerate(pay)]
    return got_even, got_odd, *got


def shards(tracer, east_speed, north_speed, mixing, depth_levels, sensitivity):
    levels, rows, columns = tracer.shape
    assert levels * slot == lanes and rows % sublanes == 0 and columns % lanes == 0
    f32 = jnp.float32
    field = jax.ShapeDtypeStruct((levels, rows, columns), f32)
    first_size = 5 * levels + sublanes
    second_size = 4 * levels + sublanes
    border_size = 8 * levels
    block = pltpu.VMEM((levels, rows, columns), f32)
    params = pltpu.CompilerParams(vmem_limit_bytes=32 * 1024 * 1024)
    far = pl.BlockSpec(memory_space=pl.ANY)

    def lines(size):
        return jax.ShapeDtypeStruct((size, columns), f32)

    def space(size):
        return pltpu.VMEM((size, columns), f32)

    def tiles(count):
        return jax.ShapeDtypeStruct((rows, count * lanes), f32)

    given = (tracer, east_speed, north_speed, mixing, depth_levels)
    near = tuple(jax.ShapeDtypeStruct(given[i].shape, given[i].dtype) for i in (0, 1, 2, 4))
    links = jax.ShapeDtypeStruct(mixing.shape, f32)
    plane = jax.ShapeDtypeStruct((rows, columns), f32)
    distant = [pltpu.with_memory_space_constraint(array, pltpu.HBM) for array in given + (sensitivity,)]
    outcome = pl.pallas_call(
        factor_kernel,
        in_specs=[far] * 6,
        out_shape=near
        + (links, field, plane, field, lines(first_size), lines(first_size), tiles(4), tiles(3), tiles(3), lines(first_size), lines(first_size), lines(levels)),
        scratch_shapes=[pltpu.VMEM(mixing.shape, f32), block, block, pltpu.SemaphoreType.DMA((6,))],
        compiler_params=params,
    )(*distant)
    tracer, east_speed, north_speed, depth_levels, *factors, weight = outcome[:8]
    *messages, up, down, beside = outcome[8:]
    pay_even, pay_odd, outer, pay_chip, pay_core = messages
    cells = levels * rows * columns
    inner = pl.CostEstimate(flops=80 * cells, bytes_accessed=24 * cells, transcendentals=0)

    got1 = exchange(pay_even, pay_odd, pay_chip, pay_core)
    tile = lambda *shape, kind=f32: jax.ShapeDtypeStruct(shape[:-1] + (sublanes, shape[-1]), kind)
    rows_shape = tile(levels, columns)
    outer_shapes = (rows_shape, tile(columns, kind=depth_levels.dtype), tile(levels - 1, columns), rows_shape, tile(columns))
    forward, linear, *outers = pl.pallas_call(
        first_inner_kernel,
        out_shape=(field, field) + outer_shapes + (rows_shape,) * 3,
        compiler_params=params,
        cost_estimate=inner,
    )(tracer, weight, east_speed, north_speed, depth_levels, *factors)
    small = pltpu.VMEM(rows_shape.shape, f32)
    pay_even, pay_odd, up2, down2 = pl.pallas_call(
        edge_kernel,
        out_shape=(lines(second_size),) * 4,
        scratch_shapes=[small, small, small, space(border_size)],
        compiler_params=params,
    )(*outers, up, down, beside, outer, *got1)
    state, weight_next = pl.pallas_call(
        first_kernel,
        out_shape=(field, field),
        scratch_shapes=[block, block, space(border_size)],
        compiler_params=params,
        cost_estimate=inner,
    )(depth_levels, *factors, weight, forward, linear, up, down, beside, outer, *got1)

    def strips(count):
        return jax.ShapeDtypeStruct((count, rows, lanes), f32)

    *parts, outer2 = pl.pallas_call(
        second_inner_kernel,
        out_shape=(field, field, tiles(2), strips(levels - 1), strips(levels), tiles(1), strips(levels), tiles(4), tiles(2)),
        compiler_params=params,
        cost_estimate=inner,
    )(state, weight_next, east_speed, north_speed, depth_levels, tracer, outer, got1[2])
    got2 = exchange(pay_even, pay_odd, outer2)
    sends = pltpu.SemaphoreType.DMA((4,))
    final, adjoint = pl.pallas_call(
        second_kernel,
        out_specs=[far] * 2,
        out_shape=(field, field),
        scratch_shapes=[block] * 4 + [space(border_size), sends],
        compiler_params=params,
    )(depth_levels, *factors, *parts, up2, down2, outer2, up, down, beside, outer, *got1, *got2)
    return final, adjoint


def solution(mesh):
    block = P(None, "group", "tile")
    in_specs = (block, block, block, block, P("group", "tile"), block)
    return jax.shard_map(shards, mesh=mesh, in_specs=in_specs, out_specs=(block, block), check_vma=False)
```

```python
import functools

import jax
import jax.numpy as jnp
from jax import lax
from jax.experimental import pallas as pl
from jax.experimental.pallas import tpu as pltpu
from jax.sharding import PartitionSpec as P

diffusivity = 0.1
uptake = 0.2
lanes = 128
sublanes = 8
group_size = 8

slot = 8


def turned(value, shift, axis):
    return pltpu.roll(value, shift % value.shape[axis], axis)


def index(shape, axis):
    return lax.broadcasted_iota(jnp.int32, shape, axis)


def parities():
    return lax.rem(lax.axis_index("group"), 2) == 0, lax.rem(lax.axis_index("tile"), 2) == 0


def split(value, axis):
    step = lanes if axis == 2 else sublanes
    return [lax.slice_in_dim(value, i, i + step, axis=axis) for i in range(0, value.shape[axis], step)]


def shifted(tiles, shift, axis, edge):
    span = tiles[0].shape[axis]
    moved = [turned(tile, shift, axis) for tile in tiles]
    place = index(tiles[0].shape, axis)
    if shift > 0:
        return [jnp.where(place < shift, a, b) for a, b in zip([edge] + moved[:-1], moved)]
    return [jnp.where(place >= span + shift, a, b) for a, b in zip(moved[1:] + [edge], moved)]


def face_flux(c, behind, ahead, far, speed, is_open):
    flux = speed * (7.0 * (c + behind) - (ahead + far)) - diffusivity * (c - behind)
    return jnp.where(is_open, flux, 0.0)


def explicit_flux(tiles, speeds, opens, axis, edges):
    edge_behind, edge_far, edge_ahead, edge_flux = edges
    behind = shifted(tiles, 1, axis, edge_behind)
    ahead = shifted(tiles, -1, axis, edge_ahead)
    far = shifted(tiles, 2, axis, edge_far)
    flux = [face_flux(*each) for each in zip(tiles, behind, ahead, far, speeds, opens)]
    following = shifted(flux, -1, axis, edge_flux)
    return jnp.concatenate([g - n for g, n in zip(flux, following)], axis=axis)


def reverse_flux(tiles, speeds, opens, axis, edges):
    edge_behind, edge_sum, edge_carried, edge_far = edges
    behind = shifted(tiles, 1, axis, edge_behind)
    jump = [jnp.where(o, h - b, 0.0) for h, b, o in zip(tiles, behind, opens)]
    carried = [s * j for s, j in zip(speeds, jump)]
    seven = [7.0 * g for g in carried]
    spread = [diffusivity * j for j in jump]
    ahead = shifted([a + b for a, b in zip(seven, spread)], -1, axis, edge_sum)
    back = shifted(carried, 1, axis, edge_carried)
    far = shifted(carried, -2, axis, edge_far)
    parts = zip(seven, spread, ahead, back, far)
    return jnp.concatenate([(a - b) + c - d - e for a, b, c, d, e in parts], axis=axis)


def level_of(lane):
    return lax.div(lax.rem(lane + slot // 2, lanes), slot)


def pack_columns(k, item, packed, ahead=0):
    lane = index(packed.shape, 1)
    tile = jnp.where(lane < lanes // 2, item[:, :lanes], item[:, -lanes:])
    return jnp.where(level_of(lane + (lanes - ahead)) == k, turned(tile, slot * k + ahead, 1), packed)


def second_item(tile):
    return turned(tile, -(slot // 2), 1)


def repeated(value):
    lane = index((value.shape[0], lanes), 1)
    value = jnp.where(lane < lanes // 2, value[:, :lanes], value[:, -lanes:])
    value = jnp.where(level_of(lane) == 0, value, 0.0)
    width = slot
    while width < lanes:
        value = value + turned(value, width, 1)
        width *= 2
    return value


def edge_rows(c, h, speed, open_y):
    size = c.shape[0]
    last = slice(size - sublanes, size)
    first = slice(0, sublanes)
    g_last = jnp.where(open_y[last], speed[last] * (h[last] - turned(h[last], 1, 0)), 0.0)
    g_first = jnp.where(open_y[first], speed[first] * (h[first] - turned(h[first], 1, 0)), 0.0)
    end = size - 1
    up = [c[end - 1 : end], c[end:], h[end:], g_last[sublanes - 1 :]]
    return up, [c[0:1], c[1:2], h[0:1], g_first[1:2]]


def store_rows(found, ref):
    levels = len(found)
    for item in range(len(found[0])):
        for k in range(0, levels, sublanes):
            tile = jnp.concatenate([found[i][item] for i in range(k, k + sublanes)], axis=0)
            ref[item * levels + k : item * levels + k + sublanes, :] = tile


def inward(levels, scaled, links, inverse, joint, passed):
    middle = levels // 2
    top = bottom = None
    for i in range(levels - middle):
        k = levels - 1 - i
        bottom = scaled(k) if i == 0 else scaled(k) + (links[k] * inverse[k]) * bottom
        passed[k] = bottom
        if i < middle:
            top = scaled(i) if i == 0 else scaled(i) + (links[i - 1] * inverse[i]) * top
            passed[i] = top
    link = links[middle - 1]
    top = (top + (link * inverse[middle - 1]) * bottom) * joint
    return top, bottom + (link * inverse[middle]) * top


def outward(levels, ends, links, inverse, passed):
    middle = levels // 2
    top, bottom = ends
    yield middle - 1, top
    yield middle, bottom
    for i in range(1, levels - middle):
        k = middle + i
        bottom = passed[k] + (links[k - 1] * inverse[k]) * bottom
        yield k, bottom
        k = middle - 1 - i
        if k >= 0:
            top = passed[k] + (links[k] * inverse[k]) * top
            yield k, top


def factorized(levels, links, inverse):
    middle = levels // 2

    def pivots(order, near, far):
        share = None
        for k in order:
            pivot = 1.0
            if 0 <= far(k) < levels - 1:
                pivot = pivot + links[far(k)]
            if share is not None:
                pivot = pivot + (links[near(k)] - links[near(k)] * share)
            inverse[k] = 1.0 / pivot
            if 0 <= far(k) < levels - 1:
                share = links[far(k)] * inverse[k]
            yield

    down = pivots(range(middle), lambda k: k - 1, lambda k: k)
    up = pivots(range(levels - 1, middle - 1, -1), lambda k: k, lambda k: k - 1)
    for _ in range(levels - middle):
        next(up)
        next(down, None)
    link = links[middle - 1]
    return 1.0 / (1.0 - (link * inverse[middle - 1]) * (link * inverse[middle]))


class Half:
    def __init__(self, ref, start):
        self.ref, self.start = ref, start

    def __getitem__(self, k):
        return self.ref[k, pl.ds(self.start, sublanes), :]


class Either:
    def __init__(self, flag, first, second):
        self.flag, self.first, self.second = flag, first, second

    def __getitem__(self, where):
        return jnp.where(self.flag, self.first[where], self.second[where])


def choose(flag, ref_true, ref_false, into):
    into[...] = jnp.where(flag, ref_true[...], ref_false[...])


def factor_kernel(
    tracer_far, east_far, north_far, mixing_far, depth_far, sensitivity_far,
    tracer, east, north, depth, links, inverse, joint, weight, pay_even, pay_odd, outer, pay_chip, pay_core, up, down, beside,
    mixing, sensitivity, passed, arrived,
):
    order = (
        (depth_far, depth),
        (mixing_far, mixing),
        (sensitivity_far, sensitivity),
        (tracer_far, tracer),
        (east_far, east),
        (north_far, north),
    )
    copies = [pltpu.make_async_copy(far, near, arrived.at[i]) for i, (far, near) in enumerate(order)]
    for copy in copies:
        copy.start()
    levels, rows, columns = tracer.shape
    even_y, even_x = parities()
    copies[0].wait()
    deep = depth[...]
    depth_float = deep.astype(jnp.float32)
    packed_depth = repeated(depth_float)
    for copy in copies[1:3]:
        copy.wait()
    shallow_y = jnp.minimum(deep, turned(deep, 1, 0))
    for k in range(levels - 1):
        links[k] = jnp.where(k + 1 < deep, mixing[k], 0.0)
    joint[...] = factorized(levels, links, inverse)
    ends = inward(levels, lambda k: sensitivity[k] * inverse[k], links, inverse, joint[...], passed)
    for copy in copies[3:]:
        copy.wait()
    packed = [jnp.zeros((rows, lanes), jnp.float32)] * 5
    rows_up, rows_down, rows_beside = {}, {}, {}
    for k, current in outward(levels, ends, links, inverse, passed):
        h = jnp.where(k < deep, current, 0.0)
        weight[k] = h
        c = tracer[k]
        speed_x = east[k] * (1.0 / 12.0)
        speed_y = north[k] * (1.0 / 12.0)
        items = (c, h, speed_x, speed_y) + ((mixing[k],) if k < levels - 1 else ())
        ahead = (0, slot // 2, 0, slot // 2, slot // 2)
        packed[: len(items)] = [pack_columns(k, *each) for each in zip(items, packed, ahead)]
        rows_up[k], rows_down[k] = edge_rows(c, h, speed_y, k < shallow_y)
        rows_up[k].append(speed_y[rows - 1 :])
        rows_down[k].append(speed_y[0:1])
        rows_beside[k] = [speed_y[1:2]]
    for found, ref in ((rows_up, up), (rows_down, down), (rows_beside, beside)):
        store_rows(found, ref)
    start = lax.rem(index((rows, lanes), 1), slot) < slot // 2
    twice = ((packed[0], packed[1]), (packed[2], packed[3]), (packed_depth, packed[4]))
    first = jnp.concatenate([jnp.where(start, a, b) for a, b in twice], axis=1)
    last = jnp.concatenate([jnp.where(start, b, a) for a, b in twice], axis=1)
    pay_chip[...] = jnp.where(even_x, first, last)
    pay_core[...] = jnp.where(even_x, last, first)
    outer[...] = jnp.concatenate([packed[0], packed[1], packed[2], packed_depth], axis=1)
    at = 5 * levels
    up[at : at + sublanes, :] = jnp.broadcast_to(depth_float[rows - 1 :], (sublanes, columns))
    down[at : at + sublanes, :] = jnp.broadcast_to(depth_float[0:1], (sublanes, columns))
    choose(even_y, up, down, pay_even)
    choose(even_y, down, up, pay_odd)


def rows_of(ref, item, levels):
    return ref[item * levels : (item + 1) * levels, :]


def border_rows(level, lower, upper, up, down, speeds, deeps):
    c_far, c_near, h_near, g_near = lower
    c_next, c_over, h_next, g_over = upper
    c_two, c_one, h_one = up
    c_zero, c_first, h_zero = down
    speed_start, speed_first, speed_last, speed_end = speeds
    before, zero, one, two_last, last, after = deeps
    start_open = level < jnp.minimum(before, zero)
    first_open = level < jnp.minimum(zero, one)
    last_open = level < jnp.minimum(two_last, last)
    end_open = level < jnp.minimum(last, after)
    start = face_flux(c_zero, c_near, c_first, c_far, speed_start, start_open)
    first = jnp.where(first_open, -speed_first * c_near, 0.0)
    final = jnp.where(last_open, -speed_last * c_next, 0.0)
    finish = face_flux(c_next, c_one, c_over, c_two, speed_end, end_open)
    start_jump = jnp.where(start_open, h_zero - h_near, 0.0)
    end_jump = jnp.where(end_open, h_next - h_one, 0.0)
    start_carried = speed_start * start_jump
    end_carried = speed_end * end_jump
    return (
        start - first,
        first,
        -final,
        final - finish,
        7.0 * start_carried - diffusivity * start_jump - g_near,
        -start_carried,
        -end_carried,
        7.0 * end_carried + diffusivity * end_jump - g_over,
    )


def borders_y(levels, lower, upper, up, down, speeds, deep, deeps, border):
    end = deep.shape[0] - 1
    deeps = (deeps[0], deep[0:1], deep[1:2], deep[end - 1 : end], deep[end:], deeps[1])
    several = lambda ref, count: [rows_of(ref, i, levels) for i in range(count)]
    level = index((levels, deep.shape[1]), 0).astype(jnp.float32)
    values = border_rows(level, several(lower, 4), several(upper, 4), several(up, 3), several(down, 3), speeds, deeps)
    for item, value in enumerate(values):
        border[item * levels : (item + 1) * levels, :] = value


def placed(shape):
    lane = index(shape, 1)
    return lax.rem(lane, slot), level_of(lane).astype(jnp.float32)


def borders_x(before, after, own):
    place, level = placed(own[0].shape)
    start = place < slot // 2
    at = lambda value, distance: turned(value, -distance, 1)
    c, h, speed, deep = (jnp.where(start, mine, other) for mine, other in zip(own, before))
    deep_back = at(deep, -1)
    is_open = level < jnp.minimum(deep, deep_back)
    next_open = level < jnp.minimum(deep, at(deep, 1))
    back_open = level < jnp.minimum(deep_back, at(deep, -2))
    behind, far = at(c, -1), at(c, -2)
    flux = face_flux(c, behind, at(c, 1), far, speed, is_open) + jnp.where(next_open, at(speed, 1) * behind, 0.0)
    forward = jnp.where(place == 0, flux, jnp.where(is_open, -speed * far, 0.0))
    h_back = at(h, -1)
    jump = jnp.where(is_open, h - h_back, 0.0)
    back = jnp.where(back_open, at(speed, -1) * (h_back - at(h, -2)), 0.0)
    backward = jnp.where(place == 0, 7.0 * (speed * jump) - diffusivity * jump, 0.0) - back
    c, h, speed, deep = (jnp.where(start, other, mine) for mine, other in zip(own, after))
    deep_next = at(deep, 1)
    is_open = level < jnp.minimum(deep, at(deep, -1))
    next_open = level < jnp.minimum(deep, deep_next)
    over_open = level < jnp.minimum(deep_next, at(deep, 2))
    c_next, c_over, speed_next = at(c, 1), at(c, 2), at(speed, 1)
    flux = face_flux(c_next, c, c_over, at(c, -1), speed_next, next_open) + jnp.where(is_open, speed * c_next, 0.0)
    forward_end = jnp.where(place == slot - 1, -flux, jnp.where(next_open, speed_next * c_over, 0.0))
    h_next = at(h, 1)
    jump = jnp.where(next_open, h_next - h, 0.0)
    over = jnp.where(over_open, at(speed, 2) * (at(h, 2) - h_next), 0.0)
    total = 7.0 * (speed_next * jump) + diffusivity * jump
    backward_end = jnp.where(place == slot - 1, total, 0.0) - over
    return jnp.where(start, forward, forward_end), jnp.where(start, backward, backward_end)


def with_rows(k, levels, value, border, item):
    rows, columns = value.shape
    row = index((sublanes, columns), 0)

    def line(which):
        at = (item + which) * levels + k
        return jnp.broadcast_to(border[at : at + 1, :], (sublanes, columns))

    tiles = split(value, 0)
    tiles[0] = tiles[0] + jnp.where(row == 0, line(0), jnp.where(row == 1, line(1), 0.0))
    added = jnp.where(row == sublanes - 2, line(2), jnp.where(row == sublanes - 1, line(3), 0.0))
    tiles[-1] = tiles[-1] + added
    return jnp.concatenate(tiles, axis=0)


def with_half_rows(k, levels, value, border, item, is_last):
    row = index(value.shape, 0)

    def line(which):
        at = (item + which) * levels + k
        return jnp.broadcast_to(border[at : at + 1, :], value.shape)

    first = jnp.where(row == 0, line(0), jnp.where(row == 1, line(1), 0.0))
    last = jnp.where(row == sublanes - 2, line(2), jnp.where(row == sublanes - 1, line(3), 0.0))
    return value + jnp.where(is_last, last, first)


def with_columns(k, value, packed):
    lead = turned(packed, -slot * k, 1)
    lane = index(lead.shape, 1)
    tiles = [value[:, i : i + lanes] for i in range(0, value.shape[1], lanes)]
    tiles[0] = tiles[0] + jnp.where(lane < 2, lead, 0.0)
    tiles[-1] = tiles[-1] + jnp.where(lane >= lanes - 2, lead, 0.0)
    return jnp.concatenate(tiles, axis=1)


def step_levels(first, c, h, east_part, north_part, shallow):
    count, rows, columns = c.shape
    shallow_x, shallow_y = shallow
    level = index((count, rows, columns), 0) + first
    none = (0.0, 0.0, 0.0, 0.0)
    speeds = split(east_part * (1.0 / 12.0), 2)
    opens = split(level < shallow_x[None], 2)
    forward = explicit_flux(split(c, 2), speeds, opens, 2, none)
    backward = reverse_flux(split(h, 2), speeds, opens, 2, none)
    speeds = split(north_part * (1.0 / 12.0), 1)
    opens = split(level < shallow_y[None], 1)
    forward = forward + explicit_flux(split(c, 1), speeds, opens, 1, none)
    backward = backward + reverse_flux(split(h, 1), speeds, opens, 1, none)
    return forward, h + backward


def inner_kernel(c_ref, h_ref, east, north, depth, *rest):
    *tracer, forward, linear = rest
    levels, rows, columns = c_ref.shape
    deep = depth[...]
    lane, row = index(deep.shape, 1), index(deep.shape, 0)
    shallow_x = jnp.where(lane == 0, 0, jnp.minimum(deep, turned(deep, 1, 1)))
    shallow_y = jnp.where(row == 0, 0, jnp.minimum(deep, turned(deep, 1, 0)))
    for k in range(0, levels, group_size):
        part = slice(k, min(k + group_size, levels))
        c, h = c_ref[part], h_ref[part]
        ahead, back = step_levels(k, c, h, east[part], north[part], (shallow_x, shallow_y))
        if tracer:
            back = back - (2.0 * uptake) * tracer[0][part] * h
        linear[part] = back
        forward[part] = c + ahead - uptake * c * c


def item_of(value, item):
    return value[:, item * lanes : (item + 1) * lanes]


def take(flag, core, chip):
    return jnp.where(flag, chip, core), jnp.where(flag, core, chip)


def four_items(message):
    values, speeds, depths = (item_of(message, i) for i in range(3))
    return [values, second_item(values), speeds, depths]


def own_items(outer):
    values, shifted_values, speeds, depths = (item_of(outer, i) for i in range(4))
    return [values, second_item(shifted_values), speeds, depths]


def strip_rows(levels, message, up, down):
    c, h, speeds, deep = four_items(message)
    side = second_item(speeds)
    size = c.shape[0]
    _, level = placed(c.shape)
    is_open = level < jnp.minimum(deep, turned(deep, 1, 0))
    carried = jnp.where(is_open, side * (h - turned(h, 1, 0)), 0.0)
    at = 4 * levels
    for ref in (up, down):
        ref[at : at + sublanes, :] = jnp.zeros((sublanes, ref.shape[1]), jnp.float32)
    end = size - 1
    above = (c[end - 1 : end], c[end:], h[end:], carried[end:], deep[end:])
    below = (c[0:1], c[1:2], h[0:1], carried[1:2], deep[0:1], side[0:1])
    for ref, lines in ((up, above), (down, below)):
        for i, line in enumerate(lines):
            ref[at + i : at + i + 1, :lanes] = line


def second_inner_kernel(
    c_ref, h_ref, east, north, depth, tracer, outer, got_chip,
    forward, linear, base, strip_links, strip_inverse, strip_joint, strip_weight, strip_values,
):
    levels = c_ref.shape[0]
    inner_kernel(c_ref, h_ref, east, north, depth, tracer, forward, linear)
    _, even = parities()
    place, level = placed((outer.shape[0], lanes))
    ours = (place < slot // 2) == even
    items = four_items(got_chip)
    side, mixed = second_item(items[2]), second_item(items[3])
    strip_values[...] = jnp.concatenate([items[0], items[1], items[3], side], axis=1)
    c, h, speed, deep = (jnp.where(ours, mine, item) for mine, item in zip(own_items(outer), items))
    is_open = level < jnp.minimum(deep, turned(deep, 1, 1))
    flux = face_flux(c, turned(c, 1, 1), turned(c, -1, 1), turned(c, 2, 1), speed, is_open)
    jump = jnp.where(is_open, h - turned(h, 1, 1), 0.0)
    carried = speed * jump
    plus = 7.0 * carried + diffusivity * jump
    minus = 7.0 * carried - diffusivity * jump
    step = c + (flux - turned(flux, -1, 1)) - uptake * c * c
    reverse = h + minus + turned(plus, -1, 1) - turned(carried, 1, 1) - turned(carried, -2, 1)
    previous = jnp.where(index(deep.shape, 0) == 0, 0.0, turned(deep, 1, 0))
    opens = split(level < jnp.minimum(deep, previous), 0)
    none = (0.0, 0.0, 0.0, 0.0)
    base[:, :lanes] = step + explicit_flux(split(c, 0), split(side, 0), opens, 0, none)
    base[:, lanes:] = reverse + reverse_flux(split(h, 0), split(side, 0), opens, 0, none)
    ours = (place == 0) | (place == 1) | (place == slot - 2) | (place == slot - 1)
    mixed = jnp.where(ours & (level + 1.0 < deep), mixed, 0.0)
    for k in range(levels):
        strip_weight[k] = turned(h, -slot * k, 1)
        if k < levels - 1:
            strip_links[k] = turned(mixed, -slot * k, 1)
    strip_joint[...] = factorized(levels, strip_links, strip_inverse)


def strip_states(levels, values, base, factors, weights, got, is_last):
    links, inverse, joint = factors
    c, h, deep, side = (item_of(values, i) for i in range(4))
    place, level = placed(c.shape)
    lower = upper = got
    half = lambda value: jnp.where(is_last, value[-sublanes:], value[:sublanes])
    end = c.shape[0] - 1

    def line(ref, item):
        at = 4 * levels + item
        return jnp.broadcast_to(ref[at : at + 1, :lanes], (sublanes, lanes))

    def row_of(value, at):
        return jnp.broadcast_to(value[at : at + 1], (sublanes, lanes))

    added = border_rows(
        level[:sublanes],
        [line(lower, i) for i in range(4)],
        [line(upper, i) for i in range(4)],
        (row_of(c, end - 1), row_of(c, end), row_of(h, end)),
        (row_of(c, 0), row_of(c, 1), row_of(h, 0)),
        (row_of(side, 0), row_of(side, 1), row_of(side, end), line(upper, 5)),
        (line(lower, 4), row_of(deep, 0), row_of(deep, 1), row_of(deep, end - 1), row_of(deep, end), line(upper, 4)),
    )
    row = index((sublanes, lanes), 0)

    def bordered(value, rows):
        first = jnp.where(row == 0, rows[0], jnp.where(row == 1, rows[1], 0.0))
        last = jnp.where(row == sublanes - 2, rows[2], jnp.where(row == sublanes - 1, rows[3], 0.0))
        return half(value) + jnp.where(is_last, last, first)

    deep, level = half(deep), level[:sublanes]
    right = jnp.where(level < deep, bordered(base[:, :lanes], added[:4]), 0.0)
    linear = bordered(base[:, lanes:], added[4:])
    right, linear = ([turned(value, -slot * k, 1) for k in range(levels)] for value in (right, linear))
    passed = [None] * levels
    ends = inward(levels, lambda k: right[k] * inverse[k], links, inverse, joint, passed)
    state = dict(outward(levels, ends, links, inverse, passed))

    def scaled(k):
        return (linear[k] - (2.0 * uptake) * state[k] * weights[k]) * inverse[k]

    ends = inward(levels, scaled, links, inverse, joint, passed)
    weight = dict(outward(levels, ends, links, inverse, passed))
    packed_state = packed_weight = jnp.zeros(deep.shape, jnp.float32)
    for k in range(levels):
        here = level == float(k)
        packed_state = jnp.where(here, turned(state[k], slot * k, 1), packed_state)
        value = jnp.where(k < deep, weight[k], 0.0)
        packed_weight = jnp.where(here, turned(value, slot * k, 1), packed_weight)
    return packed_state, packed_weight


def outer_rows(value):
    axis = value.ndim - 2
    size = value.shape[axis]
    first = lax.slice_in_dim(value, 0, sublanes, axis=axis)
    last = lax.slice_in_dim(value, size - sublanes, size, axis=axis)
    return jnp.where(index(first.shape, axis) < sublanes // 2, first, last)


def first_inner_kernel(
    c_ref, h_ref, east, north, depth, links, inverse, joint,
    forward, linear, north_rows, depth_rows, links_rows, inverse_rows, joint_rows, h_rows, forward_rows, linear_rows,
):
    inner_kernel(c_ref, h_ref, east, north, depth, forward, linear)
    depth_rows[...] = outer_rows(depth[...])
    joint_rows[...] = outer_rows(joint[...])
    pairs_of = ((north, north_rows), (links, links_rows), (inverse, inverse_rows), (h_ref, h_rows))
    for whole, rows in pairs_of + ((forward, forward_rows), (linear, linear_rows)):
        for k in range(whole.shape[0]):
            rows[k] = outer_rows(whole[k])


def first_step(
    depth, links, inverse, joint, weight, forward, linear, own_up, own_down, beside, sides, got, state, passed, scaled, border
):
    levels = weight.shape[0]
    even_y, _ = parities()
    got_even, got_odd = got
    lower, upper = Either(even_y, got_odd, got_even), Either(even_y, got_even, got_odd)
    deep = depth[...]
    depth_float = deep.astype(jnp.float32)
    at = 5 * levels
    speeds = (rows_of(own_down, 4, levels), beside[...], rows_of(own_up, 4, levels), rows_of(upper, 4, levels))
    deeps = (lower[at : at + 1, :], upper[at : at + 1, :])
    borders_y(levels, lower, upper, own_up, own_down, speeds, depth_float, deeps, border)
    packed = borders_x(*sides)
    for k in range(levels):
        scaled[k] = with_rows(k, levels, forward[k], border, 0)
        state[k] = with_rows(k, levels, linear[k], border, 4)
    for k in range(levels):
        scaled[k] = jnp.where(k < deep, with_columns(k, scaled[k], packed[0]), 0.0) * inverse[k]
        state[k] = with_columns(k, state[k], packed[1])
    ends = inward(levels, lambda k: scaled[k], links, inverse, joint[...], passed)
    for k, current in outward(levels, ends, links, inverse, passed):
        scaled[k] = (state[k] - (2.0 * uptake) * current * weight[k]) * inverse[k]
        state[k] = current
    return inward(levels, lambda k: scaled[k], links, inverse, joint[...], passed)


def sides_of(got_chip, got_core, own):
    _, even = parities()
    before, after = take(even, got_core[...], got_chip[...])
    return four_items(before), four_items(after), own_items(own)


def edge_kernel(
    north, depth, links, inverse, joint, weight, forward, linear, own_up, own_down, beside, own,
    got_even, got_odd, got_chip, got_core,
    pay_even, pay_odd, up, down,
    state, passed, scaled, border,
):
    levels = weight.shape[0]
    even_y, _ = parities()
    sides = [[outer_rows(item) for item in side] for side in sides_of(got_chip, got_core, own)]
    deep = depth[...]
    ends = first_step(
        depth, links, inverse, joint, weight, forward, linear, own_up, own_down, beside,
        sides, (got_even, got_odd), state, passed, scaled, border,
    )
    shallow_y = jnp.minimum(deep, turned(deep, 1, 0))
    rows_up, rows_down = {}, {}
    for k, current in outward(levels, ends, links, inverse, passed):
        h = jnp.where(k < deep, current, 0.0)
        rows_up[k], rows_down[k] = edge_rows(state[k], h, north[k] * (1.0 / 12.0), k < shallow_y)
    store_rows(rows_up, up)
    store_rows(rows_down, down)
    strip_rows(levels, got_chip[...], up, down)
    choose(even_y, up, down, pay_even)
    choose(even_y, down, up, pay_odd)


def first_kernel(
    depth, links, inverse, joint, weight, forward, linear, own_up, own_down, beside, own,
    got_even, got_odd, got_chip, got_core,
    state, weight_next, outer_next,
    passed, scaled, border,
):
    levels = weight.shape[0]
    ends = first_step(
        depth, links, inverse, joint, weight, forward, linear, own_up, own_down, beside,
        sides_of(got_chip, got_core, own), (got_even, got_odd), state, passed, scaled, border,
    )
    deep = depth[...]
    packed = [jnp.zeros((deep.shape[0], lanes), jnp.float32)] * 2
    for k, current in outward(levels, ends, links, inverse, passed):
        h = jnp.where(k < deep, current, 0.0)
        weight_next[k] = h
        packed = [pack_columns(k, *each) for each in zip((state[k], h), packed)]
    outer_next[...] = jnp.concatenate(packed, axis=1)


def second_kernel(
    on_odd,
    depth, links, inverse, joint, forward, linear, base, strip_links, strip_inverse, strip_joint, strip_weight, strip_values,
    own_up, own_down, own, first_up, first_down, beside, first_own,
    got1_even, got1_odd, got1_chip, got1_core, got, got_core,
    *rest,
):
    final_far, adjoint_far, final, adjoint, passed, scaled, border, sent = rest[-8:]
    copies = []
    even_y, even_x = parities()
    is_last = even_y != on_odd
    start = pl.multiple_of(jnp.where(is_last, sublanes, 0), sublanes)

    def send(near, far, part):
        copy = pltpu.make_async_copy(near.at[part], far.at[part, pl.ds(start, sublanes), :], sent.at[len(copies)])
        copy.start()
        copies.append(copy)

    levels = forward.shape[0]
    halves = lambda ref: Half(ref, start)
    plane = lambda ref: ref[pl.ds(start, sublanes), :]
    cut = lambda items: [jnp.where(is_last, item[-sublanes:], item[:sublanes]) for item in items]
    before1, after1 = take(even_x, got1_core[...], got1_chip[...])
    factors = (halves(strip_links), halves(strip_inverse), plane(strip_joint))
    strip = strip_states(levels, strip_values, base, factors, halves(strip_weight), got, is_last)
    before, after = take(even_x, plane(got_core), jnp.concatenate(strip, axis=1))
    deep = depth[...]
    depth_float = deep.astype(jnp.float32)
    at = 5 * levels
    lower1, upper1 = Either(even_y, got1_odd, got1_even), Either(even_y, got1_even, got1_odd)
    deeps = (lower1[at : at + 1, :], upper1[at : at + 1, :])
    speed = rows_of(upper1, 4, levels)
    speeds = (rows_of(first_down, 4, levels), beside[...], rows_of(first_up, 4, levels), speed)
    borders_y(levels, got, got, own_up, own_down, speeds, depth_float, deeps, border)

    pair = lambda value: [item_of(value, 0), item_of(value, 1)]
    ends = (pair(before) + cut(four_items(before1)[2:]), pair(after) + cut(four_items(after1)[2:]))
    mine = cut(pair(own) + [item_of(first_own, 2), item_of(first_own, 3)])
    deep = plane(depth)
    forward, linear, links, inverse = (halves(ref) for ref in (forward, linear, links, inverse))
    packed = borders_x(*ends, mine)
    for k in range(levels):
        adjoint[k] = with_half_rows(k, levels, linear[k], border, 4, is_last)
        scaled[k] = with_half_rows(k, levels, forward[k], border, 0, is_last)
    for k in range(levels):
        scaled[k] = jnp.where(k < deep, with_columns(k, scaled[k], packed[0]), 0.0) * inverse[k]
    for k in range(levels):
        adjoint[k] = with_columns(k, adjoint[k], packed[1])
    send(adjoint, adjoint_far, slice(0, levels))
    ends = inward(levels, lambda k: scaled[k], links, inverse, plane(joint), passed)
    middle = levels // 2
    quarter = middle // 2
    for k, current in outward(levels, ends, links, inverse, passed):
        final[k] = current
        if k == middle - quarter:
            send(final, final_far, slice(middle - quarter, middle + quarter))
    send(final, final_far, slice(0, middle - quarter))
    send(final, final_far, slice(middle + quarter, levels))
    for copy in copies:
        copy.wait()


def pairs(axis, parity):
    devices = lax.axis_size(axis)
    swaps = []
    for i in range(parity, devices - 1, 2):
        swaps += [(i, i + 1), (i + 1, i)]
    return swaps


def exchange(pay_even, pay_odd, *pay):
    got_even = lax.ppermute(pay_even, "group", pairs("group", 0))
    got_odd = lax.ppermute(pay_odd, "group", pairs("group", 1))
    got = [lax.ppermute(each, "tile", pairs("tile", len(pay) - 1 - i)) for i, each in enumerate(pay)]
    return got_even, got_odd, *got


def shards(tracer, east_speed, north_speed, mixing, depth_levels, sensitivity):
    levels, rows, columns = tracer.shape
    assert levels * slot == lanes and rows == 2 * sublanes and columns % lanes == 0
    f32 = jnp.float32
    field = jax.ShapeDtypeStruct((levels, rows, columns), f32)
    first_size = 5 * levels + sublanes
    second_size = 4 * levels + sublanes
    border_size = 8 * levels
    block = pltpu.VMEM((levels, rows, columns), f32)
    params = pltpu.CompilerParams(vmem_limit_bytes=32 * 1024 * 1024)
    far = pl.BlockSpec(memory_space=pl.ANY)

    def lines(size):
        return jax.ShapeDtypeStruct((size, columns), f32)

    def space(size):
        return pltpu.VMEM((size, columns), f32)

    def tiles(count):
        return jax.ShapeDtypeStruct((rows, count * lanes), f32)

    given = (tracer, east_speed, north_speed, mixing, depth_levels)
    near = tuple(jax.ShapeDtypeStruct(given[i].shape, given[i].dtype) for i in (0, 1, 2, 4))
    links = jax.ShapeDtypeStruct(mixing.shape, f32)
    plane = jax.ShapeDtypeStruct((rows, columns), f32)
    distant = [pltpu.with_memory_space_constraint(array, pltpu.HBM) for array in given + (sensitivity,)]
    outcome = pl.pallas_call(
        factor_kernel,
        in_specs=[far] * 6,
        out_shape=near
        + (links, field, plane, field, lines(first_size), lines(first_size), tiles(4), tiles(3), tiles(3), lines(first_size), lines(first_size), lines(levels)),
        scratch_shapes=[pltpu.VMEM(mixing.shape, f32), block, block, pltpu.SemaphoreType.DMA((6,))],
        compiler_params=params,
    )(*distant)
    tracer, east_speed, north_speed, depth_levels, *factors, weight = outcome[:8]
    *messages, up, down, beside = outcome[8:]
    pay_even, pay_odd, outer, pay_chip, pay_core = messages
    cells = levels * rows * columns
    inner = pl.CostEstimate(flops=80 * cells, bytes_accessed=24 * cells, transcendentals=0)

    got1 = exchange(pay_even, pay_odd, pay_chip, pay_core)
    tile = lambda *shape, kind=f32: jax.ShapeDtypeStruct(shape[:-1] + (sublanes, shape[-1]), kind)
    rows_shape = tile(levels, columns)
    outer_shapes = (rows_shape, tile(columns, kind=depth_levels.dtype), tile(levels - 1, columns), rows_shape, tile(columns))
    forward, linear, *outers = pl.pallas_call(
        first_inner_kernel,
        out_shape=(field, field) + outer_shapes + (rows_shape,) * 3,
        compiler_params=params,
        cost_estimate=inner,
    )(tracer, weight, east_speed, north_speed, depth_levels, *factors)
    small = pltpu.VMEM(rows_shape.shape, f32)
    pay_even, pay_odd, up2, down2 = pl.pallas_call(
        edge_kernel,
        out_shape=(lines(second_size),) * 4,
        scratch_shapes=[small, small, small, space(border_size)],
        compiler_params=params,
    )(*outers, up, down, beside, outer, *got1)
    state, weight_next, outer2 = pl.pallas_call(
        first_kernel,
        out_shape=(field, field, tiles(2)),
        scratch_shapes=[block, block, space(border_size)],
        compiler_params=params,
        cost_estimate=inner,
    )(depth_levels, *factors, weight, forward, linear, up, down, beside, outer, *got1)

    def strips(count):
        return jax.ShapeDtypeStruct((count, rows, lanes), f32)

    parts = pl.pallas_call(
        second_inner_kernel,
        out_shape=(field, field, tiles(2), strips(levels - 1), strips(levels), tiles(1), strips(levels), tiles(4)),
        compiler_params=params,
        cost_estimate=inner,
    )(state, weight_next, east_speed, north_speed, depth_levels, tracer, outer, got1[2])
    got2 = exchange(pay_even, pay_odd, outer2)
    sends = pltpu.SemaphoreType.DMA((4,))
    shared = (depth_levels, *factors, *parts, up2, down2, outer2, up, down, beside, outer, *got1)

    def half(on_odd, got, *partial):
        operands = shared + (got, got2[2]) + partial
        count = len(operands)
        whole = pl.BlockSpec(memory_space=pltpu.VMEM)
        return pl.pallas_call(
            functools.partial(second_kernel, on_odd),
            in_specs=[whole] * (count - len(partial)) + [far] * len(partial),
            out_specs=[far] * 2,
            out_shape=(field, field),
            scratch_shapes=[small] * 4 + [space(border_size), sends],
            input_output_aliases={count - 2: 0, count - 1: 1} if partial else {},
            compiler_params=params,
            cost_estimate=inner,
        )(*operands)

    partial = half(False, got2[0])
    final, adjoint = half(True, got2[1], *partial)
    return final, adjoint


def solution(mesh):
    block = P(None, "group", "tile")
    in_specs = (block, block, block, block, P("group", "tile"), block)
    return jax.shard_map(shards, mesh=mesh, in_specs=in_specs, out_specs=(block, block), check_vma=False)
```

```python
import functools

import jax
import jax.numpy as jnp
from jax import lax
from jax.experimental import pallas as pl
from jax.experimental.pallas import tpu as pltpu
from jax.sharding import PartitionSpec as P

diffusivity = 0.1
uptake = 0.2
lanes = 128
sublanes = 8
group_size = 8

slot = 8


def turned(value, shift, axis):
    return pltpu.roll(value, shift % value.shape[axis], axis)


def index(shape, axis):
    return lax.broadcasted_iota(jnp.int32, shape, axis)


def parities():
    return lax.rem(lax.axis_index("group"), 2) == 0, lax.rem(lax.axis_index("tile"), 2) == 0


def split(value, axis):
    step = lanes if axis == 2 else sublanes
    return [lax.slice_in_dim(value, i, i + step, axis=axis) for i in range(0, value.shape[axis], step)]


def shifted(tiles, shift, axis, edge):
    span = tiles[0].shape[axis]
    moved = [turned(tile, shift, axis) for tile in tiles]
    place = index(tiles[0].shape, axis)
    if shift > 0:
        return [jnp.where(place < shift, a, b) for a, b in zip([edge] + moved[:-1], moved)]
    return [jnp.where(place >= span + shift, a, b) for a, b in zip(moved[1:] + [edge], moved)]


def face_flux(c, behind, ahead, far, speed, is_open):
    flux = speed * (7.0 * (c + behind) - (ahead + far)) - diffusivity * (c - behind)
    return jnp.where(is_open, flux, 0.0)


def explicit_flux(tiles, speeds, opens, axis, edges):
    edge_behind, edge_far, edge_ahead, edge_flux = edges
    behind = shifted(tiles, 1, axis, edge_behind)
    ahead = shifted(tiles, -1, axis, edge_ahead)
    far = shifted(tiles, 2, axis, edge_far)
    flux = [face_flux(*each) for each in zip(tiles, behind, ahead, far, speeds, opens)]
    following = shifted(flux, -1, axis, edge_flux)
    return jnp.concatenate([g - n for g, n in zip(flux, following)], axis=axis)


def reverse_flux(tiles, speeds, opens, axis, edges):
    edge_behind, edge_sum, edge_carried, edge_far = edges
    behind = shifted(tiles, 1, axis, edge_behind)
    jump = [jnp.where(o, h - b, 0.0) for h, b, o in zip(tiles, behind, opens)]
    carried = [s * j for s, j in zip(speeds, jump)]
    seven = [7.0 * g for g in carried]
    spread = [diffusivity * j for j in jump]
    ahead = shifted([a + b for a, b in zip(seven, spread)], -1, axis, edge_sum)
    back = shifted(carried, 1, axis, edge_carried)
    far = shifted(carried, -2, axis, edge_far)
    parts = zip(seven, spread, ahead, back, far)
    return jnp.concatenate([(a - b) + c - d - e for a, b, c, d, e in parts], axis=axis)


def level_of(lane):
    return lax.div(lax.rem(lane + slot // 2, lanes), slot)


def pack_columns(k, item, packed, ahead=0):
    lane = index(packed.shape, 1)
    tile = jnp.where(lane < lanes // 2, item[:, :lanes], item[:, -lanes:])
    return jnp.where(level_of(lane + (lanes - ahead)) == k, turned(tile, slot * k + ahead, 1), packed)


def second_item(tile):
    return turned(tile, -(slot // 2), 1)


def repeated(value):
    lane = index((value.shape[0], lanes), 1)
    value = jnp.where(lane < lanes // 2, value[:, :lanes], value[:, -lanes:])
    value = jnp.where(level_of(lane) == 0, value, 0.0)
    width = slot
    while width < lanes:
        value = value + turned(value, width, 1)
        width *= 2
    return value


def edge_rows(c, h, speed, open_y):
    size = c.shape[0]
    last = slice(size - sublanes, size)
    first = slice(0, sublanes)
    g_last = jnp.where(open_y[last], speed[last] * (h[last] - turned(h[last], 1, 0)), 0.0)
    g_first = jnp.where(open_y[first], speed[first] * (h[first] - turned(h[first], 1, 0)), 0.0)
    end = size - 1
    up = [c[end - 1 : end], c[end:], h[end:], g_last[sublanes - 1 :]]
    return up, [c[0:1], c[1:2], h[0:1], g_first[1:2]]


def store_rows(found, ref):
    levels = len(found)
    for item in range(len(found[0])):
        for k in range(0, levels, sublanes):
            tile = jnp.concatenate([found[i][item] for i in range(k, k + sublanes)], axis=0)
            ref[item * levels + k : item * levels + k + sublanes, :] = tile


def inward(levels, scaled, links, inverse, joint, passed):
    middle = levels // 2
    top = bottom = None
    for i in range(levels - middle):
        k = levels - 1 - i
        bottom = scaled(k) if i == 0 else scaled(k) + (links[k] * inverse[k]) * bottom
        passed[k] = bottom
        if i < middle:
            top = scaled(i) if i == 0 else scaled(i) + (links[i - 1] * inverse[i]) * top
            passed[i] = top
    link = links[middle - 1]
    top = (top + (link * inverse[middle - 1]) * bottom) * joint
    return top, bottom + (link * inverse[middle]) * top


def outward(levels, ends, links, inverse, passed):
    middle = levels // 2
    top, bottom = ends
    yield middle - 1, top
    yield middle, bottom
    for i in range(1, levels - middle):
        k = middle + i
        bottom = passed[k] + (links[k - 1] * inverse[k]) * bottom
        yield k, bottom
        k = middle - 1 - i
        if k >= 0:
            top = passed[k] + (links[k] * inverse[k]) * top
            yield k, top


def factorized(levels, links, inverse):
    middle = levels // 2

    def pivots(order, near, far):
        share = None
        for k in order:
            pivot = 1.0
            if 0 <= far(k) < levels - 1:
                pivot = pivot + links[far(k)]
            if share is not None:
                pivot = pivot + (links[near(k)] - links[near(k)] * share)
            inverse[k] = 1.0 / pivot
            if 0 <= far(k) < levels - 1:
                share = links[far(k)] * inverse[k]
            yield

    down = pivots(range(middle), lambda k: k - 1, lambda k: k)
    up = pivots(range(levels - 1, middle - 1, -1), lambda k: k, lambda k: k - 1)
    for _ in range(levels - middle):
        next(up)
        next(down, None)
    link = links[middle - 1]
    return 1.0 / (1.0 - (link * inverse[middle - 1]) * (link * inverse[middle]))


class Half:
    def __init__(self, ref, start):
        self.ref, self.start = ref, start

    def __getitem__(self, k):
        return self.ref[k, pl.ds(self.start, sublanes), :]


class Either:
    def __init__(self, flag, first, second):
        self.flag, self.first, self.second = flag, first, second

    def __getitem__(self, where):
        return jnp.where(self.flag, self.first[where], self.second[where])


def choose(flag, ref_true, ref_false, into):
    into[...] = jnp.where(flag, ref_true[...], ref_false[...])


def factor_kernel(
    tracer_far, east_far, north_far, mixing_far, depth_far, sensitivity_far,
    tracer, east, north, depth, links, inverse, joint, weight, pay_even, pay_odd, outer, pay_chip, pay_core, up, down, beside,
    mixing, sensitivity, passed, arrived,
):
    order = (
        (depth_far, depth),
        (mixing_far, mixing),
        (sensitivity_far, sensitivity),
        (tracer_far, tracer),
        (east_far, east),
        (north_far, north),
    )
    copies = [pltpu.make_async_copy(far, near, arrived.at[i]) for i, (far, near) in enumerate(order)]
    for copy in copies:
        copy.start()
    levels, rows, columns = tracer.shape
    even_y, even_x = parities()
    copies[0].wait()
    deep = depth[...]
    depth_float = deep.astype(jnp.float32)
    packed_depth = repeated(depth_float)
    for copy in copies[1:3]:
        copy.wait()
    shallow_y = jnp.minimum(deep, turned(deep, 1, 0))
    for k in range(levels - 1):
        links[k] = jnp.where(k + 1 < deep, mixing[k], 0.0)
    joint[...] = factorized(levels, links, inverse)
    ends = inward(levels, lambda k: sensitivity[k] * inverse[k], links, inverse, joint[...], passed)
    for copy in copies[3:]:
        copy.wait()
    packed = [jnp.zeros((rows, lanes), jnp.float32)] * 5
    rows_up, rows_down, rows_beside = {}, {}, {}
    for k, current in outward(levels, ends, links, inverse, passed):
        h = jnp.where(k < deep, current, 0.0)
        weight[k] = h
        c = tracer[k]
        speed_x = east[k] * (1.0 / 12.0)
        speed_y = north[k] * (1.0 / 12.0)
        items = (c, h, speed_x, speed_y) + ((mixing[k],) if k < levels - 1 else ())
        ahead = (0, slot // 2, 0, slot // 2, slot // 2)
        packed[: len(items)] = [pack_columns(k, *each) for each in zip(items, packed, ahead)]
        rows_up[k], rows_down[k] = edge_rows(c, h, speed_y, k < shallow_y)
        rows_up[k].append(speed_y[rows - 1 :])
        rows_down[k].append(speed_y[0:1])
        rows_beside[k] = [speed_y[1:2]]
    for found, ref in ((rows_up, up), (rows_down, down), (rows_beside, beside)):
        store_rows(found, ref)
    start = lax.rem(index((rows, lanes), 1), slot) < slot // 2
    twice = ((packed[0], packed[1]), (packed[2], packed[3]), (packed_depth, packed[4]))
    first = jnp.concatenate([jnp.where(start, a, b) for a, b in twice], axis=1)
    last = jnp.concatenate([jnp.where(start, b, a) for a, b in twice], axis=1)
    pay_chip[...] = jnp.where(even_x, first, last)
    pay_core[...] = jnp.where(even_x, last, first)
    outer[...] = jnp.concatenate([packed[0], packed[1], packed[2], packed_depth], axis=1)
    at = 5 * levels
    up[at : at + sublanes, :] = jnp.broadcast_to(depth_float[rows - 1 :], (sublanes, columns))
    down[at : at + sublanes, :] = jnp.broadcast_to(depth_float[0:1], (sublanes, columns))
    choose(even_y, up, down, pay_even)
    choose(even_y, down, up, pay_odd)


def rows_of(ref, item, levels):
    return ref[item * levels : (item + 1) * levels, :]


def border_rows(level, lower, upper, up, down, speeds, deeps):
    c_far, c_near, h_near, g_near = lower
    c_next, c_over, h_next, g_over = upper
    c_two, c_one, h_one = up
    c_zero, c_first, h_zero = down
    speed_start, speed_first, speed_last, speed_end = speeds
    before, zero, one, two_last, last, after = deeps
    start_open = level < jnp.minimum(before, zero)
    first_open = level < jnp.minimum(zero, one)
    last_open = level < jnp.minimum(two_last, last)
    end_open = level < jnp.minimum(last, after)
    start = face_flux(c_zero, c_near, c_first, c_far, speed_start, start_open)
    first = jnp.where(first_open, -speed_first * c_near, 0.0)
    final = jnp.where(last_open, -speed_last * c_next, 0.0)
    finish = face_flux(c_next, c_one, c_over, c_two, speed_end, end_open)
    start_jump = jnp.where(start_open, h_zero - h_near, 0.0)
    end_jump = jnp.where(end_open, h_next - h_one, 0.0)
    start_carried = speed_start * start_jump
    end_carried = speed_end * end_jump
    return (
        start - first,
        first,
        -final,
        final - finish,
        7.0 * start_carried - diffusivity * start_jump - g_near,
        -start_carried,
        -end_carried,
        7.0 * end_carried + diffusivity * end_jump - g_over,
    )


def borders_y(levels, lower, upper, up, down, speeds, deep, deeps, border, is_last=None):
    end = deep.shape[0] - 1
    deeps = (deeps[0], deep[0:1], deep[1:2], deep[end - 1 : end], deep[end:], deeps[1])
    several = lambda ref, count: [rows_of(ref, i, levels) for i in range(count)]
    level = index((levels, deep.shape[1]), 0).astype(jnp.float32)
    values = border_rows(level, several(lower, 4), several(upper, 4), several(up, 3), several(down, 3), speeds, deeps)
    if is_last is not None:
        ends = ((values[0], values[2]), (values[1], values[3]), (values[4], values[6]), (values[5], values[7]))
        values = [jnp.where(is_last, last, first) for first, last in ends]
    for item, value in enumerate(values):
        border[item * levels : (item + 1) * levels, :] = value


def placed(shape):
    lane = index(shape, 1)
    return lax.rem(lane, slot), level_of(lane).astype(jnp.float32)


def borders_x(before, after, own):
    place, level = placed(own[0].shape)
    start = place < slot // 2
    at = lambda value, distance: turned(value, -distance, 1)
    c, h, speed, deep = (jnp.where(start, mine, other) for mine, other in zip(own, before))
    deep_back = at(deep, -1)
    is_open = level < jnp.minimum(deep, deep_back)
    next_open = level < jnp.minimum(deep, at(deep, 1))
    back_open = level < jnp.minimum(deep_back, at(deep, -2))
    behind, far = at(c, -1), at(c, -2)
    flux = face_flux(c, behind, at(c, 1), far, speed, is_open) + jnp.where(next_open, at(speed, 1) * behind, 0.0)
    forward = jnp.where(place == 0, flux, jnp.where(is_open, -speed * far, 0.0))
    h_back = at(h, -1)
    jump = jnp.where(is_open, h - h_back, 0.0)
    back = jnp.where(back_open, at(speed, -1) * (h_back - at(h, -2)), 0.0)
    backward = jnp.where(place == 0, 7.0 * (speed * jump) - diffusivity * jump, 0.0) - back
    c, h, speed, deep = (jnp.where(start, other, mine) for mine, other in zip(own, after))
    deep_next = at(deep, 1)
    is_open = level < jnp.minimum(deep, at(deep, -1))
    next_open = level < jnp.minimum(deep, deep_next)
    over_open = level < jnp.minimum(deep_next, at(deep, 2))
    c_next, c_over, speed_next = at(c, 1), at(c, 2), at(speed, 1)
    flux = face_flux(c_next, c, c_over, at(c, -1), speed_next, next_open) + jnp.where(is_open, speed * c_next, 0.0)
    forward_end = jnp.where(place == slot - 1, -flux, jnp.where(next_open, speed_next * c_over, 0.0))
    h_next = at(h, 1)
    jump = jnp.where(next_open, h_next - h, 0.0)
    over = jnp.where(over_open, at(speed, 2) * (at(h, 2) - h_next), 0.0)
    total = 7.0 * (speed_next * jump) + diffusivity * jump
    backward_end = jnp.where(place == slot - 1, total, 0.0) - over
    return jnp.where(start, forward, forward_end), jnp.where(start, backward, backward_end)


def with_rows(k, levels, value, border, item):
    rows, columns = value.shape
    row = index((sublanes, columns), 0)

    def line(which):
        at = (item + which) * levels + k
        return jnp.broadcast_to(border[at : at + 1, :], (sublanes, columns))

    tiles = split(value, 0)
    tiles[0] = tiles[0] + jnp.where(row == 0, line(0), jnp.where(row == 1, line(1), 0.0))
    added = jnp.where(row == sublanes - 2, line(2), jnp.where(row == sublanes - 1, line(3), 0.0))
    tiles[-1] = tiles[-1] + added
    return jnp.concatenate(tiles, axis=0)


def with_half_rows(k, levels, value, border, item, is_last):
    row = index(value.shape, 0) - jnp.where(is_last, sublanes - 2, 0)

    def line(which):
        at = (item + which) * levels + k
        return jnp.broadcast_to(border[at : at + 1, :], value.shape)

    return value + jnp.where(row == 0, line(0), jnp.where(row == 1, line(1), 0.0))


def with_columns(k, value, packed):
    lead = turned(packed, -slot * k, 1)
    lane = index(lead.shape, 1)
    tiles = [value[:, i : i + lanes] for i in range(0, value.shape[1], lanes)]
    tiles[0] = tiles[0] + jnp.where(lane < 2, lead, 0.0)
    tiles[-1] = tiles[-1] + jnp.where(lane >= lanes - 2, lead, 0.0)
    return jnp.concatenate(tiles, axis=1)


def step_levels(first, c, h, east_part, north_part, shallow):
    count, rows, columns = c.shape
    shallow_x, shallow_y = shallow
    level = index((count, rows, columns), 0) + first
    none = (0.0, 0.0, 0.0, 0.0)
    speeds = split(east_part * (1.0 / 12.0), 2)
    opens = split(level < shallow_x[None], 2)
    forward = explicit_flux(split(c, 2), speeds, opens, 2, none)
    backward = reverse_flux(split(h, 2), speeds, opens, 2, none)
    speeds = split(north_part * (1.0 / 12.0), 1)
    opens = split(level < shallow_y[None], 1)
    forward = forward + explicit_flux(split(c, 1), speeds, opens, 1, none)
    backward = backward + reverse_flux(split(h, 1), speeds, opens, 1, none)
    return forward, h + backward


def inner_kernel(c_ref, h_ref, east, north, depth, *rest):
    *tracer, forward, linear = rest
    levels, rows, columns = c_ref.shape
    deep = depth[...]
    lane, row = index(deep.shape, 1), index(deep.shape, 0)
    shallow_x = jnp.where(lane == 0, 0, jnp.minimum(deep, turned(deep, 1, 1)))
    shallow_y = jnp.where(row == 0, 0, jnp.minimum(deep, turned(deep, 1, 0)))
    for k in range(0, levels, group_size):
        part = slice(k, min(k + group_size, levels))
        c, h = c_ref[part], h_ref[part]
        ahead, back = step_levels(k, c, h, east[part], north[part], (shallow_x, shallow_y))
        if tracer:
            back = back - (2.0 * uptake) * tracer[0][part] * h
        linear[part] = back
        forward[part] = c + ahead - uptake * c * c


def item_of(value, item):
    return value[:, item * lanes : (item + 1) * lanes]


def take(flag, core, chip):
    return jnp.where(flag, chip, core), jnp.where(flag, core, chip)


def four_items(message):
    values, speeds, depths = (item_of(message, i) for i in range(3))
    return [values, second_item(values), speeds, depths]


def own_items(outer):
    values, shifted_values, speeds, depths = (item_of(outer, i) for i in range(4))
    return [values, second_item(shifted_values), speeds, depths]


def strip_rows(levels, message, up, down):
    c, h, speeds, deep = four_items(message)
    side = second_item(speeds)
    size = c.shape[0]
    _, level = placed(c.shape)
    is_open = level < jnp.minimum(deep, turned(deep, 1, 0))
    carried = jnp.where(is_open, side * (h - turned(h, 1, 0)), 0.0)
    at = 4 * levels
    for ref in (up, down):
        ref[at : at + sublanes, :] = jnp.zeros((sublanes, ref.shape[1]), jnp.float32)
    end = size - 1
    above = (c[end - 1 : end], c[end:], h[end:], carried[end:], deep[end:])
    below = (c[0:1], c[1:2], h[0:1], carried[1:2], deep[0:1], side[0:1])
    for ref, lines in ((up, above), (down, below)):
        for i, line in enumerate(lines):
            ref[at + i : at + i + 1, :lanes] = line


def second_inner_kernel(
    c_ref, h_ref, east, north, depth, tracer, outer, got_chip,
    forward, linear, base, strip_links, strip_inverse, strip_joint, strip_weight, strip_values,
):
    levels = c_ref.shape[0]
    inner_kernel(c_ref, h_ref, east, north, depth, tracer, forward, linear)
    _, even = parities()
    place, level = placed((outer.shape[0], lanes))
    ours = (place < slot // 2) == even
    items = four_items(got_chip)
    side, mixed = second_item(items[2]), second_item(items[3])
    strip_values[...] = jnp.concatenate([items[0], items[1], items[3], side], axis=1)
    c, h, speed, deep = (jnp.where(ours, mine, item) for mine, item in zip(own_items(outer), items))
    is_open = level < jnp.minimum(deep, turned(deep, 1, 1))
    flux = face_flux(c, turned(c, 1, 1), turned(c, -1, 1), turned(c, 2, 1), speed, is_open)
    jump = jnp.where(is_open, h - turned(h, 1, 1), 0.0)
    carried = speed * jump
    plus = 7.0 * carried + diffusivity * jump
    minus = 7.0 * carried - diffusivity * jump
    step = c + (flux - turned(flux, -1, 1)) - uptake * c * c
    reverse = h + minus + turned(plus, -1, 1) - turned(carried, 1, 1) - turned(carried, -2, 1)
    previous = jnp.where(index(deep.shape, 0) == 0, 0.0, turned(deep, 1, 0))
    opens = split(level < jnp.minimum(deep, previous), 0)
    none = (0.0, 0.0, 0.0, 0.0)
    base[:, :lanes] = step + explicit_flux(split(c, 0), split(side, 0), opens, 0, none)
    base[:, lanes:] = reverse + reverse_flux(split(h, 0), split(side, 0), opens, 0, none)
    ours = (place == 0) | (place == 1) | (place == slot - 2) | (place == slot - 1)
    mixed = jnp.where(ours & (level + 1.0 < deep), mixed, 0.0)
    for k in range(levels):
        strip_weight[k] = turned(h, -slot * k, 1)
        if k < levels - 1:
            strip_links[k] = turned(mixed, -slot * k, 1)
    strip_joint[...] = factorized(levels, strip_links, strip_inverse)


def strip_states(levels, values, base, factors, weights, got, is_last):
    links, inverse, joint = factors
    c, h, deep, side = (item_of(values, i) for i in range(4))
    place, level = placed(c.shape)
    lower = upper = got
    half = lambda value: jnp.where(is_last, value[-sublanes:], value[:sublanes])
    end = c.shape[0] - 1

    def line(ref, item):
        at = 4 * levels + item
        return jnp.broadcast_to(ref[at : at + 1, :lanes], (sublanes, lanes))

    def row_of(value, at):
        return jnp.broadcast_to(value[at : at + 1], (sublanes, lanes))

    added = border_rows(
        level[:sublanes],
        [line(lower, i) for i in range(4)],
        [line(upper, i) for i in range(4)],
        (row_of(c, end - 1), row_of(c, end), row_of(h, end)),
        (row_of(c, 0), row_of(c, 1), row_of(h, 0)),
        (row_of(side, 0), row_of(side, 1), row_of(side, end), line(upper, 5)),
        (line(lower, 4), row_of(deep, 0), row_of(deep, 1), row_of(deep, end - 1), row_of(deep, end), line(upper, 4)),
    )
    row = index((sublanes, lanes), 0)

    def bordered(value, rows):
        first = jnp.where(row == 0, rows[0], jnp.where(row == 1, rows[1], 0.0))
        last = jnp.where(row == sublanes - 2, rows[2], jnp.where(row == sublanes - 1, rows[3], 0.0))
        return half(value) + jnp.where(is_last, last, first)

    deep, level = half(deep), level[:sublanes]
    right = jnp.where(level < deep, bordered(base[:, :lanes], added[:4]), 0.0)
    linear = bordered(base[:, lanes:], added[4:])
    right, linear = ([turned(value, -slot * k, 1) for k in range(levels)] for value in (right, linear))
    passed = [None] * levels
    ends = inward(levels, lambda k: right[k] * inverse[k], links, inverse, joint, passed)
    state = dict(outward(levels, ends, links, inverse, passed))

    def scaled(k):
        return (linear[k] - (2.0 * uptake) * state[k] * weights[k]) * inverse[k]

    ends = inward(levels, scaled, links, inverse, joint, passed)
    weight = dict(outward(levels, ends, links, inverse, passed))
    packed_state = packed_weight = jnp.zeros(deep.shape, jnp.float32)
    for k in range(levels):
        here = level == float(k)
        packed_state = jnp.where(here, turned(state[k], slot * k, 1), packed_state)
        value = jnp.where(k < deep, weight[k], 0.0)
        packed_weight = jnp.where(here, turned(value, slot * k, 1), packed_weight)
    return packed_state, packed_weight


def outer_rows(value):
    axis = value.ndim - 2
    size = value.shape[axis]
    first = lax.slice_in_dim(value, 0, sublanes, axis=axis)
    last = lax.slice_in_dim(value, size - sublanes, size, axis=axis)
    return jnp.where(index(first.shape, axis) < sublanes // 2, first, last)


def first_inner_kernel(
    c_ref, h_ref, east, north, depth, links, inverse, joint,
    forward, linear, north_rows, depth_rows, links_rows, inverse_rows, joint_rows, h_rows, forward_rows, linear_rows,
):
    inner_kernel(c_ref, h_ref, east, north, depth, forward, linear)
    depth_rows[...] = outer_rows(depth[...])
    joint_rows[...] = outer_rows(joint[...])
    pairs_of = ((north, north_rows), (links, links_rows), (inverse, inverse_rows), (h_ref, h_rows))
    for whole, rows in pairs_of + ((forward, forward_rows), (linear, linear_rows)):
        for k in range(whole.shape[0]):
            rows[k] = outer_rows(whole[k])


def first_step(
    depth, links, inverse, joint, weight, forward, linear, own_up, own_down, beside, sides, got, state, passed, scaled, border
):
    levels = weight.shape[0]
    even_y, _ = parities()
    got_even, got_odd = got
    lower, upper = Either(even_y, got_odd, got_even), Either(even_y, got_even, got_odd)
    deep = depth[...]
    depth_float = deep.astype(jnp.float32)
    at = 5 * levels
    speeds = (rows_of(own_down, 4, levels), beside[...], rows_of(own_up, 4, levels), rows_of(upper, 4, levels))
    deeps = (lower[at : at + 1, :], upper[at : at + 1, :])
    borders_y(levels, lower, upper, own_up, own_down, speeds, depth_float, deeps, border)
    packed = borders_x(*sides)
    for k in range(levels):
        scaled[k] = with_rows(k, levels, forward[k], border, 0)
        state[k] = with_rows(k, levels, linear[k], border, 4)
    for k in range(levels):
        scaled[k] = jnp.where(k < deep, with_columns(k, scaled[k], packed[0]), 0.0) * inverse[k]
        state[k] = with_columns(k, state[k], packed[1])
    ends = inward(levels, lambda k: scaled[k], links, inverse, joint[...], passed)
    for k, current in outward(levels, ends, links, inverse, passed):
        scaled[k] = (state[k] - (2.0 * uptake) * current * weight[k]) * inverse[k]
        state[k] = current
    return inward(levels, lambda k: scaled[k], links, inverse, joint[...], passed)


def sides_of(got_chip, got_core, own):
    _, even = parities()
    before, after = take(even, got_core[...], got_chip[...])
    return four_items(before), four_items(after), own_items(own)


def edge_kernel(
    north, depth, links, inverse, joint, weight, forward, linear, own_up, own_down, beside, own,
    got_even, got_odd, got_chip, got_core,
    pay_even, pay_odd, up, down,
    state, passed, scaled, border,
):
    levels = weight.shape[0]
    even_y, _ = parities()
    sides = [[outer_rows(item) for item in side] for side in sides_of(got_chip, got_core, own)]
    deep = depth[...]
    ends = first_step(
        depth, links, inverse, joint, weight, forward, linear, own_up, own_down, beside,
        sides, (got_even, got_odd), state, passed, scaled, border,
    )
    shallow_y = jnp.minimum(deep, turned(deep, 1, 0))
    rows_up, rows_down = {}, {}
    for k, current in outward(levels, ends, links, inverse, passed):
        h = jnp.where(k < deep, current, 0.0)
        rows_up[k], rows_down[k] = edge_rows(state[k], h, north[k] * (1.0 / 12.0), k < shallow_y)
    store_rows(rows_up, up)
    store_rows(rows_down, down)
    strip_rows(levels, got_chip[...], up, down)
    choose(even_y, up, down, pay_even)
    choose(even_y, down, up, pay_odd)


def first_kernel(
    depth, links, inverse, joint, weight, forward, linear, own_up, own_down, beside, own,
    got_even, got_odd, got_chip, got_core,
    state, weight_next, outer_next,
    passed, scaled, border,
):
    levels = weight.shape[0]
    ends = first_step(
        depth, links, inverse, joint, weight, forward, linear, own_up, own_down, beside,
        sides_of(got_chip, got_core, own), (got_even, got_odd), state, passed, scaled, border,
    )
    deep = depth[...]
    packed = [jnp.zeros((deep.shape[0], lanes), jnp.float32)] * 2
    for k, current in outward(levels, ends, links, inverse, passed):
        h = jnp.where(k < deep, current, 0.0)
        weight_next[k] = h
        packed = [pack_columns(k, *each) for each in zip((state[k], h), packed)]
    outer_next[...] = jnp.concatenate(packed, axis=1)


def second_kernel(
    on_odd,
    depth, links, inverse, joint, forward, linear, base, strip_links, strip_inverse, strip_joint, strip_weight, strip_values,
    own_up, own_down, own, first_up, first_down, beside, first_own,
    got1_even, got1_odd, got1_chip, got1_core, got, got_core,
    *rest,
):
    final_far, adjoint_far, final, adjoint, passed, scaled, border, sent = rest[-8:]
    copies = []
    even_y, even_x = parities()
    is_last = even_y != on_odd
    start = pl.multiple_of(jnp.where(is_last, sublanes, 0), sublanes)

    def send(near, far, part):
        copy = pltpu.make_async_copy(near.at[part], far.at[part, pl.ds(start, sublanes), :], sent.at[len(copies)])
        copy.start()
        copies.append(copy)

    levels = forward.shape[0]
    halves = lambda ref: Half(ref, start)
    plane = lambda ref: ref[pl.ds(start, sublanes), :]
    cut = lambda items: [jnp.where(is_last, item[-sublanes:], item[:sublanes]) for item in items]
    before1, after1 = take(even_x, got1_core[...], got1_chip[...])
    factors = (halves(strip_links), halves(strip_inverse), plane(strip_joint))
    strip = strip_states(levels, strip_values, base, factors, halves(strip_weight), got, is_last)
    before, after = take(even_x, plane(got_core), jnp.concatenate(strip, axis=1))
    deep = depth[...]
    depth_float = deep.astype(jnp.float32)
    at = 5 * levels
    lower1, upper1 = Either(even_y, got1_odd, got1_even), Either(even_y, got1_even, got1_odd)
    deeps = (lower1[at : at + 1, :], upper1[at : at + 1, :])
    speed = rows_of(upper1, 4, levels)
    speeds = (rows_of(first_down, 4, levels), beside[...], rows_of(first_up, 4, levels), speed)
    borders_y(levels, got, got, own_up, own_down, speeds, depth_float, deeps, border, is_last)

    pair = lambda value: [item_of(value, 0), item_of(value, 1)]
    ends = (pair(before) + cut(four_items(before1)[2:]), pair(after) + cut(four_items(after1)[2:]))
    mine = cut(pair(own) + [item_of(first_own, 2), item_of(first_own, 3)])
    deep = plane(depth)
    forward, linear, links, inverse = (halves(ref) for ref in (forward, linear, links, inverse))
    packed = borders_x(*ends, mine)
    for k in range(levels):
        adjoint[k] = with_half_rows(k, levels, linear[k], border, 2, is_last)
        scaled[k] = with_half_rows(k, levels, forward[k], border, 0, is_last)
    for k in range(levels):
        scaled[k] = jnp.where(k < deep, with_columns(k, scaled[k], packed[0]), 0.0) * inverse[k]
    for k in range(levels):
        adjoint[k] = with_columns(k, adjoint[k], packed[1])
    send(adjoint, adjoint_far, slice(0, levels))
    ends = inward(levels, lambda k: scaled[k], links, inverse, plane(joint), passed)
    middle = levels // 2
    quarter = middle // 2
    for k, current in outward(levels, ends, links, inverse, passed):
        final[k] = current
        if k == middle - quarter:
            send(final, final_far, slice(middle - quarter, middle + quarter))
    send(final, final_far, slice(0, middle - quarter))
    send(final, final_far, slice(middle + quarter, levels))
    for copy in copies:
        copy.wait()


def pairs(axis, parity):
    devices = lax.axis_size(axis)
    swaps = []
    for i in range(parity, devices - 1, 2):
        swaps += [(i, i + 1), (i + 1, i)]
    return swaps


def exchange(pay_even, pay_odd, *pay):
    got_even = lax.ppermute(pay_even, "group", pairs("group", 0))
    got_odd = lax.ppermute(pay_odd, "group", pairs("group", 1))
    got = [lax.ppermute(each, "tile", pairs("tile", len(pay) - 1 - i)) for i, each in enumerate(pay)]
    return got_even, got_odd, *got


def shards(tracer, east_speed, north_speed, mixing, depth_levels, sensitivity):
    levels, rows, columns = tracer.shape
    assert levels * slot == lanes and rows == 2 * sublanes and columns % lanes == 0
    f32 = jnp.float32
    field = jax.ShapeDtypeStruct((levels, rows, columns), f32)
    first_size = 5 * levels + sublanes
    second_size = 4 * levels + sublanes
    border_size = 8 * levels
    block = pltpu.VMEM((levels, rows, columns), f32)
    params = pltpu.CompilerParams(vmem_limit_bytes=32 * 1024 * 1024)
    far = pl.BlockSpec(memory_space=pl.ANY)

    def lines(size):
        return jax.ShapeDtypeStruct((size, columns), f32)

    def space(size):
        return pltpu.VMEM((size, columns), f32)

    def tiles(count):
        return jax.ShapeDtypeStruct((rows, count * lanes), f32)

    given = (tracer, east_speed, north_speed, mixing, depth_levels)
    near = tuple(jax.ShapeDtypeStruct(given[i].shape, given[i].dtype) for i in (0, 1, 2, 4))
    links = jax.ShapeDtypeStruct(mixing.shape, f32)
    plane = jax.ShapeDtypeStruct((rows, columns), f32)
    distant = [pltpu.with_memory_space_constraint(array, pltpu.HBM) for array in given + (sensitivity,)]
    outcome = pl.pallas_call(
        factor_kernel,
        in_specs=[far] * 6,
        out_shape=near
        + (links, field, plane, field, lines(first_size), lines(first_size), tiles(4), tiles(3), tiles(3), lines(first_size), lines(first_size), lines(levels)),
        scratch_shapes=[pltpu.VMEM(mixing.shape, f32), block, block, pltpu.SemaphoreType.DMA((6,))],
        compiler_params=params,
    )(*distant)
    tracer, east_speed, north_speed, depth_levels, *factors, weight = outcome[:8]
    *messages, up, down, beside = outcome[8:]
    pay_even, pay_odd, outer, pay_chip, pay_core = messages
    cells = levels * rows * columns
    inner = pl.CostEstimate(flops=80 * cells, bytes_accessed=24 * cells, transcendentals=0)

    got1 = exchange(pay_even, pay_odd, pay_chip, pay_core)
    tile = lambda *shape, kind=f32: jax.ShapeDtypeStruct(shape[:-1] + (sublanes, shape[-1]), kind)
    rows_shape = tile(levels, columns)
    outer_shapes = (rows_shape, tile(columns, kind=depth_levels.dtype), tile(levels - 1, columns), rows_shape, tile(columns))
    forward, linear, *outers = pl.pallas_call(
        first_inner_kernel,
        out_shape=(field, field) + outer_shapes + (rows_shape,) * 3,
        compiler_params=params,
        cost_estimate=inner,
    )(tracer, weight, east_speed, north_speed, depth_levels, *factors)
    small = pltpu.VMEM(rows_shape.shape, f32)
    pay_even, pay_odd, up2, down2 = pl.pallas_call(
        edge_kernel,
        out_shape=(lines(second_size),) * 4,
        scratch_shapes=[small, small, small, space(border_size)],
        compiler_params=params,
    )(*outers, up, down, beside, outer, *got1)
    state, weight_next, outer2 = pl.pallas_call(
        first_kernel,
        out_shape=(field, field, tiles(2)),
        scratch_shapes=[block, block, space(border_size)],
        compiler_params=params,
        cost_estimate=inner,
    )(depth_levels, *factors, weight, forward, linear, up, down, beside, outer, *got1)

    def strips(count):
        return jax.ShapeDtypeStruct((count, rows, lanes), f32)

    parts = pl.pallas_call(
        second_inner_kernel,
        out_shape=(field, field, tiles(2), strips(levels - 1), strips(levels), tiles(1), strips(levels), tiles(4)),
        compiler_params=params,
        cost_estimate=inner,
    )(state, weight_next, east_speed, north_speed, depth_levels, tracer, outer, got1[2])
    got2 = exchange(pay_even, pay_odd, outer2)
    sends = pltpu.SemaphoreType.DMA((4,))
    shared = (depth_levels, *factors, *parts, up2, down2, outer2, up, down, beside, outer, *got1)

    def half(on_odd, got, *partial):
        operands = shared + (got, got2[2]) + partial
        count = len(operands)
        whole = pl.BlockSpec(memory_space=pltpu.VMEM)
        return pl.pallas_call(
            functools.partial(second_kernel, on_odd),
            in_specs=[whole] * (count - len(partial)) + [far] * len(partial),
            out_specs=[far] * 2,
            out_shape=(field, field),
            scratch_shapes=[small] * 4 + [space(border_size), sends],
            input_output_aliases={count - 2: 0, count - 1: 1} if partial else {},
            compiler_params=params,
            cost_estimate=inner,
        )(*operands)

    partial = half(False, got2[0])
    final, adjoint = half(True, got2[1], *partial)
    return final, adjoint


def solution(mesh):
    block = P(None, "group", "tile")
    in_specs = (block, block, block, block, P("group", "tile"), block)
    return jax.shard_map(shards, mesh=mesh, in_specs=in_specs, out_specs=(block, block), check_vma=False)
```
